32 devices in a mesh: flux: 4 (over z), obs: 8 (over y, x, core).
Axes of the slice: x: 2, y: 2, z: 4, core: 2. Of those that a mesh axis runs over, the one named last changes fastest.
Arguments:
- footprint: bfloat16 [256, 4, 4, 2, 4096], P(('flux', 'obs')), may hold values from 0.00049972534 to 0.049804688
- obs_hour: int32 [256, 4], P(('flux', 'obs')), may hold values from 0 to 3
- tile_list: int32 [256, 4], P(('flux', 'obs')), may hold values from 0 to 511, as said below
- tile_row: int32 [512], replicated, may hold values from 0 to 511, as said below
- flux: bfloat16 [512, 5, 4096], P('flux'), may hold values from -6 to 6
- observed: float32 [256, 4], P(('flux', 'obs')), may hold values from -18 to 18
- obs_var: float32 [256, 4], P(('flux', 'obs')), may hold values from 0.5 to 4
Outputs:
- modeled: float32 [256, 4], P(('flux', 'obs'))
- gradient: float32 [512, 5, 4096], P('flux', None, 'obs')
The draws below stay inside these ranges and needn't reach their ends.
Inputs may be any that keep to these rules, and one draw needn't show every extreme that they name: `tile_row`: A permutation: every tile has its own storage row, and the row r lies on index r // 128 of flux. `tile_list`: among the 32 listed tiles of one device's 8 blocks, at most 16 have storage rows on one index of flux; on every device some index of flux gets exactly 16.
All inputs are finite; a program needn't handle non-finite values.
Results may differ from the reference program's by a relative error of at most 0.0019.
Values may be sent and summed in bfloat16 or wider, within the bound.
No kernel may reach another device: no remote copies, remote signals or barrier semaphores. Data moves between devices by JAX's collectives and lax.ppermute only.
A program may use at most 64 MiB of HBM per device.

```python
import math
import jax
import jax.numpy as jnp
from jax import lax

TILE_CELLS = 4096
LAGS = 2
SPAN_HOURS = 4
OBS_BLK = 4
KSLOT = 4
NTILES = 512
BLK_DEV = 8
HOURS = 5
TILE_DEV = 128
BLOCKS = 256
CAP = 16


def storage_order(key):
    return jax.random.permutation(jax.random.fold_in(key, 11), NTILES).astype(jnp.int32)


def draw_tile_row(key, part):
    return storage_order(key)


def draw_tile_list(key, part):
    storage = storage_order(key)
    inverse = jnp.argsort(storage, stable=True).astype(jnp.int32)
    owners = NTILES // TILE_DEV
    devices = BLOCKS // BLK_DEV
    columns = devices // owners
    slot_count = BLK_DEV * KSLOT
    owner_pool = jnp.arange(owners * CAP, dtype=jnp.int32) // CAP

    def one_device(device):
        column = device % columns
        hot_key = jax.random.fold_in(jax.random.fold_in(key, 29), column)
        hottest = jax.random.randint(hot_key, (), 0, owners)
        device_key = jax.random.fold_in(jax.random.fold_in(key, 37), device)
        first_key, second_key, third_key = jax.random.split(device_key, 3)
        ranking = jax.random.permutation(first_key, owners * CAP).astype(jnp.int32)
        scores = jnp.where(owner_pool == hottest, ranking - owners * CAP, ranking)
        chosen = owner_pool[jnp.argsort(scores, stable=True)][:slot_count]
        chosen = chosen[jax.random.permutation(second_key, slot_count)]
        samples = jax.random.randint(third_key, (3, slot_count), 0, TILE_DEV)
        local_index = jnp.min(samples, axis=0)
        return inverse[chosen * TILE_DEV + local_index].reshape(BLK_DEV, KSLOT)
    listed = jax.vmap(one_device)(jnp.arange(devices, dtype=jnp.int32))
    return listed.reshape(BLOCKS, KSLOT).astype(jnp.int32)


def place_ends(drawn, own_key, low, top_value):
    index_at = [jax.random.randint(jax.random.fold_in(own_key, axis), (), 0, length) for axis, length in enumerate(drawn.shape)]
    widest = drawn.shape.index(max(drawn.shape))
    beside = index_at[:widest] + [(index_at[widest] + 1) % drawn.shape[widest]] + index_at[widest + 1:]
    return drawn.at[tuple(index_at)].set(low).at[tuple(beside)].set(top_value)


def block_levels(own_key, extent, cuts, least, largest):
    factor_of = 1.0
    for dim, shards_of in cuts:
        heights = jax.random.uniform(jax.random.fold_in(jax.random.fold_in(own_key, 6), dim), (shards_of,), jnp.float32, least / len(cuts), largest / len(cuts))
        factor_of = factor_of * jnp.repeat(jnp.exp(heights), extent[dim] // shards_of).reshape((-1,) + (1,) * (len(extent) - 1 - dim))
    return factor_of


def bell_draw(stream_key, dims, scale, limit, cuts=(), kind=jnp.bfloat16):
    values = jax.random.normal(stream_key, dims, jnp.float32) * scale
    if len(cuts) > 0:
        values = block_levels(stream_key, dims, cuts, -0.22, 0.18) * values
    return jnp.clip(values, min=-limit, max=limit).astype(kind)


def setup_inputs(seed: int = 0) -> dict:
    streams_of = jax.random.split(jax.random.key(seed), 8)
    return {
        "footprint": jnp.clip(jnp.exp(math.log(0.049804688) - 4.6018058 * jax.random.uniform(streams_of[0], (BLOCKS, KSLOT, OBS_BLK, LAGS, TILE_CELLS), jnp.float32) ** block_levels(streams_of[0], (BLOCKS, KSLOT, OBS_BLK, LAGS, TILE_CELLS), ((0, 32),), -0.2, 0.2)), 0.00049972534, 0.049804688).astype(jnp.bfloat16),
        "obs_hour": place_ends(jax.random.randint(streams_of[1], (BLOCKS, OBS_BLK), 0, SPAN_HOURS), jax.random.fold_in(streams_of[1], 1), 0, SPAN_HOURS - 1).astype(jnp.int32),
        "tile_list": draw_tile_list(jax.random.fold_in(streams_of[7], 71), 0),
        "tile_row": draw_tile_row(jax.random.fold_in(streams_of[7], 71), 0),
        "flux": bell_draw(streams_of[4], (NTILES, HOURS, TILE_CELLS), 1.0, 6.0, ((0, 4),)),
        "observed": bell_draw(streams_of[5], (BLOCKS, OBS_BLK), 3.0, 18.0, ((0, 32),), jnp.float32),
        "obs_var": jnp.clip(jnp.exp(math.log(4.0) - 2.0794415 * jax.random.uniform(streams_of[6], (BLOCKS, OBS_BLK), jnp.float32) ** block_levels(streams_of[6], (BLOCKS, OBS_BLK), ((0, 32),), -0.2, 0.2)), 0.5, 4.0),
    }


def hour_select(hour_rows):
    target = hour_rows[:, :, None] + jnp.arange(LAGS, dtype=jnp.int32)[None, None, :]
    return (target[..., None] == jnp.arange(HOURS, dtype=jnp.int32)).astype(jnp.float32)


def reference(footprint, obs_hour, tile_list, tile_row, flux, observed, obs_var):
    groups = BLOCKS // BLK_DEV
    storage = tile_row[tile_list].astype(jnp.int32)
    foot_groups = footprint.reshape(groups, BLK_DEV, KSLOT, OBS_BLK, LAGS, TILE_CELLS)
    hour_groups = obs_hour.reshape(groups, BLK_DEV, OBS_BLK)
    row_groups = storage.reshape(groups, BLK_DEV, KSLOT)

    def forward(pieces):
        footprints, hour_rows, rows_here = pieces
        windows = flux[rows_here].astype(jnp.float32)
        select = hour_select(hour_rows)
        products = jnp.einsum("bkolc,bkhc->bkolh", footprints.astype(jnp.float32), windows, precision=lax.Precision.HIGHEST)
        partial_value = jnp.sum(products * select[:, None], axis=(3, 4))
        return jnp.sum(partial_value, axis=1)

    modeled = lax.map(forward, (foot_groups, hour_groups, row_groups)).reshape(BLOCKS, OBS_BLK)
    scaled = ((modeled - observed) / obs_var).astype(jnp.bfloat16)
    scaled_groups = scaled.reshape(groups, BLK_DEV, OBS_BLK)

    def adjoint(running, pieces):
        footprints, hour_rows, rows_here, scaled_here = pieces
        coefficient = (hour_select(hour_rows) * scaled_here.astype(jnp.float32)[:, :, None, None]).astype(jnp.bfloat16)
        contributions = jnp.einsum("bolh,bkolc->bkhc", coefficient.astype(jnp.float32), footprints.astype(jnp.float32), precision=lax.Precision.HIGHEST)
        updated = running.at[rows_here.reshape(-1)].add(contributions.reshape(BLK_DEV * KSLOT, HOURS, TILE_CELLS))
        return updated, jnp.zeros((), jnp.float32)

    start = jnp.zeros((NTILES, HOURS, TILE_CELLS), jnp.float32)
    gradient = lax.scan(adjoint, start, (foot_groups, hour_groups, row_groups, scaled_groups))[0]
    return modeled, gradient
```

```python
import functools

import jax
import jax.numpy as jnp
from jax import lax
from jax.experimental import pallas as pl
from jax.experimental.pallas import tpu as pltpu
from jax.sharding import PartitionSpec as P

LANES = 128
VMEM_BYTES = 48 * 1024 * 1024


def iota(shape, dim):
    return lax.broadcasted_iota(jnp.int32, shape, dim)


def pack_kernel(
    dims, list_ref, row_ref, hour_ref, seen_ref, var_ref, feet_ref, send_ref, meta_ref, place, count
):
    owners, columns, capacity, tiles, blocks, width, soundings, lags = dims
    per_slot = soundings * lags
    rows = capacity * per_slot

    @pl.when(pl.program_id(0) == 0)
    def _():
        shape = (owners * rows // LANES, LANES)
        flat = iota(shape, 0) * LANES + iota(shape, 1)
        slot_at, inner = flat // per_slot, flat % per_slot
        sounding, lag = inner // lags, inner % lags
        key_at = iota((1, blocks * width * per_slot), 1)
        key = jnp.zeros(key_at.shape, jnp.int32)
        target = jnp.full(shape, -1, jnp.int32)
        index = jnp.full(shape, -1, jnp.int32)
        seen = jnp.zeros(shape, jnp.float32)
        spread = jnp.ones(shape, jnp.float32)
        for o in range(owners):
            count[o] = 0
        for b in range(blocks):
            hours = jnp.zeros(shape, jnp.int32)
            block_seen = jnp.zeros(shape, jnp.float32)
            block_var = jnp.ones(shape, jnp.float32)
            for o in range(soundings):
                here = sounding == o
                hours = jnp.where(here, (hour_ref[o, b] + lag) * tiles, hours)
                block_seen = jnp.where(here, seen_ref[o, b], block_seen)
                block_var = jnp.where(here, var_ref[o, b], block_var)
            for k in range(width):
                stored = row_ref[list_ref[k, b]]
                owner = lax.div(stored, jnp.int32(tiles))
                position = count[owner]
                count[owner] = position + 1
                goes = owner * capacity + position
                here = slot_at == goes
                target = jnp.where(here, hours + (stored - owner * tiles), target)
                index = jnp.where(here, b * soundings + sounding, index)
                seen = jnp.where(here, block_seen, seen)
                spread = jnp.where(here, block_var, spread)
                key = jnp.where(
                    key_at // per_slot == b * width + k, goes * per_slot + key_at % per_slot, key
                )
        place[...] = (iota(place.shape, 0) == key).astype(jnp.bfloat16)
        fields = (target.astype(jnp.float32), index.astype(jnp.float32), seen, spread)
        for o in range(owners):
            first = o * rows
            for f, field in enumerate(fields):
                part = field[
                    first // LANES : first // LANES + 1, first % LANES : first % LANES + rows
                ]
                meta_ref[o, :, f, :] = jnp.broadcast_to(part, (columns, rows))

    packed = jnp.dot(place[...], feet_ref[...], preferred_element_type=jnp.float32)
    send_ref[...] = packed.astype(jnp.bfloat16).reshape(send_ref.shape)


def forward_kernel(dims, at_ref, meta_ref, flux_ref, feet_ref, out_ref, acc):
    rows, copies, devices, states = dims
    step = pl.program_id(0)
    hours, tiles, cells = flux_ref.shape
    pieces = feet_ref.shape[0] // LANES
    per_piece = LANES // rows
    lane = iota((8, LANES), 1)

    @pl.when(step == 0)
    def _():
        acc[...] = jnp.zeros_like(acc)

    products = lax.dot_general(
        flux_ref[...].reshape(hours * tiles, cells),
        feet_ref[...],
        (((1,), (1,)), ((), ())),
        preferred_element_type=jnp.float32,
    )
    level = iota((hours * tiles, LANES), 0)
    for n in range(pieces):
        piece = step * pieces + n
        target = meta_ref[0, pl.ds(piece, 1), :].astype(jnp.int32)
        index = meta_ref[1, pl.ds(piece, 1), :].astype(jnp.int32)
        chosen = jnp.where(level == target, products[:, n * LANES : (n + 1) * LANES], 0.0)
        partial = jnp.sum(chosen, axis=0, keepdims=True)
        for part in range(per_piece):
            device = piece * per_piece + part
            block = pl.ds(pl.multiple_of(device // 32 * 8, 8), 8)
            total = acc[block, :]
            for q in range(states // 8):
                mine = (index == q * 8 + iota((8, LANES), 0)) & (lane // rows == part)
                column = jnp.sum(jnp.where(mine, partial, 0.0), axis=1, keepdims=True)
                total = jnp.where(lane == q * 32 + device % 32, column, total)
            acc[block, :] = total

    @pl.when(step == pl.num_programs(0) - 1)
    def _():
        out_ref[...] = jnp.broadcast_to(acc[...][None], out_ref.shape)


def adjoint_kernel(dims, at_ref, sums_ref, meta_ref, feet_ref, modeled_ref, grad_ref, model, coef):
    rows, devices, states, soundings = dims
    step = pl.program_id(0)
    hours, tiles, cells = grad_ref.shape
    pieces = feet_ref.shape[0] // LANES
    per_piece = LANES // rows
    lane = iota((8, LANES), 1)

    @pl.when(step == 0)
    def _():
        model[...] = jnp.sum(sums_ref[...], axis=0)
        me = at_ref[0]
        own = model[pl.ds(pl.multiple_of(me // 32 * 8, 8), 8), :]
        result = jnp.zeros(modeled_ref.shape, jnp.float32)
        at_block = iota(modeled_ref.shape, 1)
        for q in range(states // 8):
            column = jnp.sum(
                jnp.where(lane == q * 32 + me % 32, own, 0.0), axis=1, keepdims=True
            )
            for half in range(8 // soundings):
                part = column[half * soundings : (half + 1) * soundings]
                result = jnp.where(at_block == q * (8 // soundings) + half, part, result)
        modeled_ref[...] = result

    level = iota((hours * tiles, LANES), 0)
    for n in range(pieces):
        piece = step * pieces + n
        target = meta_ref[0, pl.ds(piece, 1), :].astype(jnp.int32)
        index = meta_ref[1, pl.ds(piece, 1), :].astype(jnp.int32)
        gathered = jnp.zeros((8, LANES), jnp.float32)
        for part in range(per_piece):
            device = piece * per_piece + part
            block = model[pl.ds(pl.multiple_of(device // 32 * 8, 8), 8), :]
            for q in range(states // 8):
                column = jnp.sum(
                    jnp.where(lane == q * 32 + device % 32, block, 0.0), axis=1, keepdims=True
                )
                mine = (index == q * 8 + iota((8, LANES), 0)) & (lane // rows == part)
                gathered = jnp.where(mine, column, gathered)
        value = jnp.sum(gathered, axis=0, keepdims=True)
        seen = meta_ref[2, pl.ds(piece, 1), :]
        spread = meta_ref[3, pl.ds(piece, 1), :]
        scaled = ((value - seen) / spread).astype(jnp.bfloat16).astype(jnp.float32)
        coef[:, n * LANES : (n + 1) * LANES] = jnp.where(level == target, scaled, 0.0).astype(
            jnp.bfloat16
        )
    terms = jnp.dot(coef[...], feet_ref[...], preferred_element_type=jnp.float32)
    terms = terms.reshape(grad_ref.shape)

    @pl.when(step == 0)
    def _():
        grad_ref[...] = terms

    @pl.when(step > 0)
    def _():
        grad_ref[...] += terms


def shards(footprint, obs_hour, tile_list, tile_row, flux, observed, obs_var):
    owners, columns = lax.axis_size("flux"), lax.axis_size("obs")
    devices = owners * columns
    blocks, width, soundings, lags, cells = footprint.shape
    tiles, hours = flux.shape[:2]
    capacity = 2 * blocks * width // owners
    per_slot = soundings * lags
    rows = capacity * per_slot
    part = cells // columns
    states = blocks * soundings
    both = ("flux", "obs")
    params = pltpu.CompilerParams(vmem_limit_bytes=VMEM_BYTES)
    smem = pl.BlockSpec(memory_space=pltpu.SMEM)

    send, meta = pl.pallas_call(
        functools.partial(
            pack_kernel, (owners, columns, capacity, tiles, blocks, width, soundings, lags)
        ),
        grid=(columns,),
        out_shape=(
            jax.ShapeDtypeStruct((owners, columns, rows, part), jnp.bfloat16),
            jax.ShapeDtypeStruct((owners, columns, 4, rows), jnp.float32),
        ),
        in_specs=[smem] * 5
        + [pl.BlockSpec((blocks * width * per_slot, part), lambda j: (0, j))],
        out_specs=(
            pl.BlockSpec((owners, 1, rows, part), lambda j: (0, j, 0, 0)),
            pl.BlockSpec((owners, columns, 4, rows), lambda j: (0, 0, 0, 0)),
        ),
        scratch_shapes=[
            pltpu.VMEM((owners * rows, blocks * width * per_slot), jnp.bfloat16),
            pltpu.SMEM((owners,), jnp.int32),
        ],
        compiler_params=params,
        name="pack",
    )(
        tile_list.T,
        tile_row,
        obs_hour.T,
        observed.T,
        obs_var.T,
        footprint.reshape(blocks * width * per_slot, cells),
    )
    feet = lax.all_to_all(
        send.reshape(devices, rows, part), both, split_axis=0, concat_axis=0, tiled=True
    ).reshape(devices * rows, part)
    meta = lax.all_to_all(
        meta.reshape(devices, 4, rows), both, split_axis=0, concat_axis=0, tiled=True
    )
    meta = meta.transpose(1, 0, 2).reshape(4, devices * rows // LANES, LANES)

    total = devices * rows
    chunk = min(1024, total)
    pages = states * devices // LANES
    one_shot = devices <= 64
    copies = devices if one_shot else 1
    at = jnp.stack([lax.axis_index("flux") * columns + lax.axis_index("obs"), lax.axis_index("obs")])
    sums = pl.pallas_call(
        functools.partial(forward_kernel, (rows, copies, devices, states)),
        grid_spec=pltpu.PrefetchScalarGridSpec(
            num_scalar_prefetch=1,
            grid=(total // chunk,),
            in_specs=[
                pl.BlockSpec(meta.shape, lambda i, at: (0, 0, 0)),
                pl.BlockSpec((hours, tiles, part), lambda i, at: (0, 0, at[1])),
                pl.BlockSpec((chunk, part), lambda i, at: (i, 0)),
            ],
            out_specs=pl.BlockSpec((copies, pages, LANES), lambda i, at: (0, 0, 0)),
            scratch_shapes=[pltpu.VMEM((pages, LANES), jnp.float32)],
        ),
        out_shape=jax.ShapeDtypeStruct((copies, pages, LANES), jnp.float32),
        compiler_params=params,
        name="forward",
    )(at, meta, flux.transpose(1, 0, 2), feet)
    if one_shot:
        sums = lax.all_to_all(sums, both, split_axis=0, concat_axis=0, tiled=True)
    else:
        sums = lax.psum(sums, both)
    modeled, gradient = pl.pallas_call(
        functools.partial(adjoint_kernel, (rows, devices, states, soundings)),
        grid_spec=pltpu.PrefetchScalarGridSpec(
            num_scalar_prefetch=1,
            grid=(total // chunk,),
            in_specs=[
                pl.BlockSpec((copies, pages, LANES), lambda i, at: (0, 0, 0)),
                pl.BlockSpec(meta.shape, lambda i, at: (0, 0, 0)),
                pl.BlockSpec((chunk, part), lambda i, at: (i, 0)),
            ],
            out_specs=(
                pl.BlockSpec((soundings, blocks), lambda i, at: (0, 0)),
                pl.BlockSpec((hours, tiles, part), lambda i, at: (0, 0, 0)),
            ),
            scratch_shapes=[
                pltpu.VMEM((pages, LANES), jnp.float32),
                pltpu.VMEM((hours * tiles, chunk), jnp.bfloat16),
            ],
        ),
        out_shape=(
            jax.ShapeDtypeStruct((soundings, blocks), jnp.float32),
            jax.ShapeDtypeStruct((hours, tiles, part), jnp.float32),
        ),
        compiler_params=params,
        name="adjoint",
    )(at, sums, meta, feet)
    return modeled.T, gradient.transpose(1, 0, 2)


def solution(mesh):
    placed = (
        P(("flux", "obs"), None, None, None, None),
        P(("flux", "obs"), None),
        P(("flux", "obs"), None),
        P(),
        P("flux", None, None),
        P(("flux", "obs"), None),
        P(("flux", "obs"), None),
    )
    return jax.shard_map(
        shards,
        mesh=mesh,
        in_specs=placed,
        out_specs=(P(("flux", "obs"), None), P("flux", None, "obs")),
        check_vma=False,
    )
```

```python
import functools

import jax
import jax.numpy as jnp
from jax import lax
from jax.experimental import pallas as pl
from jax.experimental.pallas import tpu as pltpu
from jax.sharding import PartitionSpec as P

LANES = 128
VMEM_BYTES = 48 * 1024 * 1024
LEVELS = (5, 6, 7, 8, 9, 10, 12, 14, 16)


def iota(shape, dim):
    return lax.broadcasted_iota(jnp.int32, shape, dim)


def thirds(value):
    high = value.astype(jnp.bfloat16).astype(jnp.float32)
    rest = value - high
    middle = rest.astype(jnp.bfloat16).astype(jnp.float32)
    return high, middle, (rest - middle).astype(jnp.bfloat16).astype(jnp.float32)


class Sizes:
    def __init__(self, owners, columns, footprint, flux):
        self.owners, self.columns = owners, columns
        self.devices = owners * columns
        self.blocks, self.width, self.soundings, self.lags, cells = footprint
        self.tiles, self.hours = flux[0], flux[1]
        self.span = self.hours - self.lags + 1
        self.half = self.span * self.tiles // 2
        self.slots = self.blocks * self.width
        self.per_slot = self.soundings * self.lags
        self.part = cells // columns
        self.lane_tiles = self.part // LANES
        self.first = self.slots // owners
        self.rows = self.first * self.per_slot
        self.spill = self.slots // 2 * self.per_slot
        self.second = columns * self.first * self.per_slot
        self.notes = 8 * (self.second // self.part)
        self.states = self.blocks * self.soundings
        self.per_page = 8 * LANES // self.states
        self.pages = self.devices // self.per_page


def read_notes(sizes, notes, plane):
    lane = iota((1, notes.shape[1]), 1)
    inner = lax.rem(lane, jnp.int32(sizes.per_slot))
    base = notes[0:1]
    target = (base + sizes.half).astype(jnp.int32) + lax.rem(inner, jnp.int32(sizes.lags)) * sizes.tiles
    target = jnp.where(base > sizes.half - 0.5, -1, target)
    place = notes[1:2].astype(jnp.int32)
    block = lax.rem(place, jnp.int32(sizes.blocks))
    device = plane * sizes.columns + lax.div(place, jnp.int32(sizes.blocks))
    state = block * sizes.soundings + lax.div(inner, jnp.int32(sizes.lags))
    row = lax.div(device, jnp.int32(sizes.per_page)) * 8 + lax.rem(state, jnp.int32(8))
    column = lax.div(state, jnp.int32(8)) * sizes.per_page + lax.rem(device, jnp.int32(sizes.per_page))
    return target, row, column


def first_round(sizes, ref, step):
    sources, count = ref.shape[0], sizes.rows
    feet = jnp.concatenate(
        [
            ref[:, n * count : (n + 1) * count, :].reshape(sources * count, LANES)
            for n in range(sizes.lane_tiles)
        ],
        axis=1,
    )
    end = sizes.lane_tiles * count
    notes = jnp.concatenate(
        [ref[s, end : end + 8, :].astype(jnp.float32)[:, :count] for s in range(sources)], axis=1
    )
    lane = iota((1, sources * count), 1)
    plane = lax.div(step * sources + lax.div(lane, jnp.int32(count)), jnp.int32(sizes.columns))
    return feet, notes, plane


def second_round(sizes, ref):
    count = ref.shape[1] - sizes.notes
    notes = jnp.concatenate(
        [ref[0, n * 8 : (n + 1) * 8, :].astype(jnp.float32) for n in range(sizes.notes // 8)], axis=1
    )
    return ref[0, sizes.notes :, :], notes[:, :count]


def partial_sums(sizes, flux_ref, feet, notes, plane):
    target, row, column = read_notes(sizes, notes, plane)
    count = feet.shape[0]
    levels = sizes.hours * sizes.tiles
    products = lax.dot_general(
        flux_ref[...].reshape(levels, sizes.part),
        feet,
        (((1,), (1,)), ((), ())),
        preferred_element_type=jnp.float32,
    )
    chosen = jnp.where(iota((levels, count), 0) == target, products, 0.0)
    partial = jnp.sum(chosen, axis=0, keepdims=True)
    height = 8 * sizes.pages
    spread = jnp.where(iota((height, count), 0) == row, partial, 0.0)
    terms = jnp.concatenate(thirds(spread), axis=0).astype(jnp.bfloat16)
    lanes = (iota((LANES, count), 0) == column).astype(jnp.bfloat16)
    sums = lax.dot_general(
        terms, lanes, (((1,), (1,)), ((), ())), preferred_element_type=jnp.float32
    )
    return sums[:height] + sums[height : 2 * height] + sums[2 * height :]


def gradient_terms(sizes, model, feet, notes, plane):
    target, row, column = read_notes(sizes, notes, plane)
    count = feet.shape[0]
    height = 8 * sizes.pages
    lanes = (iota((LANES, count), 0) == column).astype(jnp.bfloat16)
    taken = jnp.dot(model, lanes, preferred_element_type=jnp.float32)
    taken = taken[:height] + taken[height : 2 * height] + taken[2 * height :]
    value = jnp.sum(
        jnp.where(iota((height, count), 0) == row, taken, 0.0), axis=0, keepdims=True
    )
    seen = notes[2:3] + notes[3:4] + notes[4:5]
    spread = notes[5:6] + notes[6:7] + notes[7:8]
    scaled = ((value - seen) / spread).astype(jnp.bfloat16).astype(jnp.float32)
    levels = sizes.hours * sizes.tiles
    coefficient = jnp.where(iota((levels, count), 0) == target, scaled, 0.0).astype(jnp.bfloat16)
    return jnp.dot(coefficient, feet, preferred_element_type=jnp.float32)


def pack_kernel(
    sizes, at_ref, list_ref, row_ref, hour_ref, seen_ref, var_ref, feet_ref, send_ref, *rest
):
    spills = rest[: sizes.columns]
    place, first_notes, spill_notes, count = rest[sizes.columns :]
    owners, per_slot = sizes.owners, sizes.per_slot
    step = pl.program_id(0)

    @pl.when(step == 0)
    def _():
        field, lane = iota((16, LANES), 0), iota((16, LANES), 1)
        inner = lane % per_slot
        sounding = inner // sizes.lags
        slot_at = lane // per_slot
        key_at = iota((1, sizes.slots * per_slot), 1)
        key = jnp.zeros(key_at.shape, jnp.int32)
        empty = jnp.where(field == 0, jnp.float32(sizes.half), 0.0)
        empty = jnp.where(field == 5, 1.0, jnp.where(field == 8, -1.0, empty))
        for o in range(owners):
            count[o] = 0
            first_notes[o] = empty[:8]
        count[owners] = 0
        left = empty
        for b in range(sizes.blocks):
            base = jnp.zeros(field.shape, jnp.float32)
            seen = jnp.zeros(field.shape, jnp.float32)
            spread = jnp.ones(field.shape, jnp.float32)
            for o in range(sizes.soundings):
                here = sounding == o
                hour = hour_ref[o, b] * sizes.tiles - sizes.half
                base = jnp.where(here, hour.astype(jnp.float32), base)
                seen = jnp.where(here, seen_ref[o, b], seen)
                spread = jnp.where(here, var_ref[o, b], spread)
            column = (b + sizes.blocks * at_ref[1]).astype(jnp.float32)
            pattern = jnp.where(field == 0, base, jnp.where(field == 1, column, 0.0))
            for n, term in enumerate(thirds(seen) + thirds(spread)):
                pattern = jnp.where(field == 2 + n, term, pattern)
            for k in range(sizes.width):
                stored = row_ref[list_ref[k, b]]
                owner = lax.div(stored, jnp.int32(sizes.tiles))
                tile = (stored - owner * sizes.tiles).astype(jnp.float32)
                position = count[owner]
                count[owner] = position + 1
                keep = position < sizes.first
                over = count[owners]
                count[owners] = over + jnp.where(keep, 0, 1)
                goes = jnp.where(
                    keep, owner * sizes.first + position, owners * sizes.first + over
                )
                value = jnp.where(field == 0, pattern + tile, pattern)
                value = jnp.where(field == 8, owner.astype(jnp.float32), value)
                value = jnp.where(
                    field == 9, (position - sizes.first).astype(jnp.float32), value
                )
                first_notes[owner] = jnp.where(
                    slot_at[:8] == jnp.where(keep, position, -1), value[:8], first_notes[owner]
                )
                left = jnp.where(slot_at == jnp.where(keep, -1, over), value, left)
                key = jnp.where(
                    key_at // per_slot == b * sizes.width + k,
                    goes * per_slot + key_at % per_slot,
                    key,
                )
        spill_notes[...] = left
        place[...] = (iota(place.shape, 0) == key).astype(jnp.bfloat16)

    packed = jnp.dot(place[...], feet_ref[...], preferred_element_type=jnp.float32)
    packed = packed.astype(jnp.bfloat16)
    rows = sizes.rows
    end = sizes.lane_tiles * rows
    for o in range(owners):
        for n in range(sizes.lane_tiles):
            send_ref[o, 0, n * rows : (n + 1) * rows, :] = packed[
                o * rows : (o + 1) * rows, n * LANES : (n + 1) * LANES
            ]
        send_ref[o, 0, end : end + 8, :] = first_notes[o].astype(jnp.bfloat16)
    for d in range(sizes.columns):

        @pl.when(step == d)
        def _():
            for n in range(sizes.lane_tiles):
                spills[d][n * sizes.spill : (n + 1) * sizes.spill, :] = packed[
                    owners * rows :, n * LANES : (n + 1) * LANES
                ]
            end = sizes.lane_tiles * sizes.spill
            spills[d][end : end + 16, :] = spill_notes[...].astype(jnp.bfloat16)


def regroup_kernel(sizes, *refs):
    spills = refs[: sizes.columns]
    send_ref, total_ref, feet, notes, place = refs[sizes.columns :]
    owner = pl.program_id(0)
    spill = sizes.spill
    end = sizes.lane_tiles * spill

    @pl.when(owner == 0)
    def _():
        for d, ref in enumerate(spills):
            for n in range(sizes.lane_tiles):
                feet[d * spill : (d + 1) * spill, n * LANES : (n + 1) * LANES] = ref[
                    n * spill : (n + 1) * spill, :
                ]
            notes[:, d * spill : (d + 1) * spill] = ref[end : end + 16, :].astype(jnp.float32)
        total_ref[...] = jnp.zeros_like(total_ref)

    mine = notes[8:9, :] == owner.astype(jnp.float32)
    total = jnp.zeros((1, 1), jnp.float32)
    keys = []
    for d in range(sizes.columns):
        here = mine[:, d * spill : (d + 1) * spill]
        position = total + notes[9:10, d * spill : (d + 1) * spill]
        inner = lax.rem(iota((1, spill), 1), jnp.int32(sizes.per_slot))
        keys.append(
            jnp.where(here, position.astype(jnp.int32) * sizes.per_slot + inner, -1)
        )
        total = total + jnp.sum(
            jnp.where(here, 1.0 / sizes.per_slot, 0.0), axis=1, keepdims=True
        )
    key = jnp.concatenate(keys, axis=1)
    place[...] = (iota(place.shape, 0) == key).astype(jnp.bfloat16)
    send_ref[0, sizes.notes :, :] = jnp.dot(
        place[...], feet[...], preferred_element_type=jnp.float32
    ).astype(jnp.bfloat16)
    moved = lax.dot_general(
        notes[0:8, :].astype(jnp.bfloat16),
        place[...],
        (((1,), (1,)), ((), ())),
        preferred_element_type=jnp.float32,
    )
    field, lane = iota(moved.shape, 0), iota(moved.shape, 1)
    empty = jnp.where(field == 0, jnp.float32(sizes.half), jnp.where(field == 5, 1.0, 0.0))
    moved = jnp.where(lane.astype(jnp.float32) < total * sizes.per_slot, moved, empty)
    moved = moved.astype(jnp.bfloat16)
    for n in range(sizes.notes // 8):
        send_ref[0, n * 8 : (n + 1) * 8, :] = moved[:, n * sizes.part : (n + 1) * sizes.part]
    total_ref[...] = jnp.maximum(total_ref[...], total)


def forward_first_kernel(sizes, at_ref, flux_ref, got_ref, out_ref):
    step = pl.program_id(0)
    feet, notes, plane = first_round(sizes, got_ref, step)
    sums = partial_sums(sizes, flux_ref, feet, notes, plane)

    @pl.when(step == 0)
    def _():
        out_ref[...] = sums

    @pl.when(step > 0)
    def _():
        out_ref[...] += sums


def forward_second_kernel(sizes, at_ref, flux_ref, got_ref, before_ref, out_ref, total):
    plane = pl.program_id(0)
    feet, notes = second_round(sizes, got_ref)
    sums = partial_sums(sizes, flux_ref, feet, notes, plane)

    @pl.when(plane == 0)
    def _():
        total[...] = before_ref[...] + sums

    @pl.when(plane > 0)
    def _():
        total[...] += sums

    @pl.when(plane == pl.num_programs(0) - 1)
    def _():
        out_ref[...] = jnp.broadcast_to(total[...][None], out_ref.shape)


def adjoint_kernel(
    sizes, chunks, at_ref, sums_ref, one_ref, two_ref, modeled_ref, grad_ref, model
):
    step = pl.program_id(0)

    @pl.when(step == 0)
    def _():
        sums = jnp.sum(sums_ref[...], axis=0)
        model[...] = jnp.concatenate(thirds(sums), axis=0).astype(jnp.bfloat16)
        me = at_ref[0]
        page, within = lax.div(me, sizes.per_page), lax.rem(me, sizes.per_page)
        lane = iota((8, LANES), 1)
        own = jnp.zeros((8, LANES), jnp.float32)
        for p in range(sizes.pages):
            own = jnp.where(page == p, sums[p * 8 : (p + 1) * 8], own)
        result = jnp.zeros(modeled_ref.shape, jnp.float32)
        at_block = iota(modeled_ref.shape, 1)
        each = 8 // sizes.soundings
        for q in range(sizes.states // 8):
            picked = jnp.where(lane == q * sizes.per_page + within, own, 0.0)
            column = jnp.sum(picked, axis=1, keepdims=True)
            for n in range(each):
                values = column[n * sizes.soundings : (n + 1) * sizes.soundings]
                result = jnp.where(at_block == q * each + n, values, result)
        modeled_ref[...] = result

    @pl.when(step < chunks)
    def _():
        feet, notes, plane = first_round(sizes, one_ref, step)
        terms = gradient_terms(sizes, model[...], feet, notes, plane).reshape(grad_ref.shape)

        @pl.when(step == 0)
        def _():
            grad_ref[...] = terms

        @pl.when(step > 0)
        def _():
            grad_ref[...] += terms

    @pl.when(step >= chunks)
    def _():
        feet, notes = second_round(sizes, two_ref)
        terms = gradient_terms(sizes, model[...], feet, notes, step - chunks)
        grad_ref[...] += terms.reshape(grad_ref.shape)


def shards(footprint, obs_hour, tile_list, tile_row, flux, observed, obs_var):
    sizes = Sizes(
        lax.axis_size("flux"), lax.axis_size("obs"), footprint.shape, flux.shape
    )
    owners, columns, devices, part = sizes.owners, sizes.columns, sizes.devices, sizes.part
    both = ("flux", "obs")
    params = pltpu.CompilerParams(vmem_limit_bytes=VMEM_BYTES)
    smem = pl.BlockSpec(memory_space=pltpu.SMEM)
    me = lax.axis_index("flux") * columns + lax.axis_index("obs")
    at = jnp.stack([me, lax.axis_index("obs")])
    flux = flux.transpose(1, 0, 2)

    first_height = sizes.lane_tiles * sizes.rows + 8
    spill_height = sizes.lane_tiles * sizes.spill + 16
    all_slots = sizes.slots * sizes.per_slot
    send, *spills = pl.pallas_call(
        functools.partial(pack_kernel, sizes),
        grid_spec=pltpu.PrefetchScalarGridSpec(
            num_scalar_prefetch=1,
            grid=(columns,),
            in_specs=[smem] * 5
            + [pl.BlockSpec((all_slots, part), lambda d, at: (0, d ^ at[1]))],
            out_specs=[
                pl.BlockSpec((owners, 1, first_height, LANES), lambda d, at: (0, d ^ at[1], 0, 0))
            ]
            + [pl.BlockSpec((spill_height, LANES), lambda d, at: (0, 0))] * columns,
            scratch_shapes=[
                pltpu.VMEM((owners * sizes.rows + sizes.spill, all_slots), jnp.bfloat16),
                pltpu.VMEM((owners, 8, LANES), jnp.float32),
                pltpu.VMEM((16, LANES), jnp.float32),
                pltpu.SMEM((owners + 1,), jnp.int32),
            ],
        ),
        out_shape=[jax.ShapeDtypeStruct((owners, columns, first_height, LANES), jnp.bfloat16)]
        + [jax.ShapeDtypeStruct((spill_height, LANES), jnp.bfloat16)] * columns,
        compiler_params=params,
        name="pack",
    )(
        at,
        tile_list.T,
        tile_row,
        obs_hour.T,
        observed.T,
        obs_var.T,
        footprint.reshape(all_slots, sizes.lane_tiles * columns * LANES),
    )
    got = lax.all_to_all(
        send.reshape(devices, first_height, LANES), both, split_axis=0, concat_axis=0, tiled=True
    )
    spills = spills[:1] + [
        lax.ppermute(spills[d], "obs", [(i, i ^ d) for i in range(columns)])
        for d in range(1, columns)
    ]
    second_height = sizes.notes + sizes.second
    send_second, total = pl.pallas_call(
        functools.partial(regroup_kernel, sizes),
        grid=(owners,),
        in_specs=[pl.BlockSpec((spill_height, LANES), lambda o: (0, 0))] * columns,
        out_specs=(
            pl.BlockSpec((1, second_height, part), lambda o: (o, 0, 0)),
            pl.BlockSpec((8, LANES), lambda o: (0, 0)),
        ),
        out_shape=(
            jax.ShapeDtypeStruct((owners, second_height, part), jnp.bfloat16),
            jax.ShapeDtypeStruct((8, LANES), jnp.float32),
        ),
        scratch_shapes=[
            pltpu.VMEM((columns * sizes.spill, part), jnp.bfloat16),
            pltpu.VMEM((16, columns * sizes.spill), jnp.float32),
            pltpu.VMEM((sizes.second, columns * sizes.spill), jnp.bfloat16),
        ],
        compiler_params=params,
        name="regroup",
    )(*spills)
    apart = 1
    while apart < owners:
        other = lax.ppermute(total, "flux", [(i, i ^ apart) for i in range(owners)])
        total = jnp.maximum(total, other)
        apart *= 2
    most = columns * sizes.first
    needed = total[0, 0]
    level = sum((needed > n * most // 16).astype(jnp.int32) for n in LEVELS[:-1])

    sources = min(devices, 1024 // sizes.rows)
    chunks = devices // sources
    copies = devices if devices <= 64 else 1
    height = 8 * sizes.pages
    flux_spec = pl.BlockSpec((sizes.hours, sizes.tiles, part), lambda i, at: (0, 0, at[1]))

    def finish(sixteenths):
        count = sizes.notes + sizes.second * sixteenths // 16

        def run(flux, got, send_second, at):
            got_second = lax.all_to_all(
                send_second[:, :count], "flux", split_axis=0, concat_axis=0, tiled=True
            )
            early = pl.pallas_call(
                functools.partial(forward_first_kernel, sizes),
                grid_spec=pltpu.PrefetchScalarGridSpec(
                    num_scalar_prefetch=1,
                    grid=(chunks,),
                    in_specs=[
                        flux_spec,
                        pl.BlockSpec((sources, first_height, LANES), lambda i, at: (i, 0, 0)),
                    ],
                    out_specs=pl.BlockSpec((height, LANES), lambda i, at: (0, 0)),
                ),
                out_shape=jax.ShapeDtypeStruct((height, LANES), jnp.float32),
                compiler_params=params,
                name="forward_first",
            )(at, flux, got)
            sums = pl.pallas_call(
                functools.partial(forward_second_kernel, sizes),
                grid_spec=pltpu.PrefetchScalarGridSpec(
                    num_scalar_prefetch=1,
                    grid=(owners,),
                    in_specs=[
                        flux_spec,
                        pl.BlockSpec((1, count, part), lambda i, at: (i, 0, 0)),
                        pl.BlockSpec((height, LANES), lambda i, at: (0, 0)),
                    ],
                    out_specs=pl.BlockSpec((copies, height, LANES), lambda i, at: (0, 0, 0)),
                    scratch_shapes=[pltpu.VMEM((height, LANES), jnp.float32)],
                ),
                out_shape=jax.ShapeDtypeStruct((copies, height, LANES), jnp.float32),
                compiler_params=params,
                name="forward_second",
            )(at, flux, got_second, early)
            if copies > 1:
                sums = lax.all_to_all(sums, both, split_axis=0, concat_axis=0, tiled=True)
            else:
                sums = lax.psum(sums, both)
            return pl.pallas_call(
                functools.partial(adjoint_kernel, sizes, chunks),
                grid_spec=pltpu.PrefetchScalarGridSpec(
                    num_scalar_prefetch=1,
                    grid=(chunks + owners,),
                    in_specs=[
                        pl.BlockSpec((copies, height, LANES), lambda i, at: (0, 0, 0)),
                        pl.BlockSpec(
                            (sources, first_height, LANES),
                            lambda i, at: (jnp.minimum(i, chunks - 1), 0, 0),
                        ),
                        pl.BlockSpec(
                            (1, count, part), lambda i, at: (jnp.maximum(i - chunks, 0), 0, 0)
                        ),
                    ],
                    out_specs=(
                        pl.BlockSpec((sizes.soundings, sizes.blocks), lambda i, at: (0, 0)),
                        pl.BlockSpec((sizes.hours, sizes.tiles, part), lambda i, at: (0, 0, 0)),
                    ),
                    scratch_shapes=[pltpu.VMEM((3 * height, LANES), jnp.bfloat16)],
                ),
                out_shape=(
                    jax.ShapeDtypeStruct((sizes.soundings, sizes.blocks), jnp.float32),
                    jax.ShapeDtypeStruct((sizes.hours, sizes.tiles, part), jnp.float32),
                ),
                compiler_params=params,
                name="adjoint",
            )(at, sums, got, got_second)

        return run

    modeled, gradient = lax.switch(
        level, [finish(n) for n in LEVELS], flux, got, send_second, at
    )
    return modeled.T, gradient.transpose(1, 0, 2)


def solution(mesh):
    placed = (
        P(("flux", "obs"), None, None, None, None),
        P(("flux", "obs"), None),
        P(("flux", "obs"), None),
        P(),
        P("flux", None, None),
        P(("flux", "obs"), None),
        P(("flux", "obs"), None),
    )
    return jax.shard_map(
        shards,
        mesh=mesh,
        in_specs=placed,
        out_specs=(P(("flux", "obs"), None), P("flux", None, "obs")),
        check_vma=False,
    )
```

```python
import functools

import jax
import jax.numpy as jnp
from jax import lax
from jax.experimental import pallas as pl
from jax.experimental.pallas import tpu as pltpu
from jax.sharding import PartitionSpec as P

LANES = 128
VMEM_BYTES = 48 * 1024 * 1024
LEVELS = (5, 6, 7, 8, 9, 10, 12, 14, 16)


def iota(shape, dim):
    return lax.broadcasted_iota(jnp.int32, shape, dim)


def thirds(value):
    high = value.astype(jnp.bfloat16).astype(jnp.float32)
    rest = value - high
    middle = rest.astype(jnp.bfloat16).astype(jnp.float32)
    return high, middle, (rest - middle).astype(jnp.bfloat16).astype(jnp.float32)


class Sizes:
    def __init__(self, owners, columns, footprint, flux):
        self.owners, self.columns = owners, columns
        self.devices = owners * columns
        self.blocks, self.width, self.soundings, self.lags, cells = footprint
        self.tiles, self.hours = flux[0], flux[1]
        self.span = self.hours - self.lags + 1
        self.half = self.span * self.tiles // 2
        self.slots = self.blocks * self.width
        self.per_slot = self.soundings * self.lags
        self.part = cells // columns
        self.lane_tiles = self.part // LANES
        self.first = self.slots // owners
        self.rows = self.first * self.per_slot
        self.spill = self.slots // 2 * self.per_slot
        self.second = columns * self.first * self.per_slot
        self.notes = 8 * (self.second // self.part)
        self.states = self.blocks * self.soundings
        self.per_page = 8 * LANES // self.states
        self.pages = self.devices // self.per_page


def read_notes(sizes, notes, plane):
    lane = iota((1, notes.shape[1]), 1)
    inner = lax.rem(lane, jnp.int32(sizes.per_slot))
    base = notes[0:1]
    target = (base + sizes.half).astype(jnp.int32) + lax.rem(inner, jnp.int32(sizes.lags)) * sizes.tiles
    target = jnp.where(base > sizes.half - 0.5, -1, target)
    place = notes[1:2].astype(jnp.int32)
    block = lax.rem(place, jnp.int32(sizes.blocks))
    device = plane * sizes.columns + lax.div(place, jnp.int32(sizes.blocks))
    state = block * sizes.soundings + lax.div(inner, jnp.int32(sizes.lags))
    row = lax.div(device, jnp.int32(sizes.per_page)) * 8 + lax.rem(state, jnp.int32(8))
    column = lax.div(state, jnp.int32(8)) * sizes.per_page + lax.rem(device, jnp.int32(sizes.per_page))
    return target, row, column


def first_round(sizes, ref, step):
    sources, count = ref.shape[0], sizes.rows
    feet = jnp.concatenate(
        [
            ref[:, n * count : (n + 1) * count, :].reshape(sources * count, LANES)
            for n in range(sizes.lane_tiles)
        ],
        axis=1,
    )
    end = sizes.lane_tiles * count
    notes = jnp.concatenate(
        [ref[s, end : end + 8, :].astype(jnp.float32)[:, :count] for s in range(sources)], axis=1
    )
    lane = iota((1, sources * count), 1)
    plane = lax.div(step * sources + lax.div(lane, jnp.int32(count)), jnp.int32(sizes.columns))
    return feet, notes, plane


def second_round(sizes, ref):
    planes, count = ref.shape[0], ref.shape[1] - sizes.notes
    feet = ref[:, sizes.notes :, :].reshape(planes * count, sizes.part)
    notes = []
    for p in range(planes):
        parts = [
            ref[p, n * 8 : (n + 1) * 8, :].astype(jnp.float32) for n in range(sizes.notes // 8)
        ]
        notes.append(jnp.concatenate(parts, axis=1)[:, :count])
    plane = lax.div(iota((1, planes * count), 1), jnp.int32(count))
    return feet, jnp.concatenate(notes, axis=1), plane


def partial_sums(sizes, flux_ref, feet, notes, plane):
    target, row, column = read_notes(sizes, notes, plane)
    count = feet.shape[0]
    levels = sizes.hours * sizes.tiles
    products = lax.dot_general(
        flux_ref[...].reshape(levels, sizes.part),
        feet,
        (((1,), (1,)), ((), ())),
        preferred_element_type=jnp.float32,
    )
    chosen = jnp.where(iota((levels, count), 0) == target, products, 0.0)
    partial = jnp.sum(chosen, axis=0, keepdims=True)
    height = 8 * sizes.pages
    spread = jnp.where(iota((height, count), 0) == row, partial, 0.0)
    terms = jnp.concatenate(thirds(spread), axis=0).astype(jnp.bfloat16)
    lanes = (iota((LANES, count), 0) == column).astype(jnp.bfloat16)
    sums = lax.dot_general(
        terms, lanes, (((1,), (1,)), ((), ())), preferred_element_type=jnp.float32
    )
    return sums[:height] + sums[height : 2 * height] + sums[2 * height :]


def gradient_terms(sizes, model, feet, notes, plane):
    target, row, column = read_notes(sizes, notes, plane)
    count = feet.shape[0]
    height = 8 * sizes.pages
    lanes = (iota((LANES, count), 0) == column).astype(jnp.bfloat16)
    taken = jnp.dot(model, lanes, preferred_element_type=jnp.float32)
    taken = taken[:height] + taken[height : 2 * height] + taken[2 * height :]
    value = jnp.sum(
        jnp.where(iota((height, count), 0) == row, taken, 0.0), axis=0, keepdims=True
    )
    seen = notes[2:3] + notes[3:4] + notes[4:5]
    spread = notes[5:6] + notes[6:7] + notes[7:8]
    scaled = ((value - seen) / spread).astype(jnp.bfloat16).astype(jnp.float32)
    levels = sizes.hours * sizes.tiles
    coefficient = jnp.where(iota((levels, count), 0) == target, scaled, 0.0).astype(jnp.bfloat16)
    return jnp.dot(coefficient, feet, preferred_element_type=jnp.float32)


def pack_kernel(
    sizes, at_ref, list_ref, row_ref, hour_ref, seen_ref, var_ref, feet_ref, send_ref, *rest
):
    spills = rest[: sizes.columns]
    place, first_notes, spill_notes, count = rest[sizes.columns :]
    owners, per_slot = sizes.owners, sizes.per_slot
    step = pl.program_id(0)

    @pl.when(step == 0)
    def _():
        field, lane = iota((16, LANES), 0), iota((16, LANES), 1)
        inner = lane % per_slot
        sounding = inner // sizes.lags
        slot_at = lane // per_slot
        key_at = iota((1, sizes.slots * per_slot), 1)
        key = jnp.zeros(key_at.shape, jnp.int32)
        empty = jnp.where(field == 0, jnp.float32(sizes.half), 0.0)
        empty = jnp.where(field == 5, 1.0, jnp.where(field == 8, -1.0, empty))
        for o in range(owners):
            count[o] = 0
            first_notes[o] = empty[:8]
        count[owners] = 0
        left = empty
        for b in range(sizes.blocks):
            base = jnp.zeros(field.shape, jnp.float32)
            seen = jnp.zeros(field.shape, jnp.float32)
            spread = jnp.ones(field.shape, jnp.float32)
            for o in range(sizes.soundings):
                here = sounding == o
                hour = hour_ref[o, b] * sizes.tiles - sizes.half
                base = jnp.where(here, hour.astype(jnp.float32), base)
                seen = jnp.where(here, seen_ref[o, b], seen)
                spread = jnp.where(here, var_ref[o, b], spread)
            column = (b + sizes.blocks * at_ref[1]).astype(jnp.float32)
            pattern = jnp.where(field == 0, base, jnp.where(field == 1, column, 0.0))
            for n, term in enumerate(thirds(seen) + thirds(spread)):
                pattern = jnp.where(field == 2 + n, term, pattern)
            for k in range(sizes.width):
                stored = row_ref[list_ref[k, b]]
                owner = lax.div(stored, jnp.int32(sizes.tiles))
                tile = (stored - owner * sizes.tiles).astype(jnp.float32)
                position = count[owner]
                count[owner] = position + 1
                keep = position < sizes.first
                over = count[owners]
                count[owners] = over + jnp.where(keep, 0, 1)
                goes = jnp.where(
                    keep, owner * sizes.first + position, owners * sizes.first + over
                )
                value = jnp.where(field == 0, pattern + tile, pattern)
                value = jnp.where(field == 8, owner.astype(jnp.float32), value)
                value = jnp.where(
                    field == 9, (position - sizes.first).astype(jnp.float32), value
                )
                first_notes[owner] = jnp.where(
                    slot_at[:8] == jnp.where(keep, position, -1), value[:8], first_notes[owner]
                )
                left = jnp.where(slot_at == jnp.where(keep, -1, over), value, left)
                key = jnp.where(
                    key_at // per_slot == b * sizes.width + k,
                    goes * per_slot + key_at % per_slot,
                    key,
                )
        spill_notes[...] = left
        place[...] = (iota(place.shape, 0) == key).astype(jnp.bfloat16)

    packed = jnp.dot(place[...], feet_ref[...], preferred_element_type=jnp.float32)
    packed = packed.astype(jnp.bfloat16)
    rows = sizes.rows
    end = sizes.lane_tiles * rows
    for o in range(owners):
        for n in range(sizes.lane_tiles):
            send_ref[o, 0, n * rows : (n + 1) * rows, :] = packed[
                o * rows : (o + 1) * rows, n * LANES : (n + 1) * LANES
            ]
        send_ref[o, 0, end : end + 8, :] = first_notes[o].astype(jnp.bfloat16)
    for d in range(sizes.columns):

        @pl.when(step == d)
        def _():
            for n in range(sizes.lane_tiles):
                spills[d][n * sizes.spill : (n + 1) * sizes.spill, :] = packed[
                    owners * rows :, n * LANES : (n + 1) * LANES
                ]
            end = sizes.lane_tiles * sizes.spill
            spills[d][end : end + 16, :] = spill_notes[...].astype(jnp.bfloat16)


def level_kernel(sizes, *refs):
    owners = jnp.concatenate([ref[8:9, :].astype(jnp.float32) for ref in refs[:-1]], axis=0)
    most = jnp.zeros((1, 1), jnp.float32)
    for o in range(sizes.owners):
        here = jnp.sum(jnp.where(owners == o, 1.0, 0.0), axis=0, keepdims=True)
        most = jnp.maximum(most, jnp.sum(here, axis=1, keepdims=True))
    level = jnp.zeros((1, 1), jnp.int32)
    for n in LEVELS[:-1]:
        level = level + jnp.where(most > sizes.second * n // 16, 1, 0)
    refs[-1][...] = jnp.broadcast_to(level, refs[-1].shape)


def regroup_kernel(sizes, *refs):
    spills = refs[: sizes.columns]
    send_ref, feet, notes, place = refs[sizes.columns :]
    owner = pl.program_id(0)
    spill = sizes.spill
    end = sizes.lane_tiles * spill

    @pl.when(owner == 0)
    def _():
        for d, ref in enumerate(spills):
            for n in range(sizes.lane_tiles):
                feet[d * spill : (d + 1) * spill, n * LANES : (n + 1) * LANES] = ref[
                    n * spill : (n + 1) * spill, :
                ]
            notes[:, d * spill : (d + 1) * spill] = ref[end : end + 16, :].astype(jnp.float32)

    mine = notes[8:9, :] == owner.astype(jnp.float32)
    total = jnp.zeros((1, 1), jnp.float32)
    keys = []
    for d in range(sizes.columns):
        here = mine[:, d * spill : (d + 1) * spill]
        position = total + notes[9:10, d * spill : (d + 1) * spill]
        inner = lax.rem(iota((1, spill), 1), jnp.int32(sizes.per_slot))
        keys.append(
            jnp.where(here, position.astype(jnp.int32) * sizes.per_slot + inner, -1)
        )
        total = total + jnp.sum(
            jnp.where(here, 1.0 / sizes.per_slot, 0.0), axis=1, keepdims=True
        )
    key = jnp.concatenate(keys, axis=1)
    place[...] = (iota(place.shape, 0) == key).astype(jnp.bfloat16)
    send_ref[0, sizes.notes :, :] = jnp.dot(
        place[...], feet[...], preferred_element_type=jnp.float32
    ).astype(jnp.bfloat16)
    moved = lax.dot_general(
        notes[0:8, :].astype(jnp.bfloat16),
        place[...],
        (((1,), (1,)), ((), ())),
        preferred_element_type=jnp.float32,
    )
    field, lane = iota(moved.shape, 0), iota(moved.shape, 1)
    empty = jnp.where(field == 0, jnp.float32(sizes.half), jnp.where(field == 5, 1.0, 0.0))
    moved = jnp.where(lane.astype(jnp.float32) < total * sizes.per_slot, moved, empty)
    moved = moved.astype(jnp.bfloat16)
    for n in range(sizes.notes // 8):
        send_ref[0, n * 8 : (n + 1) * 8, :] = moved[:, n * sizes.part : (n + 1) * sizes.part]


def forward_first_kernel(sizes, at_ref, flux_ref, got_ref, out_ref):
    step = pl.program_id(0)
    feet, notes, plane = first_round(sizes, got_ref, step)
    sums = partial_sums(sizes, flux_ref, feet, notes, plane)

    @pl.when(step == 0)
    def _():
        out_ref[...] = sums

    @pl.when(step > 0)
    def _():
        out_ref[...] += sums


def forward_second_kernel(sizes, at_ref, flux_ref, got_ref, before_ref, out_ref):
    feet, notes, plane = second_round(sizes, got_ref)
    sums = before_ref[...] + partial_sums(sizes, flux_ref, feet, notes, plane)
    out_ref[...] = jnp.broadcast_to(sums[None], out_ref.shape)


def adjoint_kernel(
    sizes, chunks, at_ref, sums_ref, one_ref, two_ref, modeled_ref, grad_ref, model
):
    step = pl.program_id(0)

    @pl.when(step == 0)
    def _():
        sums = jnp.sum(sums_ref[...], axis=0)
        model[...] = jnp.concatenate(thirds(sums), axis=0).astype(jnp.bfloat16)
        me = at_ref[0]
        page, within = lax.div(me, sizes.per_page), lax.rem(me, sizes.per_page)
        lane = iota((8, LANES), 1)
        own = jnp.zeros((8, LANES), jnp.float32)
        for p in range(sizes.pages):
            own = jnp.where(page == p, sums[p * 8 : (p + 1) * 8], own)
        result = jnp.zeros(modeled_ref.shape, jnp.float32)
        at_block = iota(modeled_ref.shape, 1)
        each = 8 // sizes.soundings
        for q in range(sizes.states // 8):
            picked = jnp.where(lane == q * sizes.per_page + within, own, 0.0)
            column = jnp.sum(picked, axis=1, keepdims=True)
            for n in range(each):
                values = column[n * sizes.soundings : (n + 1) * sizes.soundings]
                result = jnp.where(at_block == q * each + n, values, result)
        modeled_ref[...] = result

    @pl.when(step < chunks)
    def _():
        feet, notes, plane = first_round(sizes, one_ref, step)
        terms = gradient_terms(sizes, model[...], feet, notes, plane).reshape(grad_ref.shape)

        @pl.when(step == 0)
        def _():
            grad_ref[...] = terms

        @pl.when(step > 0)
        def _():
            grad_ref[...] += terms

    @pl.when(step == chunks)
    def _():
        feet, notes, plane = second_round(sizes, two_ref)
        terms = gradient_terms(sizes, model[...], feet, notes, plane)
        grad_ref[...] += terms.reshape(grad_ref.shape)


def shards(footprint, obs_hour, tile_list, tile_row, flux, observed, obs_var):
    sizes = Sizes(
        lax.axis_size("flux"), lax.axis_size("obs"), footprint.shape, flux.shape
    )
    owners, columns, devices, part = sizes.owners, sizes.columns, sizes.devices, sizes.part
    both = ("flux", "obs")
    params = pltpu.CompilerParams(vmem_limit_bytes=VMEM_BYTES)
    smem = pl.BlockSpec(memory_space=pltpu.SMEM)
    me = lax.axis_index("flux") * columns + lax.axis_index("obs")
    at = jnp.stack([me, lax.axis_index("obs")])
    flux = flux.transpose(1, 0, 2)

    first_height = sizes.lane_tiles * sizes.rows + 8
    spill_height = sizes.lane_tiles * sizes.spill + 16
    all_slots = sizes.slots * sizes.per_slot
    send, *spills = pl.pallas_call(
        functools.partial(pack_kernel, sizes),
        grid_spec=pltpu.PrefetchScalarGridSpec(
            num_scalar_prefetch=1,
            grid=(columns,),
            in_specs=[smem] * 5
            + [pl.BlockSpec((all_slots, part), lambda d, at: (0, d ^ at[1]))],
            out_specs=[
                pl.BlockSpec((owners, 1, first_height, LANES), lambda d, at: (0, d ^ at[1], 0, 0))
            ]
            + [pl.BlockSpec((spill_height, LANES), lambda d, at: (0, 0))] * columns,
            scratch_shapes=[
                pltpu.VMEM((owners * sizes.rows + sizes.spill, all_slots), jnp.bfloat16),
                pltpu.VMEM((owners, 8, LANES), jnp.float32),
                pltpu.VMEM((16, LANES), jnp.float32),
                pltpu.SMEM((owners + 1,), jnp.int32),
            ],
        ),
        out_shape=[pltpu.HBM((owners, columns, first_height, LANES), jnp.bfloat16)]
        + [jax.ShapeDtypeStruct((spill_height, LANES), jnp.bfloat16)] * columns,
        compiler_params=params,
        name="pack",
    )(
        at,
        tile_list.T,
        tile_row,
        obs_hour.T,
        observed.T,
        obs_var.T,
        footprint.reshape(all_slots, sizes.lane_tiles * columns * LANES),
    )
    got = lax.all_to_all(
        send.reshape(devices, first_height, LANES), both, split_axis=0, concat_axis=0, tiled=True
    )
    spills = spills[:1] + [
        lax.ppermute(spills[d], "obs", [(i, i ^ d) for i in range(columns)])
        for d in range(1, columns)
    ]
    second_height = sizes.notes + sizes.second
    notes_at = spill_height // 16 - 1
    level = pl.pallas_call(
        functools.partial(level_kernel, sizes),
        grid=(1,),
        in_specs=[pl.BlockSpec((16, LANES), lambda i: (notes_at, 0))] * columns,
        out_specs=pl.BlockSpec((8, LANES), lambda i: (0, 0)),
        out_shape=jax.ShapeDtypeStruct((8, LANES), jnp.int32),
        compiler_params=params,
        name="level",
    )(*spills)
    apart = 1
    while apart < owners:
        others = [
            lax.ppermute(level, "flux", [(i, i ^ n) for i in range(owners)])
            for n in range(apart, min(4 * apart, owners), apart)
        ]
        for other in others:
            level = jnp.maximum(level, other)
        apart *= 4
    send_second = pl.pallas_call(
        functools.partial(regroup_kernel, sizes),
        grid=(owners,),
        in_specs=[pl.BlockSpec((spill_height, LANES), lambda o: (0, 0))] * columns,
        out_specs=pl.BlockSpec((1, second_height, part), lambda o: (o, 0, 0)),
        out_shape=jax.ShapeDtypeStruct((owners, second_height, part), jnp.bfloat16),
        scratch_shapes=[
            pltpu.VMEM((columns * sizes.spill, part), jnp.bfloat16),
            pltpu.VMEM((16, columns * sizes.spill), jnp.float32),
            pltpu.VMEM((sizes.second, columns * sizes.spill), jnp.bfloat16),
        ],
        compiler_params=params,
        name="regroup",
    )(*spills)
    sources = min(devices, 1024 // sizes.rows)
    chunks = devices // sources
    copies = devices if devices <= 64 else 1
    height = 8 * sizes.pages
    flux_spec = pl.BlockSpec((sizes.hours, sizes.tiles, part), lambda i, at: (0, 0, at[1]))

    def finish(sixteenths):
        count = sizes.notes + sizes.second * sixteenths // 16

        def run(flux, got, send_second, at):
            got_second = lax.all_to_all(
                send_second[:, :count], "flux", split_axis=0, concat_axis=0, tiled=True
            )
            early = pl.pallas_call(
                functools.partial(forward_first_kernel, sizes),
                grid_spec=pltpu.PrefetchScalarGridSpec(
                    num_scalar_prefetch=1,
                    grid=(chunks,),
                    in_specs=[
                        flux_spec,
                        pl.BlockSpec((sources, first_height, LANES), lambda i, at: (i, 0, 0)),
                    ],
                    out_specs=pl.BlockSpec((height, LANES), lambda i, at: (0, 0)),
                ),
                out_shape=jax.ShapeDtypeStruct((height, LANES), jnp.float32),
                compiler_params=params,
                name="forward_first",
            )(at, flux, got)
            sums = pl.pallas_call(
                functools.partial(forward_second_kernel, sizes),
                grid_spec=pltpu.PrefetchScalarGridSpec(
                    num_scalar_prefetch=1,
                    grid=(1,),
                    in_specs=[
                        flux_spec,
                        pl.BlockSpec((owners, count, part), lambda i, at: (0, 0, 0)),
                        pl.BlockSpec((height, LANES), lambda i, at: (0, 0)),
                    ],
                    out_specs=pl.BlockSpec((copies, height, LANES), lambda i, at: (0, 0, 0)),
                ),
                out_shape=jax.ShapeDtypeStruct((copies, height, LANES), jnp.float32),
                compiler_params=params,
                name="forward_second",
            )(at, flux, got_second, early)
            if copies > 1:
                sums = lax.all_to_all(sums, both, split_axis=0, concat_axis=0, tiled=True)
            else:
                sums = lax.psum(sums, both)
            return pl.pallas_call(
                functools.partial(adjoint_kernel, sizes, chunks),
                grid_spec=pltpu.PrefetchScalarGridSpec(
                    num_scalar_prefetch=1,
                    grid=(chunks + 1,),
                    in_specs=[
                        pl.BlockSpec((copies, height, LANES), lambda i, at: (0, 0, 0)),
                        pl.BlockSpec(
                            (sources, first_height, LANES),
                            lambda i, at: (jnp.minimum(i, chunks - 1), 0, 0),
                        ),
                        pl.BlockSpec((owners, count, part), lambda i, at: (0, 0, 0)),
                    ],
                    out_specs=(
                        pl.BlockSpec((sizes.soundings, sizes.blocks), lambda i, at: (0, 0)),
                        pl.BlockSpec((sizes.hours, sizes.tiles, part), lambda i, at: (0, 0, 0)),
                    ),
                    scratch_shapes=[pltpu.VMEM((3 * height, LANES), jnp.bfloat16)],
                ),
                out_shape=(
                    jax.ShapeDtypeStruct((sizes.soundings, sizes.blocks), jnp.float32),
                    jax.ShapeDtypeStruct((sizes.hours, sizes.tiles, part), jnp.float32),
                ),
                compiler_params=params,
                name="adjoint",
            )(at, sums, got, got_second)

        return run

    modeled, gradient = lax.switch(
        level[0, 0], [finish(n) for n in LEVELS], flux, got, send_second, at
    )
    return modeled.T, gradient.transpose(1, 0, 2)


def solution(mesh):
    placed = (
        P(("flux", "obs"), None, None, None, None),
        P(("flux", "obs"), None),
        P(("flux", "obs"), None),
        P(),
        P("flux", None, None),
        P(("flux", "obs"), None),
        P(("flux", "obs"), None),
    )
    return jax.shard_map(
        shards,
        mesh=mesh,
        in_specs=placed,
        out_specs=(P(("flux", "obs"), None), P("flux", None, "obs")),
        check_vma=False,
    )
```

```python
import functools

import jax
import jax.numpy as jnp
from jax import lax
from jax.experimental import pallas as pl
from jax.experimental.pallas import tpu as pltpu
from jax.sharding import PartitionSpec as P

LANES = 128
VMEM_BYTES = 48 * 1024 * 1024
BASE = 8
REST = (0, 2, 8)


def iota(shape, dim):
    return lax.broadcasted_iota(jnp.int32, shape, dim)


def thirds(value):
    high = value.astype(jnp.bfloat16).astype(jnp.float32)
    rest = value - high
    middle = rest.astype(jnp.bfloat16).astype(jnp.float32)
    return high, middle, (rest - middle).astype(jnp.bfloat16).astype(jnp.float32)


class Sizes:
    def __init__(self, owners, columns, footprint, flux):
        self.owners, self.columns = owners, columns
        self.devices = owners * columns
        self.blocks, self.width, self.soundings, self.lags, cells = footprint
        self.tiles, self.hours = flux[0], flux[1]
        self.span = self.hours - self.lags + 1
        self.half = self.span * self.tiles // 2
        self.slots = self.blocks * self.width
        self.per_slot = self.soundings * self.lags
        self.part = cells // columns
        self.lane_tiles = self.part // LANES
        self.first = self.slots // owners
        self.rows = self.first * self.per_slot
        self.spill = self.slots // 2 * self.per_slot
        self.second = columns * self.first * self.per_slot
        self.base = self.second * BASE // 16
        self.notes = 8 * (self.second // self.part)
        self.states = self.blocks * self.soundings
        self.per_page = 8 * LANES // self.states
        self.pages = self.devices // self.per_page


def read_notes(sizes, notes, plane):
    lane = iota((1, notes.shape[1]), 1)
    inner = lax.rem(lane, jnp.int32(sizes.per_slot))
    base = notes[0:1]
    target = (base + sizes.half).astype(jnp.int32) + lax.rem(inner, jnp.int32(sizes.lags)) * sizes.tiles
    target = jnp.where(base > sizes.half - 0.5, -1, target)
    place = notes[1:2].astype(jnp.int32)
    block = lax.rem(place, jnp.int32(sizes.blocks))
    device = plane * sizes.columns + lax.div(place, jnp.int32(sizes.blocks))
    state = block * sizes.soundings + lax.div(inner, jnp.int32(sizes.lags))
    row = lax.div(device, jnp.int32(sizes.per_page)) * 8 + lax.rem(state, jnp.int32(8))
    column = lax.div(state, jnp.int32(8)) * sizes.per_page + lax.rem(device, jnp.int32(sizes.per_page))
    return target, row, column


def first_round(sizes, ref, step):
    sources, count = ref.shape[0], sizes.rows
    feet = jnp.concatenate(
        [
            ref[:, n * count : (n + 1) * count, :].reshape(sources * count, LANES)
            for n in range(sizes.lane_tiles)
        ],
        axis=1,
    )
    end = sizes.lane_tiles * count
    notes = jnp.concatenate(
        [ref[s, end : end + 8, :].astype(jnp.float32)[:, :count] for s in range(sources)], axis=1
    )
    lane = iota((1, sources * count), 1)
    plane = lax.div(step * sources + lax.div(lane, jnp.int32(count)), jnp.int32(sizes.columns))
    return feet, notes, plane


def second_round(sizes, flux_index, bases, rests, with_bases=True):
    notes = [
        jnp.concatenate(
            [ref[n * 8 : (n + 1) * 8, :].astype(jnp.float32) for n in range(sizes.notes // 8)],
            axis=1,
        )
        for ref in bases
    ]
    feet, kept, planes = [], [], []
    if with_bases:
        feet += [ref[sizes.notes :, :] for ref in bases]
        kept += [each[:, : sizes.base] for each in notes]
        planes.append(lax.div(iota((1, len(bases) * sizes.base), 1), jnp.int32(sizes.base)))
    if rests:
        more = rests[0].shape[0]
        feet += [ref[...] for ref in rests]
        kept += [each[:, sizes.base : sizes.base + more] for each in notes]
        planes.append(lax.div(iota((1, len(rests) * more), 1), jnp.int32(more)))
    plane = lax.bitwise_xor(jnp.concatenate(planes, axis=1), flux_index)
    return jnp.concatenate(feet, axis=0), jnp.concatenate(kept, axis=1), plane


def partial_sums(sizes, flux_ref, feet, notes, plane):
    target, row, column = read_notes(sizes, notes, plane)
    count = feet.shape[0]
    levels = sizes.hours * sizes.tiles
    products = lax.dot_general(
        flux_ref[...].reshape(levels, sizes.part),
        feet,
        (((1,), (1,)), ((), ())),
        preferred_element_type=jnp.float32,
    )
    chosen = jnp.where(iota((levels, count), 0) == target, products, 0.0)
    partial = jnp.sum(chosen, axis=0, keepdims=True)
    height = 8 * sizes.pages
    spread = jnp.where(iota((height, count), 0) == row, partial, 0.0)
    terms = jnp.concatenate(thirds(spread), axis=0).astype(jnp.bfloat16)
    lanes = (iota((LANES, count), 0) == column).astype(jnp.bfloat16)
    sums = lax.dot_general(
        terms, lanes, (((1,), (1,)), ((), ())), preferred_element_type=jnp.float32
    )
    return sums[:height] + sums[height : 2 * height] + sums[2 * height :]


def gradient_terms(sizes, model, feet, notes, plane):
    target, row, column = read_notes(sizes, notes, plane)
    count = feet.shape[0]
    height = 8 * sizes.pages
    lanes = (iota((LANES, count), 0) == column).astype(jnp.bfloat16)
    taken = jnp.dot(model, lanes, preferred_element_type=jnp.float32)
    taken = taken[:height] + taken[height : 2 * height] + taken[2 * height :]
    value = jnp.sum(
        jnp.where(iota((height, count), 0) == row, taken, 0.0), axis=0, keepdims=True
    )
    seen = notes[2:3] + notes[3:4] + notes[4:5]
    spread = notes[5:6] + notes[6:7] + notes[7:8]
    scaled = ((value - seen) / spread).astype(jnp.bfloat16).astype(jnp.float32)
    levels = sizes.hours * sizes.tiles
    coefficient = jnp.where(iota((levels, count), 0) == target, scaled, 0.0).astype(jnp.bfloat16)
    return jnp.dot(coefficient, feet, preferred_element_type=jnp.float32)


def pack_kernel(
    sizes, at_ref, list_ref, row_ref, hour_ref, seen_ref, var_ref, feet_ref, send_ref, *rest
):
    spills = rest[: sizes.columns]
    place, first_notes, spill_notes, count = rest[sizes.columns :]
    owners, per_slot = sizes.owners, sizes.per_slot
    step = pl.program_id(0)

    @pl.when(step == 0)
    def _():
        field, lane = iota((16, LANES), 0), iota((16, LANES), 1)
        inner = lane % per_slot
        sounding = inner // sizes.lags
        slot_at = lane // per_slot
        key_at = iota((1, sizes.slots * per_slot), 1)
        key = jnp.zeros(key_at.shape, jnp.int32)
        empty = jnp.where(field == 0, jnp.float32(sizes.half), 0.0)
        empty = jnp.where(field == 5, 1.0, jnp.where(field == 8, -1.0, empty))
        for o in range(owners):
            count[o] = 0
            first_notes[o] = empty[:8]
        count[owners] = 0
        left = empty
        for b in range(sizes.blocks):
            base = jnp.zeros(field.shape, jnp.float32)
            seen = jnp.zeros(field.shape, jnp.float32)
            spread = jnp.ones(field.shape, jnp.float32)
            for o in range(sizes.soundings):
                here = sounding == o
                hour = hour_ref[o, b] * sizes.tiles - sizes.half
                base = jnp.where(here, hour.astype(jnp.float32), base)
                seen = jnp.where(here, seen_ref[o, b], seen)
                spread = jnp.where(here, var_ref[o, b], spread)
            column = (b + sizes.blocks * at_ref[1]).astype(jnp.float32)
            pattern = jnp.where(field == 0, base, jnp.where(field == 1, column, 0.0))
            for n, term in enumerate(thirds(seen) + thirds(spread)):
                pattern = jnp.where(field == 2 + n, term, pattern)
            for k in range(sizes.width):
                stored = row_ref[list_ref[k, b]]
                owner = lax.div(stored, jnp.int32(sizes.tiles))
                tile = (stored - owner * sizes.tiles).astype(jnp.float32)
                position = count[owner]
                count[owner] = position + 1
                keep = position < sizes.first
                over = count[owners]
                count[owners] = over + jnp.where(keep, 0, 1)
                goes = jnp.where(
                    keep, owner * sizes.first + position, owners * sizes.first + over
                )
                value = jnp.where(field == 0, pattern + tile, pattern)
                value = jnp.where(field == 8, owner.astype(jnp.float32), value)
                value = jnp.where(
                    field == 9, (position - sizes.first).astype(jnp.float32), value
                )
                first_notes[owner] = jnp.where(
                    slot_at[:8] == jnp.where(keep, position, -1), value[:8], first_notes[owner]
                )
                left = jnp.where(slot_at == jnp.where(keep, -1, over), value, left)
                key = jnp.where(
                    key_at // per_slot == b * sizes.width + k,
                    goes * per_slot + key_at % per_slot,
                    key,
                )
        spill_notes[...] = left
        place[...] = (iota(place.shape, 0) == key).astype(jnp.bfloat16)

    packed = jnp.dot(place[...], feet_ref[...], preferred_element_type=jnp.float32)
    packed = packed.astype(jnp.bfloat16)
    rows = sizes.rows
    end = sizes.lane_tiles * rows
    for o in range(owners):
        for n in range(sizes.lane_tiles):
            send_ref[o, 0, n * rows : (n + 1) * rows, :] = packed[
                o * rows : (o + 1) * rows, n * LANES : (n + 1) * LANES
            ]
        send_ref[o, 0, end : end + 8, :] = first_notes[o].astype(jnp.bfloat16)
    for d in range(sizes.columns):

        @pl.when(step == d)
        def _():
            for n in range(sizes.lane_tiles):
                spills[d][n * sizes.spill : (n + 1) * sizes.spill, :] = packed[
                    owners * rows :, n * LANES : (n + 1) * LANES
                ]
            end = sizes.lane_tiles * sizes.spill
            spills[d][end : end + 16, :] = spill_notes[...].astype(jnp.bfloat16)


def level_kernel(sizes, *refs):
    owners = jnp.concatenate([ref[8:9, :].astype(jnp.float32) for ref in refs[:-1]], axis=0)
    most = jnp.zeros((1, 1), jnp.float32)
    for o in range(sizes.owners):
        here = jnp.sum(jnp.where(owners == o, 1.0, 0.0), axis=0, keepdims=True)
        most = jnp.maximum(most, jnp.sum(here, axis=1, keepdims=True))
    level = jnp.zeros((1, 1), jnp.int32)
    for n in REST[:-1]:
        level = level + jnp.where(most > sizes.base + sizes.second * n // 16, 1, 0)
    refs[-1][...] = jnp.broadcast_to(level, refs[-1].shape)


def regroup_kernel(sizes, at_ref, *refs):
    columns, owners, spill = sizes.columns, sizes.owners, sizes.spill
    spills, bases = refs[:columns], refs[columns : columns + owners]
    rests = refs[columns + owners : columns + 2 * owners]
    feet, notes, place = refs[columns + 2 * owners :]
    step = pl.program_id(0)
    owner = at_ref[2] ^ step
    end = sizes.lane_tiles * spill

    @pl.when(step == 0)
    def _():
        for d, ref in enumerate(spills):
            for n in range(sizes.lane_tiles):
                feet[d * spill : (d + 1) * spill, n * LANES : (n + 1) * LANES] = ref[
                    n * spill : (n + 1) * spill, :
                ]
            notes[:, d * spill : (d + 1) * spill] = ref[end : end + 16, :].astype(jnp.float32)

    mine = notes[8:9, :] == owner.astype(jnp.float32)
    total = jnp.zeros((1, 1), jnp.float32)
    keys = []
    for d in range(columns):
        here = mine[:, d * spill : (d + 1) * spill]
        position = total + notes[9:10, d * spill : (d + 1) * spill]
        inner = lax.rem(iota((1, spill), 1), jnp.int32(sizes.per_slot))
        keys.append(
            jnp.where(here, position.astype(jnp.int32) * sizes.per_slot + inner, -1)
        )
        total = total + jnp.sum(
            jnp.where(here, 1.0 / sizes.per_slot, 0.0), axis=1, keepdims=True
        )
    key = jnp.concatenate(keys, axis=1)
    place[...] = (iota(place.shape, 0) == key).astype(jnp.bfloat16)
    sorted_feet = jnp.dot(place[...], feet[...], preferred_element_type=jnp.float32)
    sorted_feet = sorted_feet.astype(jnp.bfloat16)
    moved = lax.dot_general(
        notes[0:8, :].astype(jnp.bfloat16),
        place[...],
        (((1,), (1,)), ((), ())),
        preferred_element_type=jnp.float32,
    )
    field, lane = iota(moved.shape, 0), iota(moved.shape, 1)
    empty = jnp.where(field == 0, jnp.float32(sizes.half), jnp.where(field == 5, 1.0, 0.0))
    moved = jnp.where(lane.astype(jnp.float32) < total * sizes.per_slot, moved, empty)
    moved = moved.astype(jnp.bfloat16)
    for o in range(owners):

        @pl.when(step == o)
        def _():
            for n in range(sizes.notes // 8):
                bases[o][n * 8 : (n + 1) * 8, :] = moved[
                    :, n * sizes.part : (n + 1) * sizes.part
                ]
            bases[o][sizes.notes :, :] = sorted_feet[: sizes.base]
            rests[o][...] = sorted_feet[sizes.base :]


def forward_first_kernel(sizes, at_ref, flux_ref, got_ref, out_ref):
    step = pl.program_id(0)
    feet, notes, plane = first_round(sizes, got_ref, step)
    sums = partial_sums(sizes, flux_ref, feet, notes, plane)

    @pl.when(step == 0)
    def _():
        out_ref[...] = sums

    @pl.when(step > 0)
    def _():
        out_ref[...] += sums


def forward_second_kernel(sizes, more, at_ref, flux_ref, before_ref, *refs):
    bases, rests, out_ref = refs[: sizes.owners], refs[sizes.owners : -1], refs[-1]
    feet, notes, plane = second_round(sizes, at_ref[2], bases, rests, not more)
    sums = before_ref[0] + partial_sums(sizes, flux_ref, feet, notes, plane)
    out_ref[...] = jnp.broadcast_to(sums[None], out_ref.shape)


def adjoint_kernel(sizes, chunks, at_ref, sums_ref, one_ref, *refs):
    bases, rests = refs[: sizes.owners], refs[sizes.owners : -3]
    modeled_ref, grad_ref, model = refs[-3:]
    step = pl.program_id(0)

    @pl.when(step == 0)
    def _():
        sums = jnp.sum(sums_ref[...], axis=0)
        model[...] = jnp.concatenate(thirds(sums), axis=0).astype(jnp.bfloat16)
        me = at_ref[0]
        page, within = lax.div(me, sizes.per_page), lax.rem(me, sizes.per_page)
        lane = iota((8, LANES), 1)
        own = jnp.zeros((8, LANES), jnp.float32)
        for p in range(sizes.pages):
            own = jnp.where(page == p, sums[p * 8 : (p + 1) * 8], own)
        result = jnp.zeros(modeled_ref.shape, jnp.float32)
        at_block = iota(modeled_ref.shape, 1)
        each = 8 // sizes.soundings
        for q in range(sizes.states // 8):
            picked = jnp.where(lane == q * sizes.per_page + within, own, 0.0)
            column = jnp.sum(picked, axis=1, keepdims=True)
            for n in range(each):
                values = column[n * sizes.soundings : (n + 1) * sizes.soundings]
                result = jnp.where(at_block == q * each + n, values, result)
        modeled_ref[...] = result

    @pl.when(step < chunks)
    def _():
        feet, notes, plane = first_round(sizes, one_ref, step)
        terms = gradient_terms(sizes, model[...], feet, notes, plane).reshape(grad_ref.shape)

        @pl.when(step == 0)
        def _():
            grad_ref[...] = terms

        @pl.when(step > 0)
        def _():
            grad_ref[...] += terms

    @pl.when(step == chunks)
    def _():
        feet, notes, plane = second_round(sizes, at_ref[2], bases, rests)
        terms = gradient_terms(sizes, model[...], feet, notes, plane)
        grad_ref[...] += terms.reshape(grad_ref.shape)


def shards(footprint, obs_hour, tile_list, tile_row, flux, observed, obs_var):
    sizes = Sizes(
        lax.axis_size("flux"), lax.axis_size("obs"), footprint.shape, flux.shape
    )
    owners, columns, devices, part = sizes.owners, sizes.columns, sizes.devices, sizes.part
    both = ("flux", "obs")
    params = pltpu.CompilerParams(vmem_limit_bytes=VMEM_BYTES)
    smem = pl.BlockSpec(memory_space=pltpu.SMEM)
    me = lax.axis_index("flux") * columns + lax.axis_index("obs")
    at = jnp.stack([me, lax.axis_index("obs"), lax.axis_index("flux")])
    flux = flux.transpose(1, 0, 2)

    first_height = sizes.lane_tiles * sizes.rows + 8
    spill_height = sizes.lane_tiles * sizes.spill + 16
    all_slots = sizes.slots * sizes.per_slot
    send, *spills = pl.pallas_call(
        functools.partial(pack_kernel, sizes),
        grid_spec=pltpu.PrefetchScalarGridSpec(
            num_scalar_prefetch=1,
            grid=(columns,),
            in_specs=[smem] * 5
            + [pl.BlockSpec((all_slots, part), lambda d, at: (0, d ^ at[1]))],
            out_specs=[
                pl.BlockSpec((owners, 1, first_height, LANES), lambda d, at: (0, d ^ at[1], 0, 0))
            ]
            + [pl.BlockSpec((spill_height, LANES), lambda d, at: (0, 0))] * columns,
            scratch_shapes=[
                pltpu.VMEM((owners * sizes.rows + sizes.spill, all_slots), jnp.bfloat16),
                pltpu.VMEM((owners, 8, LANES), jnp.float32),
                pltpu.VMEM((16, LANES), jnp.float32),
                pltpu.SMEM((owners + 1,), jnp.int32),
            ],
        ),
        out_shape=[pltpu.HBM((owners, columns, first_height, LANES), jnp.bfloat16)]
        + [jax.ShapeDtypeStruct((spill_height, LANES), jnp.bfloat16)] * columns,
        compiler_params=params,
        name="pack",
    )(
        at,
        tile_list.T,
        tile_row,
        obs_hour.T,
        observed.T,
        obs_var.T,
        footprint.reshape(all_slots, sizes.lane_tiles * columns * LANES),
    )
    got = lax.all_to_all(
        send.reshape(devices, first_height, LANES), both, split_axis=0, concat_axis=0, tiled=True
    )
    spills = spills[:1] + [
        lax.ppermute(spills[d], "obs", [(i, i ^ d) for i in range(columns)])
        for d in range(1, columns)
    ]
    second_height = sizes.notes + sizes.second
    notes_at = spill_height // 16 - 1
    level = pl.pallas_call(
        functools.partial(level_kernel, sizes),
        grid=(1,),
        in_specs=[pl.BlockSpec((16, LANES), lambda i: (notes_at, 0))] * columns,
        out_specs=pl.BlockSpec((8, LANES), lambda i: (0, 0)),
        out_shape=jax.ShapeDtypeStruct((8, LANES), jnp.int32),
        compiler_params=params,
        name="level",
    )(*spills)
    apart = 1
    while apart < owners:
        others = [
            lax.ppermute(level, "flux", [(i, i ^ n) for i in range(owners)])
            for n in range(apart, min(4 * apart, owners), apart)
        ]
        for other in others:
            level = jnp.maximum(level, other)
        apart *= 4
    base_height, more_height = sizes.notes + sizes.base, sizes.second - sizes.base
    outs = [(base_height, part)] * owners + [(more_height, part)] * owners
    parts = pl.pallas_call(
        functools.partial(regroup_kernel, sizes),
        grid_spec=pltpu.PrefetchScalarGridSpec(
            num_scalar_prefetch=1,
            grid=(owners,),
            in_specs=[pl.BlockSpec((spill_height, LANES), lambda o, at: (0, 0))] * columns,
            out_specs=[pl.BlockSpec(shape, lambda o, at: (0, 0)) for shape in outs],
            scratch_shapes=[
                pltpu.VMEM((columns * sizes.spill, part), jnp.bfloat16),
                pltpu.VMEM((16, columns * sizes.spill), jnp.float32),
                pltpu.VMEM((sizes.second, columns * sizes.spill), jnp.bfloat16),
            ],
        ),
        out_shape=[jax.ShapeDtypeStruct(shape, jnp.bfloat16) for shape in outs],
        compiler_params=params,
        name="regroup",
    )(at, *spills)

    def swap(arrays):
        return arrays[:1] + [
            lax.ppermute(arrays[n], "flux", [(i, i ^ n) for i in range(owners)])
            for n in range(1, owners)
        ]

    parts = list(parts)
    bases, rests = swap(parts[:owners]), parts[owners:]

    sources = min(devices, 1024 // sizes.rows)
    chunks = devices // sources
    copies = devices if devices <= 64 else 1
    height = 8 * sizes.pages
    flux_spec = pl.BlockSpec((sizes.hours, sizes.tiles, part), lambda i, at: (0, 0, at[1]))
    base_specs = [pl.BlockSpec((base_height, part), lambda i, at: (0, 0))] * owners
    early = pl.pallas_call(
        functools.partial(forward_first_kernel, sizes),
        grid_spec=pltpu.PrefetchScalarGridSpec(
            num_scalar_prefetch=1,
            grid=(chunks,),
            in_specs=[
                flux_spec,
                pl.BlockSpec((sources, first_height, LANES), lambda i, at: (i, 0, 0)),
            ],
            out_specs=pl.BlockSpec((height, LANES), lambda i, at: (0, 0)),
        ),
        out_shape=jax.ShapeDtypeStruct((height, LANES), jnp.float32),
        compiler_params=params,
        name="forward_first",
    )(at, flux, got)

    def forward_second(flux, before, bases, rests, more):
        return pl.pallas_call(
            functools.partial(forward_second_kernel, sizes, more > 0),
            grid_spec=pltpu.PrefetchScalarGridSpec(
                num_scalar_prefetch=1,
                grid=(1,),
                in_specs=[flux_spec, pl.BlockSpec((1, height, LANES), lambda i, at: (0, 0, 0))]
                + base_specs
                + [pl.BlockSpec((more, part), lambda i, at: (0, 0))] * len(rests),
                out_specs=pl.BlockSpec((copies, height, LANES), lambda i, at: (0, 0, 0)),
            ),
            out_shape=jax.ShapeDtypeStruct((copies, height, LANES), jnp.float32),
            compiler_params=params,
            name="forward_more" if more else "forward_second",
        )(at, flux, before, *bases, *rests)

    sums = forward_second(flux, early[None], bases, [], 0)

    def finish(sixteenths):
        more = sizes.second * sixteenths // 16

        def run(flux, got, sums, bases, rests, at):
            if more:
                rests = rests[:1] + swap([rest[:more] for rest in rests])[1:]
                sums = forward_second(flux, sums, bases, rests, more)
            else:
                rests = []
            if copies > 1:
                sums = lax.all_to_all(sums, both, split_axis=0, concat_axis=0, tiled=True)
            else:
                sums = lax.psum(sums, both)
            return pl.pallas_call(
                functools.partial(adjoint_kernel, sizes, chunks),
                grid_spec=pltpu.PrefetchScalarGridSpec(
                    num_scalar_prefetch=1,
                    grid=(chunks + 1,),
                    in_specs=[
                        pl.BlockSpec((copies, height, LANES), lambda i, at: (0, 0, 0)),
                        pl.BlockSpec(
                            (sources, first_height, LANES),
                            lambda i, at: (jnp.minimum(i, chunks - 1), 0, 0),
                        ),
                    ]
                    + base_specs
                    + [pl.BlockSpec((more, part), lambda i, at: (0, 0))] * len(rests),
                    out_specs=(
                        pl.BlockSpec((sizes.soundings, sizes.blocks), lambda i, at: (0, 0)),
                        pl.BlockSpec((sizes.hours, sizes.tiles, part), lambda i, at: (0, 0, 0)),
                    ),
                    scratch_shapes=[pltpu.VMEM((3 * height, LANES), jnp.bfloat16)],
                ),
                out_shape=(
                    jax.ShapeDtypeStruct((sizes.soundings, sizes.blocks), jnp.float32),
                    jax.ShapeDtypeStruct((sizes.hours, sizes.tiles, part), jnp.float32),
                ),
                compiler_params=params,
                name="adjoint",
            )(at, sums, got, *bases, *rests)

        return run

    modeled, gradient = lax.switch(
        level[0, 0], [finish(n) for n in REST], flux, got, sums, bases, rests, at
    )
    return modeled.T, gradient.transpose(1, 0, 2)


def solution(mesh):
    placed = (
        P(("flux", "obs"), None, None, None, None),
        P(("flux", "obs"), None),
        P(("flux", "obs"), None),
        P(),
        P("flux", None, None),
        P(("flux", "obs"), None),
        P(("flux", "obs"), None),
    )
    return jax.shard_map(
        shards,
        mesh=mesh,
        in_specs=placed,
        out_specs=(P(("flux", "obs"), None), P("flux", None, "obs")),
        check_vma=False,
    )
```

```python
import functools

import jax
import jax.numpy as jnp
from jax import lax
from jax.experimental import pallas as pl
from jax.experimental.pallas import tpu as pltpu
from jax.sharding import PartitionSpec as P

LANES = 128
VMEM_BYTES = 48 * 1024 * 1024
BASE = 8
REST = (0, 2, 8)


def iota(shape, dim):
    return lax.broadcasted_iota(jnp.int32, shape, dim)


def thirds(value):
    high = value.astype(jnp.bfloat16).astype(jnp.float32)
    rest = value - high
    middle = rest.astype(jnp.bfloat16).astype(jnp.float32)
    return high, middle, (rest - middle).astype(jnp.bfloat16).astype(jnp.float32)


class Sizes:
    def __init__(self, owners, columns, footprint, flux):
        self.owners, self.columns = owners, columns
        self.devices = owners * columns
        self.blocks, self.width, self.soundings, self.lags, cells = footprint
        self.tiles, self.hours = flux[0], flux[1]
        self.span = self.hours - self.lags + 1
        self.half = self.span * self.tiles // 2
        self.slots = self.blocks * self.width
        self.per_slot = self.soundings * self.lags
        self.part = cells // columns
        self.lane_tiles = self.part // LANES
        self.first = self.slots // owners
        self.rows = self.first * self.per_slot
        self.spill = self.slots // 2 * self.per_slot
        self.second = columns * self.first * self.per_slot
        self.base = self.second * BASE // 16
        self.notes = 8 * (self.second // self.part)
        self.states = self.blocks * self.soundings
        self.per_page = 8 * LANES // self.states
        self.pages = self.devices // self.per_page


def read_notes(sizes, notes, plane):
    lane = iota((1, notes.shape[1]), 1)
    inner = lax.rem(lane, jnp.int32(sizes.per_slot))
    base = notes[0:1]
    target = (base + sizes.half).astype(jnp.int32) + lax.rem(inner, jnp.int32(sizes.lags)) * sizes.tiles
    target = jnp.where(base > sizes.half - 0.5, -1, target)
    place = notes[1:2].astype(jnp.int32)
    block = lax.rem(place, jnp.int32(sizes.blocks))
    device = plane * sizes.columns + lax.div(place, jnp.int32(sizes.blocks))
    state = block * sizes.soundings + lax.div(inner, jnp.int32(sizes.lags))
    row = lax.div(device, jnp.int32(sizes.per_page)) * 8 + lax.rem(state, jnp.int32(8))
    column = lax.div(state, jnp.int32(8)) * sizes.per_page + lax.rem(device, jnp.int32(sizes.per_page))
    return target, row, column


def first_round(sizes, ref, step):
    sources, count = ref.shape[0], sizes.rows
    feet = jnp.concatenate(
        [
            ref[:, n * count : (n + 1) * count, :].reshape(sources * count, LANES)
            for n in range(sizes.lane_tiles)
        ],
        axis=1,
    )
    end = sizes.lane_tiles * count
    notes = jnp.concatenate(
        [ref[s, end : end + 8, :].astype(jnp.float32)[:, :count] for s in range(sources)], axis=1
    )
    lane = iota((1, sources * count), 1)
    plane = lax.div(step * sources + lax.div(lane, jnp.int32(count)), jnp.int32(sizes.columns))
    return feet, notes, plane


def second_round(sizes, flux_index, bases, rests, with_bases=True):
    notes = [
        jnp.concatenate(
            [ref[n * 8 : (n + 1) * 8, :].astype(jnp.float32) for n in range(sizes.notes // 8)],
            axis=1,
        )
        for ref in bases
    ]
    feet, kept, planes = [], [], []
    if with_bases:
        feet += [ref[sizes.notes :, :] for ref in bases]
        kept += [each[:, : sizes.base] for each in notes]
        planes.append(lax.div(iota((1, len(bases) * sizes.base), 1), jnp.int32(sizes.base)))
    if rests:
        more = rests[0].shape[0]
        feet += [ref[...] for ref in rests]
        kept += [each[:, sizes.base : sizes.base + more] for each in notes]
        planes.append(lax.div(iota((1, len(rests) * more), 1), jnp.int32(more)))
    plane = lax.bitwise_xor(jnp.concatenate(planes, axis=1), flux_index)
    return jnp.concatenate(feet, axis=0), jnp.concatenate(kept, axis=1), plane


def partial_sums(sizes, flux_ref, feet, notes, plane):
    target, row, column = read_notes(sizes, notes, plane)
    count = feet.shape[0]
    levels = sizes.hours * sizes.tiles
    products = lax.dot_general(
        flux_ref[...].reshape(levels, sizes.part),
        feet,
        (((1,), (1,)), ((), ())),
        preferred_element_type=jnp.float32,
    )
    chosen = jnp.where(iota((levels, count), 0) == target, products, 0.0)
    partial = jnp.sum(chosen, axis=0, keepdims=True)
    height = 8 * sizes.pages
    spread = jnp.where(iota((height, count), 0) == row, partial, 0.0)
    terms = jnp.concatenate(thirds(spread), axis=0).astype(jnp.bfloat16)
    lanes = (iota((LANES, count), 0) == column).astype(jnp.bfloat16)
    sums = lax.dot_general(
        terms, lanes, (((1,), (1,)), ((), ())), preferred_element_type=jnp.float32
    )
    return sums[:height] + sums[height : 2 * height] + sums[2 * height :]


def gradient_terms(sizes, model, feet, notes, plane):
    target, row, column = read_notes(sizes, notes, plane)
    count = feet.shape[0]
    height = 8 * sizes.pages
    lanes = (iota((LANES, count), 0) == column).astype(jnp.bfloat16)
    taken = jnp.dot(model, lanes, preferred_element_type=jnp.float32)
    taken = taken[:height] + taken[height : 2 * height] + taken[2 * height :]
    value = jnp.sum(
        jnp.where(iota((height, count), 0) == row, taken, 0.0), axis=0, keepdims=True
    )
    seen = notes[2:3] + notes[3:4] + notes[4:5]
    spread = notes[5:6] + notes[6:7] + notes[7:8]
    scaled = ((value - seen) / spread).astype(jnp.bfloat16).astype(jnp.float32)
    levels = sizes.hours * sizes.tiles
    coefficient = jnp.where(iota((levels, count), 0) == target, scaled, 0.0).astype(jnp.bfloat16)
    return jnp.dot(coefficient, feet, preferred_element_type=jnp.float32)


def pack_kernel(
    sizes, at_ref, list_ref, row_ref, hour_ref, seen_ref, var_ref, feet_ref, send_ref, *rest
):
    spills = rest[: sizes.columns]
    place, first_notes, spill_notes, count = rest[sizes.columns :]
    owners, per_slot = sizes.owners, sizes.per_slot
    step = pl.program_id(0)

    @pl.when(step == 0)
    def _():
        field, lane = iota((16, LANES), 0), iota((16, LANES), 1)
        inner = lane % per_slot
        sounding = inner // sizes.lags
        slot_at = lane // per_slot
        key_at = iota((1, sizes.slots * per_slot), 1)
        key = jnp.zeros(key_at.shape, jnp.int32)
        empty = jnp.where(field == 0, jnp.float32(sizes.half), 0.0)
        empty = jnp.where(field == 5, 1.0, jnp.where(field == 8, -1.0, empty))
        for o in range(owners):
            count[o] = 0
            first_notes[o] = empty[:8]
        count[owners] = 0
        left = empty
        for b in range(sizes.blocks):
            base = jnp.zeros(field.shape, jnp.float32)
            seen = jnp.zeros(field.shape, jnp.float32)
            spread = jnp.ones(field.shape, jnp.float32)
            for o in range(sizes.soundings):
                here = sounding == o
                hour = hour_ref[o, b] * sizes.tiles - sizes.half
                base = jnp.where(here, hour.astype(jnp.float32), base)
                seen = jnp.where(here, seen_ref[o, b], seen)
                spread = jnp.where(here, var_ref[o, b], spread)
            column = (b + sizes.blocks * at_ref[1]).astype(jnp.float32)
            pattern = jnp.where(field == 0, base, jnp.where(field == 1, column, 0.0))
            for n, term in enumerate(thirds(seen) + thirds(spread)):
                pattern = jnp.where(field == 2 + n, term, pattern)
            for k in range(sizes.width):
                stored = row_ref[list_ref[k, b]]
                owner = lax.div(stored, jnp.int32(sizes.tiles))
                tile = (stored - owner * sizes.tiles).astype(jnp.float32)
                position = count[owner]
                count[owner] = position + 1
                keep = position < sizes.first
                over = count[owners]
                count[owners] = over + jnp.where(keep, 0, 1)
                goes = jnp.where(
                    keep, owner * sizes.first + position, owners * sizes.first + over
                )
                value = jnp.where(field == 0, pattern + tile, pattern)
                value = jnp.where(field == 8, owner.astype(jnp.float32), value)
                value = jnp.where(
                    field == 9, (position - sizes.first).astype(jnp.float32), value
                )
                first_notes[owner] = jnp.where(
                    slot_at[:8] == jnp.where(keep, position, -1), value[:8], first_notes[owner]
                )
                left = jnp.where(slot_at == jnp.where(keep, -1, over), value, left)
                key = jnp.where(
                    key_at // per_slot == b * sizes.width + k,
                    goes * per_slot + key_at % per_slot,
                    key,
                )
        counts = jnp.zeros((8, LANES), jnp.float32)
        for o in range(owners):
            over = jnp.maximum(count[o] - sizes.first, 0).astype(jnp.float32)
            counts = jnp.where(lane[:8] == sizes.rows + o, over, counts)
        for o in range(owners):
            first_notes[o] = jnp.where(lane[:8] < sizes.rows, first_notes[o], counts)
        spill_notes[...] = left
        place[...] = (iota(place.shape, 0) == key).astype(jnp.bfloat16)

    packed = jnp.dot(place[...], feet_ref[...], preferred_element_type=jnp.float32)
    packed = packed.astype(jnp.bfloat16)
    rows = sizes.rows
    end = sizes.lane_tiles * rows
    for o in range(owners):
        for n in range(sizes.lane_tiles):
            send_ref[o, 0, n * rows : (n + 1) * rows, :] = packed[
                o * rows : (o + 1) * rows, n * LANES : (n + 1) * LANES
            ]
        send_ref[o, 0, end : end + 8, :] = first_notes[o].astype(jnp.bfloat16)
    for d in range(sizes.columns):

        @pl.when(step == d)
        def _():
            for n in range(sizes.lane_tiles):
                spills[d][n * sizes.spill : (n + 1) * sizes.spill, :] = packed[
                    owners * rows :, n * LANES : (n + 1) * LANES
                ]
            end = sizes.lane_tiles * sizes.spill
            spills[d][end : end + 16, :] = spill_notes[...].astype(jnp.bfloat16)


def level_of(sizes, ref):
    planes = [
        sum(
            ref[p * sizes.columns + j].astype(jnp.float32) for j in range(sizes.columns)
        )
        for p in range(sizes.owners)
    ]
    counts = functools.reduce(jnp.maximum, planes)[0:1]
    lane = iota(counts.shape, 1)
    counts = jnp.where((lane >= sizes.rows) & (lane < sizes.rows + sizes.owners), counts, 0.0)
    most = jnp.max(counts, axis=1, keepdims=True) * sizes.per_slot
    level = jnp.zeros((1, 1), jnp.int32)
    for n in REST[:-1]:
        level = level + jnp.where(most > sizes.base + sizes.second * n // 16, 1, 0)
    return level


def regroup_kernel(sizes, at_ref, *refs):
    columns, owners, spill = sizes.columns, sizes.owners, sizes.spill
    spills, bases = refs[:columns], refs[columns : columns + owners]
    rests = refs[columns + owners : columns + 2 * owners]
    feet, notes, place = refs[columns + 2 * owners :]
    step = pl.program_id(0)
    owner = at_ref[2] ^ step
    end = sizes.lane_tiles * spill

    @pl.when(step == 0)
    def _():
        for d, ref in enumerate(spills):
            for n in range(sizes.lane_tiles):
                feet[d * spill : (d + 1) * spill, n * LANES : (n + 1) * LANES] = ref[
                    n * spill : (n + 1) * spill, :
                ]
            notes[:, d * spill : (d + 1) * spill] = ref[end : end + 16, :].astype(jnp.float32)

    mine = notes[8:9, :] == owner.astype(jnp.float32)
    total = jnp.zeros((1, 1), jnp.float32)
    keys = []
    for d in range(columns):
        here = mine[:, d * spill : (d + 1) * spill]
        position = total + notes[9:10, d * spill : (d + 1) * spill]
        inner = lax.rem(iota((1, spill), 1), jnp.int32(sizes.per_slot))
        keys.append(
            jnp.where(here, position.astype(jnp.int32) * sizes.per_slot + inner, -1)
        )
        total = total + jnp.sum(
            jnp.where(here, 1.0 / sizes.per_slot, 0.0), axis=1, keepdims=True
        )
    key = jnp.concatenate(keys, axis=1)
    place[...] = (iota(place.shape, 0) == key).astype(jnp.bfloat16)
    sorted_feet = jnp.dot(place[...], feet[...], preferred_element_type=jnp.float32)
    sorted_feet = sorted_feet.astype(jnp.bfloat16)
    moved = lax.dot_general(
        notes[0:8, :].astype(jnp.bfloat16),
        place[...],
        (((1,), (1,)), ((), ())),
        preferred_element_type=jnp.float32,
    )
    field, lane = iota(moved.shape, 0), iota(moved.shape, 1)
    empty = jnp.where(field == 0, jnp.float32(sizes.half), jnp.where(field == 5, 1.0, 0.0))
    moved = jnp.where(lane.astype(jnp.float32) < total * sizes.per_slot, moved, empty)
    moved = moved.astype(jnp.bfloat16)
    for o in range(owners):

        @pl.when(step == o)
        def _():
            for n in range(sizes.notes // 8):
                bases[o][n * 8 : (n + 1) * 8, :] = moved[
                    :, n * sizes.part : (n + 1) * sizes.part
                ]
            bases[o][sizes.notes :, :] = sorted_feet[: sizes.base]
            rests[o][...] = sorted_feet[sizes.base :]


def forward_first_kernel(sizes, at_ref, flux_ref, got_ref, all_ref, out_ref, level_ref):
    step = pl.program_id(0)
    feet, notes, plane = first_round(sizes, got_ref, step)
    sums = partial_sums(sizes, flux_ref, feet, notes, plane)

    @pl.when(step == 0)
    def _():
        out_ref[...] = sums
        level_ref[...] = jnp.broadcast_to(level_of(sizes, all_ref), level_ref.shape)

    @pl.when(step > 0)
    def _():
        out_ref[...] += sums


def forward_second_kernel(sizes, more, at_ref, flux_ref, before_ref, *refs):
    bases, rests, out_ref = refs[: sizes.owners], refs[sizes.owners : -1], refs[-1]
    feet, notes, plane = second_round(sizes, at_ref[2], bases, rests, not more)
    sums = before_ref[0] + partial_sums(sizes, flux_ref, feet, notes, plane)
    out_ref[...] = jnp.broadcast_to(sums[None], out_ref.shape)


def adjoint_kernel(sizes, chunks, at_ref, sums_ref, one_ref, *refs):
    bases, rests = refs[: sizes.owners], refs[sizes.owners : -3]
    modeled_ref, grad_ref, model = refs[-3:]
    step = pl.program_id(0)

    @pl.when(step == 0)
    def _():
        sums = jnp.sum(sums_ref[...], axis=0)
        model[...] = jnp.concatenate(thirds(sums), axis=0).astype(jnp.bfloat16)
        me = at_ref[0]
        page, within = lax.div(me, sizes.per_page), lax.rem(me, sizes.per_page)
        lane = iota((8, LANES), 1)
        own = jnp.zeros((8, LANES), jnp.float32)
        for p in range(sizes.pages):
            own = jnp.where(page == p, sums[p * 8 : (p + 1) * 8], own)
        result = jnp.zeros(modeled_ref.shape, jnp.float32)
        at_block = iota(modeled_ref.shape, 1)
        each = 8 // sizes.soundings
        for q in range(sizes.states // 8):
            picked = jnp.where(lane == q * sizes.per_page + within, own, 0.0)
            column = jnp.sum(picked, axis=1, keepdims=True)
            for n in range(each):
                values = column[n * sizes.soundings : (n + 1) * sizes.soundings]
                result = jnp.where(at_block == q * each + n, values, result)
        modeled_ref[...] = result

    @pl.when(step < chunks)
    def _():
        feet, notes, plane = first_round(sizes, one_ref, step)
        terms = gradient_terms(sizes, model[...], feet, notes, plane).reshape(grad_ref.shape)

        @pl.when(step == 0)
        def _():
            grad_ref[...] = terms

        @pl.when(step > 0)
        def _():
            grad_ref[...] += terms

    @pl.when(step == chunks)
    def _():
        feet, notes, plane = second_round(sizes, at_ref[2], bases, rests)
        terms = gradient_terms(sizes, model[...], feet, notes, plane)
        grad_ref[...] += terms.reshape(grad_ref.shape)


def shards(footprint, obs_hour, tile_list, tile_row, flux, observed, obs_var):
    sizes = Sizes(
        lax.axis_size("flux"), lax.axis_size("obs"), footprint.shape, flux.shape
    )
    owners, columns, devices, part = sizes.owners, sizes.columns, sizes.devices, sizes.part
    both = ("flux", "obs")
    params = pltpu.CompilerParams(vmem_limit_bytes=VMEM_BYTES)
    smem = pl.BlockSpec(memory_space=pltpu.SMEM)
    me = lax.axis_index("flux") * columns + lax.axis_index("obs")
    at = jnp.stack([me, lax.axis_index("obs"), lax.axis_index("flux")])
    flux = flux.transpose(1, 0, 2)

    first_height = sizes.lane_tiles * sizes.rows + 8
    spill_height = sizes.lane_tiles * sizes.spill + 16
    all_slots = sizes.slots * sizes.per_slot
    send, *spills = pl.pallas_call(
        functools.partial(pack_kernel, sizes),
        grid_spec=pltpu.PrefetchScalarGridSpec(
            num_scalar_prefetch=1,
            grid=(columns,),
            in_specs=[smem] * 5
            + [pl.BlockSpec((all_slots, part), lambda d, at: (0, d ^ at[1]))],
            out_specs=[
                pl.BlockSpec((owners, 1, first_height, LANES), lambda d, at: (0, d ^ at[1], 0, 0))
            ]
            + [pl.BlockSpec((spill_height, LANES), lambda d, at: (0, 0))] * columns,
            scratch_shapes=[
                pltpu.VMEM((owners * sizes.rows + sizes.spill, all_slots), jnp.bfloat16),
                pltpu.VMEM((owners, 8, LANES), jnp.float32),
                pltpu.VMEM((16, LANES), jnp.float32),
                pltpu.SMEM((owners + 1,), jnp.int32),
            ],
        ),
        out_shape=[pltpu.HBM((owners, columns, first_height, LANES), jnp.bfloat16)]
        + [jax.ShapeDtypeStruct((spill_height, LANES), jnp.bfloat16)] * columns,
        compiler_params=params,
        name="pack",
    )(
        at,
        tile_list.T,
        tile_row,
        obs_hour.T,
        observed.T,
        obs_var.T,
        footprint.reshape(all_slots, sizes.lane_tiles * columns * LANES),
    )
    got = lax.all_to_all(
        send.reshape(devices, first_height, LANES), both, split_axis=0, concat_axis=0, tiled=True
    )
    spills = spills[:1] + [
        lax.ppermute(spills[d], "obs", [(i, i ^ d) for i in range(columns)])
        for d in range(1, columns)
    ]
    second_height = sizes.notes + sizes.second
    base_height, more_height = sizes.notes + sizes.base, sizes.second - sizes.base
    outs = [(base_height, part)] * owners + [(more_height, part)] * owners
    parts = pl.pallas_call(
        functools.partial(regroup_kernel, sizes),
        grid_spec=pltpu.PrefetchScalarGridSpec(
            num_scalar_prefetch=1,
            grid=(owners,),
            in_specs=[pl.BlockSpec((spill_height, LANES), lambda o, at: (0, 0))] * columns,
            out_specs=[pl.BlockSpec(shape, lambda o, at: (0, 0)) for shape in outs],
            scratch_shapes=[
                pltpu.VMEM((columns * sizes.spill, part), jnp.bfloat16),
                pltpu.VMEM((16, columns * sizes.spill), jnp.float32),
                pltpu.VMEM((sizes.second, columns * sizes.spill), jnp.bfloat16),
            ],
        ),
        out_shape=[jax.ShapeDtypeStruct(shape, jnp.bfloat16) for shape in outs],
        compiler_params=params,
        name="regroup",
    )(at, *spills)

    def swap(arrays):
        return arrays[:1] + [
            lax.ppermute(arrays[n], "flux", [(i, i ^ n) for i in range(owners)])
            for n in range(1, owners)
        ]

    parts = list(parts)
    bases, rests = swap(parts[:owners]), parts[owners:]

    sources = min(devices, 1024 // sizes.rows)
    chunks = devices // sources
    copies = devices if devices <= 64 else 1
    height = 8 * sizes.pages
    flux_spec = pl.BlockSpec((sizes.hours, sizes.tiles, part), lambda i, at: (0, 0, at[1]))
    base_specs = [pl.BlockSpec((base_height, part), lambda i, at: (0, 0))] * owners
    early, level = pl.pallas_call(
        functools.partial(forward_first_kernel, sizes),
        grid_spec=pltpu.PrefetchScalarGridSpec(
            num_scalar_prefetch=1,
            grid=(chunks,),
            in_specs=[
                flux_spec,
                pl.BlockSpec((sources, first_height, LANES), lambda i, at: (i, 0, 0)),
                pl.BlockSpec((devices, 8, LANES), lambda i, at: (0, first_height // 8 - 1, 0)),
            ],
            out_specs=(
                pl.BlockSpec((height, LANES), lambda i, at: (0, 0)),
                pl.BlockSpec((8, LANES), lambda i, at: (0, 0)),
            ),
        ),
        out_shape=(
            jax.ShapeDtypeStruct((height, LANES), jnp.float32),
            jax.ShapeDtypeStruct((8, LANES), jnp.int32),
        ),
        compiler_params=params,
        name="forward_first",
    )(at, flux, got, got)

    def forward_second(flux, before, bases, rests, more):
        return pl.pallas_call(
            functools.partial(forward_second_kernel, sizes, more > 0),
            grid_spec=pltpu.PrefetchScalarGridSpec(
                num_scalar_prefetch=1,
                grid=(1,),
                in_specs=[flux_spec, pl.BlockSpec((1, height, LANES), lambda i, at: (0, 0, 0))]
                + base_specs
                + [pl.BlockSpec((more, part), lambda i, at: (0, 0))] * len(rests),
                out_specs=pl.BlockSpec((copies, height, LANES), lambda i, at: (0, 0, 0)),
            ),
            out_shape=jax.ShapeDtypeStruct((copies, height, LANES), jnp.float32),
            compiler_params=params,
            name="forward_more" if more else "forward_second",
        )(at, flux, before, *bases, *rests)

    sums = forward_second(flux, early[None], bases, [], 0)

    def finish(sixteenths):
        more = sizes.second * sixteenths // 16

        def run(flux, got, sums, bases, rests, at):
            if more:
                rests = rests[:1] + swap([rest[:more] for rest in rests])[1:]
                sums = forward_second(flux, sums, bases, rests, more)
            else:
                rests = []
            if copies > 1:
                sums = lax.all_to_all(sums, both, split_axis=0, concat_axis=0, tiled=True)
            else:
                sums = lax.psum(sums, both)
            return pl.pallas_call(
                functools.partial(adjoint_kernel, sizes, chunks),
                grid_spec=pltpu.PrefetchScalarGridSpec(
                    num_scalar_prefetch=1,
                    grid=(chunks + 1,),
                    in_specs=[
                        pl.BlockSpec((copies, height, LANES), lambda i, at: (0, 0, 0)),
                        pl.BlockSpec(
                            (sources, first_height, LANES),
                            lambda i, at: (jnp.minimum(i, chunks - 1), 0, 0),
                        ),
                    ]
                    + base_specs
                    + [pl.BlockSpec((more, part), lambda i, at: (0, 0))] * len(rests),
                    out_specs=(
                        pl.BlockSpec((sizes.soundings, sizes.blocks), lambda i, at: (0, 0)),
                        pl.BlockSpec((sizes.hours, sizes.tiles, part), lambda i, at: (0, 0, 0)),
                    ),
                    scratch_shapes=[pltpu.VMEM((3 * height, LANES), jnp.bfloat16)],
                ),
                out_shape=(
                    jax.ShapeDtypeStruct((sizes.soundings, sizes.blocks), jnp.float32),
                    jax.ShapeDtypeStruct((sizes.hours, sizes.tiles, part), jnp.float32),
                ),
                compiler_params=params,
                name="adjoint",
            )(at, sums, got, *bases, *rests)

        return run

    modeled, gradient = lax.switch(
        level[0, 0], [finish(n) for n in REST], flux, got, sums, bases, rests, at
    )
    return modeled.T, gradient.transpose(1, 0, 2)


def solution(mesh):
    placed = (
        P(("flux", "obs"), None, None, None, None),
        P(("flux", "obs"), None),
        P(("flux", "obs"), None),
        P(),
        P("flux", None, None),
        P(("flux", "obs"), None),
        P(("flux", "obs"), None),
    )
    return jax.shard_map(
        shards,
        mesh=mesh,
        in_specs=placed,
        out_specs=(P(("flux", "obs"), None), P("flux", None, "obs")),
        check_vma=False,
    )
```

```python
import functools

import jax
import jax.numpy as jnp
from jax import lax
from jax.experimental import pallas as pl
from jax.experimental.pallas import tpu as pltpu
from jax.sharding import PartitionSpec as P

LANES = 128
VMEM_BYTES = 48 * 1024 * 1024
ALL_VMEM_BYTES = 60 * 1024 * 1024
BASE = 8
REST = (0, 2, 8)
PACK_STEPS = 2


def iota(shape, dim):
    return lax.broadcasted_iota(jnp.int32, shape, dim)


def thirds(value):
    high = value.astype(jnp.bfloat16).astype(jnp.float32)
    rest = value - high
    middle = rest.astype(jnp.bfloat16).astype(jnp.float32)
    return high, middle, (rest - middle).astype(jnp.bfloat16).astype(jnp.float32)


class Sizes:
    def __init__(self, owners, columns, footprint, flux):
        self.owners, self.columns = owners, columns
        self.devices = owners * columns
        self.blocks, self.width, self.soundings, self.lags, cells = footprint
        self.tiles, self.hours = flux[0], flux[1]
        self.span = self.hours - self.lags + 1
        self.half = self.span * self.tiles // 2
        self.slots = self.blocks * self.width
        self.per_slot = self.soundings * self.lags
        self.part = cells // columns
        self.lane_tiles = self.part // LANES
        self.first = self.slots // owners
        self.rows = self.first * self.per_slot
        self.spill = self.slots // 2 * self.per_slot
        self.second = columns * self.first * self.per_slot
        self.base = self.second * BASE // 16
        self.notes = 8 * (self.second // self.part)
        self.states = self.blocks * self.soundings
        self.per_page = 8 * LANES // self.states
        self.pages = self.devices // self.per_page


def read_notes(sizes, notes, plane):
    lane = iota((1, notes.shape[1]), 1)
    inner = lax.rem(lane, jnp.int32(sizes.per_slot))
    base = notes[0:1]
    target = (base + sizes.half).astype(jnp.int32) + lax.rem(inner, jnp.int32(sizes.lags)) * sizes.tiles
    target = jnp.where(base > sizes.half - 0.5, -1, target)
    place = notes[1:2].astype(jnp.int32)
    block = lax.rem(place, jnp.int32(sizes.blocks))
    device = plane * sizes.columns + lax.div(place, jnp.int32(sizes.blocks))
    state = block * sizes.soundings + lax.div(inner, jnp.int32(sizes.lags))
    row = lax.div(device, jnp.int32(sizes.per_page)) * 8 + lax.rem(state, jnp.int32(8))
    column = lax.div(state, jnp.int32(8)) * sizes.per_page + lax.rem(device, jnp.int32(sizes.per_page))
    return target, row, column


def first_round(sizes, ref, step):
    sources, count = ref.shape[0], sizes.rows
    feet = jnp.concatenate(
        [
            ref[:, n * count : (n + 1) * count, :].reshape(sources * count, LANES)
            for n in range(sizes.lane_tiles)
        ],
        axis=1,
    )
    end = sizes.lane_tiles * count
    notes = jnp.concatenate(
        [ref[s, end : end + 8, :].astype(jnp.float32)[:, :count] for s in range(sources)], axis=1
    )
    lane = iota((1, sources * count), 1)
    plane = lax.div(step * sources + lax.div(lane, jnp.int32(count)), jnp.int32(sizes.columns))
    return feet, notes, plane


def second_round(sizes, flux_index, bases, rests, with_bases=True):
    notes = [
        jnp.concatenate(
            [ref[n * 8 : (n + 1) * 8, :].astype(jnp.float32) for n in range(sizes.notes // 8)],
            axis=1,
        )
        for ref in bases
    ]
    feet, kept, planes = [], [], []
    if with_bases:
        feet += [ref[sizes.notes :, :] for ref in bases]
        kept += [each[:, : sizes.base] for each in notes]
        planes.append(lax.div(iota((1, len(bases) * sizes.base), 1), jnp.int32(sizes.base)))
    if rests:
        more = rests[0].shape[0]
        feet += [ref[...] for ref in rests]
        kept += [each[:, sizes.base : sizes.base + more] for each in notes]
        planes.append(lax.div(iota((1, len(rests) * more), 1), jnp.int32(more)))
    plane = lax.bitwise_xor(jnp.concatenate(planes, axis=1), flux_index)
    return jnp.concatenate(feet, axis=0), jnp.concatenate(kept, axis=1), plane


def partial_sums(sizes, flux_ref, feet, notes, plane):
    target, row, column = read_notes(sizes, notes, plane)
    count = feet.shape[0]
    levels = sizes.hours * sizes.tiles
    products = lax.dot_general(
        flux_ref[...].reshape(levels, sizes.part),
        feet,
        (((1,), (1,)), ((), ())),
        preferred_element_type=jnp.float32,
    )
    chosen = jnp.where(iota((levels, count), 0) == target, products, 0.0)
    partial = jnp.sum(chosen, axis=0, keepdims=True)
    height = 8 * sizes.pages
    spread = jnp.where(iota((height, count), 0) == row, partial, 0.0)
    terms = jnp.concatenate(thirds(spread), axis=0).astype(jnp.bfloat16)
    lanes = (iota((LANES, count), 0) == column).astype(jnp.bfloat16)
    sums = lax.dot_general(
        terms, lanes, (((1,), (1,)), ((), ())), preferred_element_type=jnp.float32
    )
    return sums[:height] + sums[height : 2 * height] + sums[2 * height :]


def gradient_terms(sizes, model, feet, notes, plane):
    target, row, column = read_notes(sizes, notes, plane)
    count = feet.shape[0]
    height = 8 * sizes.pages
    lanes = (iota((LANES, count), 0) == column).astype(jnp.bfloat16)
    taken = jnp.dot(model, lanes, preferred_element_type=jnp.float32)
    taken = taken[:height] + taken[height : 2 * height] + taken[2 * height :]
    value = jnp.sum(
        jnp.where(iota((height, count), 0) == row, taken, 0.0), axis=0, keepdims=True
    )
    seen = notes[2:3] + notes[3:4] + notes[4:5]
    spread = notes[5:6] + notes[6:7] + notes[7:8]
    scaled = ((value - seen) / spread).astype(jnp.bfloat16).astype(jnp.float32)
    levels = sizes.hours * sizes.tiles
    coefficient = jnp.where(iota((levels, count), 0) == target, scaled, 0.0).astype(jnp.bfloat16)
    return jnp.dot(coefficient, feet, preferred_element_type=jnp.float32)


def pack_kernel(sizes, at_ref, *refs):
    tables, feet_ref, send_ref = refs[:5], refs[5], refs[6]
    spills = refs[7 : 7 + sizes.columns]
    place, first_notes, spill_notes, over_rows, count, *local, arrived = refs[7 + sizes.columns :]
    list_ref, row_ref, hour_ref, seen_ref, var_ref = local
    owners, per_slot = sizes.owners, sizes.per_slot
    step = pl.program_id(0)
    group = sizes.columns // PACK_STEPS

    @pl.when(step == 0)
    def _():
        copies = [
            pltpu.make_async_copy(table, here, arrived.at[n])
            for n, (table, here) in enumerate(zip(tables, local))
        ]
        for copy in copies:
            copy.start()
        for copy in copies:
            copy.wait()
        field, lane = iota((16, LANES), 0), iota((16, LANES), 1)
        inner = lane % per_slot
        sounding = inner // sizes.lags
        slot_at = lane // per_slot
        key_at = iota((1, sizes.slots * per_slot), 1)
        key = jnp.zeros(key_at.shape, jnp.int32)
        empty = jnp.where(field == 0, jnp.float32(sizes.half), 0.0)
        empty = jnp.where(field == 5, 1.0, jnp.where(field == 8, -1.0, empty))
        for o in range(owners):
            count[o] = 0
            first_notes[o] = empty[:8]
        count[owners] = 0
        left = empty
        for b in range(sizes.blocks):
            base = jnp.zeros(field.shape, jnp.float32)
            seen = jnp.zeros(field.shape, jnp.float32)
            spread = jnp.ones(field.shape, jnp.float32)
            for o in range(sizes.soundings):
                here = sounding == o
                hour = hour_ref[o, b] * sizes.tiles - sizes.half
                base = jnp.where(here, hour.astype(jnp.float32), base)
                seen = jnp.where(here, seen_ref[o, b], seen)
                spread = jnp.where(here, var_ref[o, b], spread)
            column = (b + sizes.blocks * at_ref[1]).astype(jnp.float32)
            pattern = jnp.where(field == 0, base, jnp.where(field == 1, column, 0.0))
            for n, term in enumerate(thirds(seen) + thirds(spread)):
                pattern = jnp.where(field == 2 + n, term, pattern)
            for k in range(sizes.width):
                stored = row_ref[list_ref[k, b]]
                owner = lax.div(stored, jnp.int32(sizes.tiles))
                tile = (stored - owner * sizes.tiles).astype(jnp.float32)
                position = count[owner]
                count[owner] = position + 1
                keep = position < sizes.first
                over = count[owners]
                count[owners] = over + jnp.where(keep, 0, 1)
                goes = jnp.where(
                    keep, owner * sizes.first + position, owners * sizes.first + over
                )
                value = jnp.where(field == 0, pattern + tile, pattern)
                value = jnp.where(field == 8, owner.astype(jnp.float32), value)
                value = jnp.where(
                    field == 9, (position - sizes.first).astype(jnp.float32), value
                )
                first_notes[owner] = jnp.where(
                    slot_at[:8] == jnp.where(keep, position, -1), value[:8], first_notes[owner]
                )
                left = jnp.where(slot_at == jnp.where(keep, -1, over), value, left)
                key = jnp.where(
                    key_at // per_slot == b * sizes.width + k,
                    goes * per_slot + key_at % per_slot,
                    key,
                )
        counts = jnp.zeros((8, LANES), jnp.float32)
        for o in range(owners):
            over = jnp.maximum(count[o] - sizes.first, 0).astype(jnp.float32)
            counts = jnp.where(lane[:8] == sizes.rows + o, over, counts)
        for o in range(owners):
            first_notes[o] = jnp.where(lane[:8] < sizes.rows, first_notes[o], counts)
        spill_notes[...] = left
        place[...] = (iota(place.shape, 0) == key).astype(jnp.bfloat16)

    feet = feet_ref[...].reshape(place.shape[1], group * sizes.part)
    packed = jnp.dot(place[...], feet, preferred_element_type=jnp.float32)
    packed = packed.astype(jnp.bfloat16)
    rows, spill, tiles = sizes.rows, sizes.spill, sizes.lane_tiles
    end = tiles * rows
    for c in range(group):
        for o in range(owners):
            for n in range(tiles):
                lanes = slice((c * tiles + n) * LANES, (c * tiles + n + 1) * LANES)
                send_ref[o, c, n * rows : (n + 1) * rows, :] = packed[
                    o * rows : (o + 1) * rows, lanes
                ]
            send_ref[o, c, end : end + 8, :] = first_notes[o].astype(jnp.bfloat16)
        for n in range(tiles):
            lanes = slice((c * tiles + n) * LANES, (c * tiles + n + 1) * LANES)
            over_rows[c, n * spill : (n + 1) * spill, :] = packed[owners * rows :, lanes]
    for d in range(sizes.columns):

        @pl.when(step == d // group)
        def _():
            spills[d][: tiles * spill, :] = over_rows[(d ^ at_ref[1]) % group]
            spills[d][tiles * spill :, :] = spill_notes[...].astype(jnp.bfloat16)


def level_of(sizes, ref):
    planes = [
        sum(
            ref[p * sizes.columns + j].astype(jnp.float32) for j in range(sizes.columns)
        )
        for p in range(sizes.owners)
    ]
    counts = functools.reduce(jnp.maximum, planes)[0:1]
    lane = iota(counts.shape, 1)
    counts = jnp.where((lane >= sizes.rows) & (lane < sizes.rows + sizes.owners), counts, 0.0)
    most = jnp.max(counts, axis=1, keepdims=True) * sizes.per_slot
    level = jnp.zeros((1, 1), jnp.int32)
    for n in REST[:-1]:
        level = level + jnp.where(most > sizes.base + sizes.second * n // 16, 1, 0)
    return level


def regroup_kernel(sizes, at_ref, *refs):
    columns, owners, spill = sizes.columns, sizes.owners, sizes.spill
    spills, bases = refs[:columns], refs[columns : columns + owners]
    rests = refs[columns + owners : columns + 2 * owners]
    feet, notes, place = refs[columns + 2 * owners :]
    step = pl.program_id(0)
    owner = at_ref[2] ^ step
    end = sizes.lane_tiles * spill

    @pl.when(step == 0)
    def _():
        for d, ref in enumerate(spills):
            for n in range(sizes.lane_tiles):
                feet[d * spill : (d + 1) * spill, n * LANES : (n + 1) * LANES] = ref[
                    n * spill : (n + 1) * spill, :
                ]
            notes[:, d * spill : (d + 1) * spill] = ref[end : end + 16, :].astype(jnp.float32)

    mine = notes[8:9, :] == owner.astype(jnp.float32)
    total = jnp.zeros((1, 1), jnp.float32)
    keys = []
    for d in range(columns):
        here = mine[:, d * spill : (d + 1) * spill]
        position = total + notes[9:10, d * spill : (d + 1) * spill]
        inner = lax.rem(iota((1, spill), 1), jnp.int32(sizes.per_slot))
        keys.append(
            jnp.where(here, position.astype(jnp.int32) * sizes.per_slot + inner, -1)
        )
        total = total + jnp.sum(
            jnp.where(here, 1.0 / sizes.per_slot, 0.0), axis=1, keepdims=True
        )
    key = jnp.concatenate(keys, axis=1)
    place[...] = (iota(place.shape, 0) == key).astype(jnp.bfloat16)
    sorted_feet = jnp.dot(place[...], feet[...], preferred_element_type=jnp.float32)
    sorted_feet = sorted_feet.astype(jnp.bfloat16)
    moved = lax.dot_general(
        notes[0:8, :].astype(jnp.bfloat16),
        place[...],
        (((1,), (1,)), ((), ())),
        preferred_element_type=jnp.float32,
    )
    field, lane = iota(moved.shape, 0), iota(moved.shape, 1)
    empty = jnp.where(field == 0, jnp.float32(sizes.half), jnp.where(field == 5, 1.0, 0.0))
    moved = jnp.where(lane.astype(jnp.float32) < total * sizes.per_slot, moved, empty)
    moved = moved.astype(jnp.bfloat16)
    for o in range(owners):

        @pl.when(step == o)
        def _():
            for n in range(sizes.notes // 8):
                bases[o][n * 8 : (n + 1) * 8, :] = moved[
                    :, n * sizes.part : (n + 1) * sizes.part
                ]
            bases[o][sizes.notes :, :] = sorted_feet[: sizes.base]
            rests[o][...] = sorted_feet[sizes.base :]


def forward_first_kernel(sizes, at_ref, flux_ref, got_ref, all_ref, out_ref, level_ref):
    step = pl.program_id(0)
    feet, notes, plane = first_round(sizes, got_ref, step)
    sums = partial_sums(sizes, flux_ref, feet, notes, plane)

    @pl.when(step == 0)
    def _():
        out_ref[...] = sums
        level_ref[...] = jnp.broadcast_to(level_of(sizes, all_ref), level_ref.shape)

    @pl.when(step > 0)
    def _():
        out_ref[...] += sums


def forward_second_kernel(sizes, more, at_ref, flux_ref, before_ref, *refs):
    bases, rests, out_ref = refs[: sizes.owners], refs[sizes.owners : -1], refs[-1]
    feet, notes, plane = second_round(sizes, at_ref[2], bases, rests, not more)
    sums = before_ref[0] + partial_sums(sizes, flux_ref, feet, notes, plane)
    out_ref[...] = jnp.broadcast_to(sums[None], out_ref.shape)


def adjoint_kernel(sizes, chunks, at_ref, sums_ref, one_ref, *refs):
    bases, rests = refs[: sizes.owners], refs[sizes.owners : -3]
    modeled_ref, grad_ref, model = refs[-3:]
    step = pl.program_id(0)

    @pl.when(step == 0)
    def _():
        sums = jnp.sum(sums_ref[...], axis=0)
        model[...] = jnp.concatenate(thirds(sums), axis=0).astype(jnp.bfloat16)
        me = at_ref[0]
        page, within = lax.div(me, sizes.per_page), lax.rem(me, sizes.per_page)
        lane = iota((8, LANES), 1)
        own = jnp.zeros((8, LANES), jnp.float32)
        for p in range(sizes.pages):
            own = jnp.where(page == p, sums[p * 8 : (p + 1) * 8], own)
        result = jnp.zeros(modeled_ref.shape, jnp.float32)
        at_block = iota(modeled_ref.shape, 1)
        each = 8 // sizes.soundings
        for q in range(sizes.states // 8):
            picked = jnp.where(lane == q * sizes.per_page + within, own, 0.0)
            column = jnp.sum(picked, axis=1, keepdims=True)
            for n in range(each):
                values = column[n * sizes.soundings : (n + 1) * sizes.soundings]
                result = jnp.where(at_block == q * each + n, values, result)
        modeled_ref[...] = result

    @pl.when(step < chunks)
    def _():
        feet, notes, plane = first_round(sizes, one_ref, step)
        terms = gradient_terms(sizes, model[...], feet, notes, plane).reshape(grad_ref.shape)

        @pl.when(step == 0)
        def _():
            grad_ref[...] = terms

        @pl.when(step > 0)
        def _():
            grad_ref[...] += terms

    @pl.when(step == chunks)
    def _():
        feet, notes, plane = second_round(sizes, at_ref[2], bases, rests)
        terms = gradient_terms(sizes, model[...], feet, notes, plane)
        grad_ref[...] += terms.reshape(grad_ref.shape)


def shards(footprint, obs_hour, tile_list, tile_row, flux, observed, obs_var):
    sizes = Sizes(
        lax.axis_size("flux"), lax.axis_size("obs"), footprint.shape, flux.shape
    )
    owners, columns, devices, part = sizes.owners, sizes.columns, sizes.devices, sizes.part
    both = ("flux", "obs")
    params = pltpu.CompilerParams(vmem_limit_bytes=VMEM_BYTES)
    me = lax.axis_index("flux") * columns + lax.axis_index("obs")
    at = jnp.stack([me, lax.axis_index("obs"), lax.axis_index("flux")])
    flux = flux.transpose(1, 0, 2)

    first_height = sizes.lane_tiles * sizes.rows + 8
    spill_height = sizes.lane_tiles * sizes.spill + 16
    all_slots = sizes.slots * sizes.per_slot
    group = columns // PACK_STEPS
    tables = (tile_list.T, tile_row, obs_hour.T, observed.T, obs_var.T)
    send, *spills = pl.pallas_call(
        functools.partial(pack_kernel, sizes),
        grid_spec=pltpu.PrefetchScalarGridSpec(
            num_scalar_prefetch=1,
            grid=(PACK_STEPS,),
            in_specs=[pl.BlockSpec(memory_space=pltpu.HBM)] * 5
            + [
                pl.BlockSpec(
                    (all_slots // sizes.lags, sizes.lags, group * part),
                    lambda i, at: (0, 0, i ^ (at[1] // group)),
                )
            ],
            out_specs=[
                pl.BlockSpec(
                    (owners, group, first_height, LANES),
                    lambda i, at: (0, i ^ (at[1] // group), 0, 0),
                )
            ]
            + [pl.BlockSpec((spill_height, LANES), lambda i, at: (0, 0))] * columns,
            scratch_shapes=[
                pltpu.VMEM((owners * sizes.rows + sizes.spill, all_slots), jnp.bfloat16),
                pltpu.VMEM((owners, 8, LANES), jnp.float32),
                pltpu.VMEM((16, LANES), jnp.float32),
                pltpu.VMEM((group, sizes.lane_tiles * sizes.spill, LANES), jnp.bfloat16),
                pltpu.SMEM((owners + 1,), jnp.int32),
            ]
            + [pltpu.SMEM(table.shape, table.dtype) for table in tables]
            + [pltpu.SemaphoreType.DMA((5,))],
        ),
        out_shape=[pltpu.HBM((owners, columns, first_height, LANES), jnp.bfloat16)]
        + [jax.ShapeDtypeStruct((spill_height, LANES), jnp.bfloat16)] * columns,
        compiler_params=pltpu.CompilerParams(vmem_limit_bytes=ALL_VMEM_BYTES),
        name="pack",
    )(
        at,
        *tables,
        footprint.reshape(all_slots // sizes.lags, sizes.lags, columns * part),
    )
    got = lax.all_to_all(
        send.reshape(devices, first_height, LANES), both, split_axis=0, concat_axis=0, tiled=True
    )
    spills = spills[:1] + [
        lax.ppermute(spills[d], "obs", [(i, i ^ d) for i in range(columns)])
        for d in range(1, columns)
    ]
    second_height = sizes.notes + sizes.second
    base_height, more_height = sizes.notes + sizes.base, sizes.second - sizes.base
    outs = [(base_height, part)] * owners + [(more_height, part)] * owners
    parts = pl.pallas_call(
        functools.partial(regroup_kernel, sizes),
        grid_spec=pltpu.PrefetchScalarGridSpec(
            num_scalar_prefetch=1,
            grid=(owners,),
            in_specs=[pl.BlockSpec((spill_height, LANES), lambda o, at: (0, 0))] * columns,
            out_specs=[pl.BlockSpec(shape, lambda o, at: (0, 0)) for shape in outs],
            scratch_shapes=[
                pltpu.VMEM((columns * sizes.spill, part), jnp.bfloat16),
                pltpu.VMEM((16, columns * sizes.spill), jnp.float32),
                pltpu.VMEM((sizes.second, columns * sizes.spill), jnp.bfloat16),
            ],
        ),
        out_shape=[jax.ShapeDtypeStruct(shape, jnp.bfloat16) for shape in outs],
        compiler_params=params,
        name="regroup",
    )(at, *spills)

    def swap(arrays):
        return arrays[:1] + [
            lax.ppermute(arrays[n], "flux", [(i, i ^ n) for i in range(owners)])
            for n in range(1, owners)
        ]

    parts = list(parts)
    bases, rests = swap(parts[:owners]), parts[owners:]

    sources = min(devices, 1024 // sizes.rows)
    chunks = devices // sources
    copies = devices if devices <= 64 else 1
    height = 8 * sizes.pages
    flux_spec = pl.BlockSpec((sizes.hours, sizes.tiles, part), lambda i, at: (0, 0, at[1]))
    base_specs = [pl.BlockSpec((base_height, part), lambda i, at: (0, 0))] * owners
    early, level = pl.pallas_call(
        functools.partial(forward_first_kernel, sizes),
        grid_spec=pltpu.PrefetchScalarGridSpec(
            num_scalar_prefetch=1,
            grid=(chunks,),
            in_specs=[
                flux_spec,
                pl.BlockSpec((sources, first_height, LANES), lambda i, at: (i, 0, 0)),
                pl.BlockSpec((devices, 8, LANES), lambda i, at: (0, first_height // 8 - 1, 0)),
            ],
            out_specs=(
                pl.BlockSpec((height, LANES), lambda i, at: (0, 0)),
                pl.BlockSpec((8, LANES), lambda i, at: (0, 0)),
            ),
        ),
        out_shape=(
            jax.ShapeDtypeStruct((height, LANES), jnp.float32),
            jax.ShapeDtypeStruct((8, LANES), jnp.int32),
        ),
        compiler_params=params,
        name="forward_first",
    )(at, flux, got, got)

    def forward_second(flux, before, bases, rests, more):
        return pl.pallas_call(
            functools.partial(forward_second_kernel, sizes, more > 0),
            grid_spec=pltpu.PrefetchScalarGridSpec(
                num_scalar_prefetch=1,
                grid=(1,),
                in_specs=[flux_spec, pl.BlockSpec((1, height, LANES), lambda i, at: (0, 0, 0))]
                + base_specs
                + [pl.BlockSpec((more, part), lambda i, at: (0, 0))] * len(rests),
                out_specs=pl.BlockSpec((copies, height, LANES), lambda i, at: (0, 0, 0)),
            ),
            out_shape=jax.ShapeDtypeStruct((copies, height, LANES), jnp.float32),
            compiler_params=params,
            name="forward_more" if more else "forward_second",
        )(at, flux, before, *bases, *rests)

    sums = forward_second(flux, early[None], bases, [], 0)

    def finish(sixteenths):
        more = sizes.second * sixteenths // 16

        def run(flux, got, sums, bases, rests, at):
            if more:
                rests = rests[:1] + swap([rest[:more] for rest in rests])[1:]
                sums = forward_second(flux, sums, bases, rests, more)
            else:
                rests = []
            if copies > 1:
                sums = lax.all_to_all(sums, both, split_axis=0, concat_axis=0, tiled=True)
            else:
                sums = lax.psum(sums, both)
            return pl.pallas_call(
                functools.partial(adjoint_kernel, sizes, chunks),
                grid_spec=pltpu.PrefetchScalarGridSpec(
                    num_scalar_prefetch=1,
                    grid=(chunks + 1,),
                    in_specs=[
                        pl.BlockSpec((copies, height, LANES), lambda i, at: (0, 0, 0)),
                        pl.BlockSpec(
                            (sources, first_height, LANES),
                            lambda i, at: (jnp.minimum(i, chunks - 1), 0, 0),
                        ),
                    ]
                    + base_specs
                    + [pl.BlockSpec((more, part), lambda i, at: (0, 0))] * len(rests),
                    out_specs=(
                        pl.BlockSpec((sizes.soundings, sizes.blocks), lambda i, at: (0, 0)),
                        pl.BlockSpec((sizes.hours, sizes.tiles, part), lambda i, at: (0, 0, 0)),
                    ),
                    scratch_shapes=[pltpu.VMEM((3 * height, LANES), jnp.bfloat16)],
                ),
                out_shape=(
                    jax.ShapeDtypeStruct((sizes.soundings, sizes.blocks), jnp.float32),
                    jax.ShapeDtypeStruct((sizes.hours, sizes.tiles, part), jnp.float32),
                ),
                compiler_params=params,
                name="adjoint",
            )(at, sums, got, *bases, *rests)

        return run

    modeled, gradient = lax.switch(
        level[0, 0], [finish(n) for n in REST], flux, got, sums, bases, rests, at
    )
    return modeled.T, gradient.transpose(1, 0, 2)


def solution(mesh):
    placed = (
        P(("flux", "obs"), None, None, None, None),
        P(("flux", "obs"), None),
        P(("flux", "obs"), None),
        P(),
        P("flux", None, None),
        P(("flux", "obs"), None),
        P(("flux", "obs"), None),
    )
    return jax.shard_map(
        shards,
        mesh=mesh,
        in_specs=placed,
        out_specs=(P(("flux", "obs"), None), P("flux", None, "obs")),
        check_vma=False,
    )
```

```python
import functools

import jax
import jax.numpy as jnp
from jax import lax
from jax.experimental import pallas as pl
from jax.experimental.pallas import tpu as pltpu
from jax.sharding import PartitionSpec as P

LANES = 128
VMEM_BYTES = 48 * 1024 * 1024
ALL_VMEM_BYTES = 60 * 1024 * 1024
BASE = 8
REST = (0, 2, 8)
PACK_STEPS = 2


def iota(shape, dim):
    return lax.broadcasted_iota(jnp.int32, shape, dim)


def thirds(value):
    high = value.astype(jnp.bfloat16).astype(jnp.float32)
    rest = value - high
    middle = rest.astype(jnp.bfloat16).astype(jnp.float32)
    return high, middle, (rest - middle).astype(jnp.bfloat16).astype(jnp.float32)


class Sizes:
    def __init__(self, owners, columns, footprint, flux):
        self.owners, self.columns = owners, columns
        self.devices = owners * columns
        self.blocks, self.width, self.soundings, self.lags, cells = footprint
        self.tiles, self.hours = flux[0], flux[1]
        self.span = self.hours - self.lags + 1
        self.half = self.span * self.tiles // 2
        self.slots = self.blocks * self.width
        self.per_slot = self.soundings * self.lags
        self.part = cells // columns
        self.lane_tiles = self.part // LANES
        self.first = self.slots // owners
        self.rows = self.first * self.per_slot
        self.spill = self.slots // 2 * self.per_slot
        self.second = columns * self.first * self.per_slot
        self.base = self.second * BASE // 16
        self.notes = 8 * (self.second // self.part)
        self.states = self.blocks * self.soundings
        self.per_page = 8 * LANES // self.states
        self.pages = self.devices // self.per_page


def read_notes(sizes, notes, plane):
    lane = iota((1, notes.shape[1]), 1)
    inner = lax.rem(lane, jnp.int32(sizes.per_slot))
    base = notes[0:1]
    target = (base + sizes.half).astype(jnp.int32) + lax.rem(inner, jnp.int32(sizes.lags)) * sizes.tiles
    target = jnp.where(base > sizes.half - 0.5, -1, target)
    place = notes[1:2].astype(jnp.int32)
    block = lax.rem(place, jnp.int32(sizes.blocks))
    device = plane * sizes.columns + lax.div(place, jnp.int32(sizes.blocks))
    state = block * sizes.soundings + lax.div(inner, jnp.int32(sizes.lags))
    row = lax.div(device, jnp.int32(sizes.per_page)) * 8 + lax.rem(state, jnp.int32(8))
    column = lax.div(state, jnp.int32(8)) * sizes.per_page + lax.rem(device, jnp.int32(sizes.per_page))
    seen = notes[2:3] + notes[3:4] + notes[4:5]
    spread = notes[5:6] + notes[6:7] + notes[7:8]
    places = [each.astype(jnp.float32) for each in (target, row, column)]
    return jnp.concatenate(places + [seen, spread, jnp.zeros((3, lane.shape[1]), jnp.float32)], axis=0)


def first_round(sizes, ref, step):
    sources, count = ref.shape[0], sizes.rows
    feet = jnp.concatenate(
        [
            ref[:, n * count : (n + 1) * count, :].reshape(sources * count, LANES)
            for n in range(sizes.lane_tiles)
        ],
        axis=1,
    )
    end = sizes.lane_tiles * count
    notes = jnp.concatenate(
        [ref[s, end : end + 8, :].astype(jnp.float32)[:, :count] for s in range(sources)], axis=1
    )
    lane = iota((1, sources * count), 1)
    plane = lax.div(step * sources + lax.div(lane, jnp.int32(count)), jnp.int32(sizes.columns))
    return feet, notes, plane


def second_round(sizes, flux_index, bases, rests, with_bases=True):
    notes = [
        jnp.concatenate(
            [ref[n * 8 : (n + 1) * 8, :].astype(jnp.float32) for n in range(sizes.notes // 8)],
            axis=1,
        )
        for ref in bases
    ]
    feet, kept, planes = [], [], []
    if with_bases:
        feet += [ref[sizes.notes :, :] for ref in bases]
        kept += [each[:, : sizes.base] for each in notes]
        planes.append(lax.div(iota((1, len(bases) * sizes.base), 1), jnp.int32(sizes.base)))
    if rests:
        more = rests[0].shape[0]
        feet += [ref[...] for ref in rests]
        kept += [each[:, sizes.base : sizes.base + more] for each in notes]
        planes.append(lax.div(iota((1, len(rests) * more), 1), jnp.int32(more)))
    plane = lax.bitwise_xor(jnp.concatenate(planes, axis=1), flux_index)
    return jnp.concatenate(feet, axis=0), jnp.concatenate(kept, axis=1), plane


def partial_sums(sizes, flux_ref, feet, read):
    target, row, column = (read[n : n + 1].astype(jnp.int32) for n in range(3))
    count = feet.shape[0]
    levels = sizes.hours * sizes.tiles
    products = lax.dot_general(
        flux_ref[...].reshape(levels, sizes.part),
        feet,
        (((1,), (1,)), ((), ())),
        preferred_element_type=jnp.float32,
    )
    chosen = jnp.where(iota((levels, count), 0) == target, products, 0.0)
    partial = jnp.sum(chosen, axis=0, keepdims=True)
    height = 8 * sizes.pages
    spread = jnp.where(iota((height, count), 0) == row, partial, 0.0)
    terms = jnp.concatenate(thirds(spread), axis=0).astype(jnp.bfloat16)
    lanes = (iota((LANES, count), 0) == column).astype(jnp.bfloat16)
    sums = lax.dot_general(
        terms, lanes, (((1,), (1,)), ((), ())), preferred_element_type=jnp.float32
    )
    return sums[:height] + sums[height : 2 * height] + sums[2 * height :]


def coefficients(sizes, model, read):
    target, row, column = (read[n : n + 1].astype(jnp.int32) for n in range(3))
    count = read.shape[1]
    height = 8 * sizes.pages
    lanes = (iota((LANES, count), 0) == column).astype(jnp.bfloat16)
    taken = jnp.dot(model, lanes, preferred_element_type=jnp.float32)
    taken = taken[:height] + taken[height : 2 * height] + taken[2 * height :]
    value = jnp.sum(
        jnp.where(iota((height, count), 0) == row, taken, 0.0), axis=0, keepdims=True
    )
    scaled = ((value - read[3:4]) / read[4:5]).astype(jnp.bfloat16).astype(jnp.float32)
    levels = sizes.hours * sizes.tiles
    return jnp.where(iota((levels, count), 0) == target, scaled, 0.0).astype(jnp.bfloat16)


def pack_kernel(sizes, at_ref, *refs):
    tables, feet_ref, send_ref = refs[:5], refs[5], refs[6]
    spills = refs[7 : 7 + sizes.columns]
    feet, sent, spilled, first_notes, count, *local = refs[7 + sizes.columns : -4]
    arrived, feet_arrived, sent_done, over_done = refs[-4:]
    list_ref, row_ref, hour_ref, seen_ref, var_ref = local
    owners, per_slot = sizes.owners, sizes.per_slot
    group = sizes.columns // PACK_STEPS
    mine = at_ref[1]
    tables = [
        pltpu.make_async_copy(table, here, arrived.at[n])
        for n, (table, here) in enumerate(zip(tables, local))
    ]
    for copy in tables:
        copy.start()
    firsts = [pl.multiple_of((i ^ (mine // group)) * group, group) for i in range(PACK_STEPS)]
    loads = []
    for i, first in enumerate(firsts):
        lanes = pl.ds(pl.multiple_of(first * sizes.part, LANES), group * sizes.part)
        loads.append(
            pltpu.make_async_copy(feet_ref.at[:, :, lanes], feet.at[i], feet_arrived.at[i])
        )
        loads[-1].start()
    for copy in tables:
        copy.wait()

    field, lane = iota((16, LANES), 0), iota((16, LANES), 1)
    inner = lane % per_slot
    sounding = inner // sizes.lags
    slot_at = lane // per_slot
    key_at = iota((1, sizes.slots * per_slot), 1)
    key = jnp.zeros(key_at.shape, jnp.int32)
    empty = jnp.where(field == 0, jnp.float32(sizes.half), 0.0)
    empty = jnp.where(field == 5, 1.0, jnp.where(field == 8, -1.0, empty))
    for o in range(owners):
        count[o] = 0
        first_notes[o] = empty[:8]
    count[owners] = 0
    left = empty
    for b in range(sizes.blocks):
        base = jnp.zeros(field.shape, jnp.float32)
        seen = jnp.zeros(field.shape, jnp.float32)
        spread = jnp.ones(field.shape, jnp.float32)
        for o in range(sizes.soundings):
            here = sounding == o
            hour = hour_ref[o, b] * sizes.tiles - sizes.half
            base = jnp.where(here, hour.astype(jnp.float32), base)
            seen = jnp.where(here, seen_ref[o, b], seen)
            spread = jnp.where(here, var_ref[o, b], spread)
        column = (b + sizes.blocks * at_ref[1]).astype(jnp.float32)
        pattern = jnp.where(field == 0, base, jnp.where(field == 1, column, 0.0))
        for n, term in enumerate(thirds(seen) + thirds(spread)):
            pattern = jnp.where(field == 2 + n, term, pattern)
        for k in range(sizes.width):
            stored = row_ref[list_ref[k, b]]
            owner = lax.div(stored, jnp.int32(sizes.tiles))
            tile = (stored - owner * sizes.tiles).astype(jnp.float32)
            position = count[owner]
            count[owner] = position + 1
            keep = position < sizes.first
            over = count[owners]
            count[owners] = over + jnp.where(keep, 0, 1)
            goes = jnp.where(
                keep, owner * sizes.first + position, owners * sizes.first + over
            )
            value = jnp.where(field == 0, pattern + tile, pattern)
            value = jnp.where(field == 8, owner.astype(jnp.float32), value)
            value = jnp.where(
                field == 9, (position - sizes.first).astype(jnp.float32), value
            )
            first_notes[owner] = jnp.where(
                slot_at[:8] == jnp.where(keep, position, -1), value[:8], first_notes[owner]
            )
            left = jnp.where(slot_at == jnp.where(keep, -1, over), value, left)
            key = jnp.where(
                key_at // per_slot == b * sizes.width + k,
                goes * per_slot + key_at % per_slot,
                key,
            )
    counts = jnp.zeros((8, LANES), jnp.float32)
    for o in range(owners):
        over = jnp.maximum(count[o] - sizes.first, 0).astype(jnp.float32)
        counts = jnp.where(lane[:8] == sizes.rows + o, over, counts)
    for o in range(owners):
        first_notes[o] = jnp.where(lane[:8] < sizes.rows, first_notes[o], counts)
    place = (iota((owners * sizes.rows + sizes.spill, key.shape[1]), 0) == key).astype(
        jnp.bfloat16
    )
    rows, spill, tiles = sizes.rows, sizes.spill, sizes.lane_tiles
    end = tiles * rows
    stores = []
    for i, first in enumerate(firsts):
        loads[i].wait()
        packed = jnp.dot(
            place,
            feet[i].reshape(key.shape[1], group * sizes.part),
            preferred_element_type=jnp.float32,
        ).astype(jnp.bfloat16)
        for c in range(group):
            for o in range(owners):
                for n in range(tiles):
                    lanes = slice((c * tiles + n) * LANES, (c * tiles + n + 1) * LANES)
                    sent[i, o, c, n * rows : (n + 1) * rows, :] = packed[
                        o * rows : (o + 1) * rows, lanes
                    ]
                sent[i, o, c, end : end + 8, :] = first_notes[o].astype(jnp.bfloat16)
            for n in range(tiles):
                lanes = slice((c * tiles + n) * LANES, (c * tiles + n + 1) * LANES)
                spilled[i, c, n * spill : (n + 1) * spill, :] = packed[owners * rows :, lanes]
            spilled[i, c, tiles * spill :, :] = left.astype(jnp.bfloat16)
        stores.append(
            pltpu.make_async_copy(
                sent.at[i], send_ref.at[:, pl.ds(first, group)], sent_done.at[i]
            )
        )
        stores[-1].start()
        for d in range(i * group, (i + 1) * group):
            stores.append(
                pltpu.make_async_copy(spilled.at[i, (d ^ mine) % group], spills[d], over_done.at[d])
            )
            stores[-1].start()
    for copy in stores:
        copy.wait()


def level_of(sizes, ref):
    planes = [
        sum(
            ref[p * sizes.columns + j].astype(jnp.float32) for j in range(sizes.columns)
        )
        for p in range(sizes.owners)
    ]
    counts = functools.reduce(jnp.maximum, planes)[0:1]
    lane = iota(counts.shape, 1)
    counts = jnp.where((lane >= sizes.rows) & (lane < sizes.rows + sizes.owners), counts, 0.0)
    most = jnp.max(counts, axis=1, keepdims=True) * sizes.per_slot
    level = jnp.zeros((1, 1), jnp.int32)
    for n in REST[:-1]:
        level = level + jnp.where(most > sizes.base + sizes.second * n // 16, 1, 0)
    return level


def regroup_kernel(sizes, at_ref, *refs):
    columns, owners, spill = sizes.columns, sizes.owners, sizes.spill
    spills, bases = refs[:columns], refs[columns : columns + owners]
    rests = refs[columns + owners : columns + 2 * owners]
    feet, notes, place = refs[columns + 2 * owners :]
    step = pl.program_id(0)
    owner = at_ref[2] ^ step
    end = sizes.lane_tiles * spill

    @pl.when(step == 0)
    def _():
        for d, ref in enumerate(spills):
            for n in range(sizes.lane_tiles):
                feet[d * spill : (d + 1) * spill, n * LANES : (n + 1) * LANES] = ref[
                    n * spill : (n + 1) * spill, :
                ]
            notes[:, d * spill : (d + 1) * spill] = ref[end : end + 16, :].astype(jnp.float32)

    mine = notes[8:9, :] == owner.astype(jnp.float32)
    total = jnp.zeros((1, 1), jnp.float32)
    keys = []
    for d in range(columns):
        here = mine[:, d * spill : (d + 1) * spill]
        position = total + notes[9:10, d * spill : (d + 1) * spill]
        inner = lax.rem(iota((1, spill), 1), jnp.int32(sizes.per_slot))
        keys.append(
            jnp.where(here, position.astype(jnp.int32) * sizes.per_slot + inner, -1)
        )
        total = total + jnp.sum(
            jnp.where(here, 1.0 / sizes.per_slot, 0.0), axis=1, keepdims=True
        )
    key = jnp.concatenate(keys, axis=1)
    place[...] = (iota(place.shape, 0) == key).astype(jnp.bfloat16)
    sorted_feet = jnp.dot(place[...], feet[...], preferred_element_type=jnp.float32)
    sorted_feet = sorted_feet.astype(jnp.bfloat16)
    moved = lax.dot_general(
        notes[0:8, :].astype(jnp.bfloat16),
        place[...],
        (((1,), (1,)), ((), ())),
        preferred_element_type=jnp.float32,
    )
    field, lane = iota(moved.shape, 0), iota(moved.shape, 1)
    empty = jnp.where(field == 0, jnp.float32(sizes.half), jnp.where(field == 5, 1.0, 0.0))
    moved = jnp.where(lane.astype(jnp.float32) < total * sizes.per_slot, moved, empty)
    moved = moved.astype(jnp.bfloat16)
    for o in range(owners):

        @pl.when(step == o)
        def _():
            for n in range(sizes.notes // 8):
                bases[o][n * 8 : (n + 1) * 8, :] = moved[
                    :, n * sizes.part : (n + 1) * sizes.part
                ]
            bases[o][sizes.notes :, :] = sorted_feet[: sizes.base]
            rests[o][...] = sorted_feet[sizes.base :]


def forward_first_kernel(
    sizes, at_ref, flux_ref, got_ref, all_ref, out_ref, level_ref, feet_ref, read_ref
):
    step = pl.program_id(0)
    feet, notes, plane = first_round(sizes, got_ref, step)
    read = read_notes(sizes, notes, plane)
    feet_ref[...], read_ref[...] = feet, read
    sums = partial_sums(sizes, flux_ref, feet, read)

    @pl.when(step == 0)
    def _():
        out_ref[...] = sums
        level_ref[...] = jnp.broadcast_to(level_of(sizes, all_ref), level_ref.shape)

    @pl.when(step > 0)
    def _():
        out_ref[...] += sums


def forward_second_kernel(sizes, more, at_ref, flux_ref, before_ref, *refs):
    bases, rests, (out_ref, read_ref) = refs[: sizes.owners], refs[sizes.owners : -2], refs[-2:]
    feet, notes, plane = second_round(sizes, at_ref[2], bases, rests, not more)
    read = read_notes(sizes, notes, plane)
    read_ref[...] = read
    sums = before_ref[0] + partial_sums(sizes, flux_ref, feet, read)
    out_ref[...] = jnp.broadcast_to(sums[None], out_ref.shape)


def adjoint_kernel(sizes, at_ref, sums_ref, feet_ref, read_ref, read_second_ref, *refs):
    bases, rests = refs[: sizes.owners], refs[sizes.owners : -4]
    modeled_ref, out_ref, grad_ref, written = refs[-4:]
    sums = jnp.sum(sums_ref[...], axis=0)
    model = jnp.concatenate(thirds(sums), axis=0).astype(jnp.bfloat16)
    me = at_ref[0]
    page, within = lax.div(me, sizes.per_page), lax.rem(me, sizes.per_page)
    lane = iota((8, LANES), 1)
    own = jnp.zeros((8, LANES), jnp.float32)
    for p in range(sizes.pages):
        own = jnp.where(page == p, sums[p * 8 : (p + 1) * 8], own)
    result = jnp.zeros(modeled_ref.shape, jnp.float32)
    at_block = iota(modeled_ref.shape, 1)
    each = 8 // sizes.soundings
    for q in range(sizes.states // 8):
        picked = jnp.where(lane == q * sizes.per_page + within, own, 0.0)
        column = jnp.sum(picked, axis=1, keepdims=True)
        for n in range(each):
            values = column[n * sizes.soundings : (n + 1) * sizes.soundings]
            result = jnp.where(at_block == q * each + n, values, result)
    modeled_ref[...] = result

    pairs = [(coefficients(sizes, model, read_ref[...]), feet_ref, 0)]
    second = coefficients(sizes, model, read_second_ref[...])
    for n, ref in enumerate(bases):
        pairs.append((second[:, n * sizes.base : (n + 1) * sizes.base], ref, sizes.notes))
    if rests:
        *rests, read_more_ref = rests
        last = coefficients(sizes, model, read_more_ref[...])
        more = rests[0].shape[0]
        for n, ref in enumerate(rests):
            pairs.append((last[:, n * more : (n + 1) * more], ref, 0))
    half = sizes.part // 2 if sizes.part > LANES else sizes.part
    copies = []
    for n in range(sizes.part // half):
        lanes = slice(n * half, (n + 1) * half)
        terms = sum(
            jnp.dot(each, ref[first:, lanes], preferred_element_type=jnp.float32)
            for each, ref, first in pairs
        )
        grad_ref[:, :, lanes] = terms.reshape(sizes.hours, sizes.tiles, half)
        copies.append(
            pltpu.make_async_copy(grad_ref.at[:, :, lanes], out_ref.at[:, :, lanes], written.at[n])
        )
        copies[-1].start()
    for copy in copies:
        copy.wait()


def shards(footprint, obs_hour, tile_list, tile_row, flux, observed, obs_var):
    sizes = Sizes(
        lax.axis_size("flux"), lax.axis_size("obs"), footprint.shape, flux.shape
    )
    owners, columns, devices, part = sizes.owners, sizes.columns, sizes.devices, sizes.part
    both = ("flux", "obs")
    params = pltpu.CompilerParams(vmem_limit_bytes=VMEM_BYTES)
    me = lax.axis_index("flux") * columns + lax.axis_index("obs")
    at = jnp.stack([me, lax.axis_index("obs"), lax.axis_index("flux")])
    flux = flux.transpose(1, 0, 2)

    first_height = sizes.lane_tiles * sizes.rows + 8
    spill_height = sizes.lane_tiles * sizes.spill + 16
    all_slots = sizes.slots * sizes.per_slot
    group = columns // PACK_STEPS
    tables = (tile_list.T, tile_row, obs_hour.T, observed.T, obs_var.T)
    send, *spills = pl.pallas_call(
        functools.partial(pack_kernel, sizes),
        in_specs=[pl.BlockSpec(memory_space=pltpu.SMEM)]
        + [pl.BlockSpec(memory_space=pltpu.HBM)] * 6,
        out_specs=[pl.BlockSpec(memory_space=pltpu.HBM)] * (1 + columns),
        scratch_shapes=[
            pltpu.VMEM(
                (PACK_STEPS, all_slots // sizes.lags, sizes.lags, group * part), jnp.bfloat16
            ),
            pltpu.VMEM((PACK_STEPS, owners, group, first_height, LANES), jnp.bfloat16),
            pltpu.VMEM((PACK_STEPS, group, spill_height, LANES), jnp.bfloat16),
            pltpu.VMEM((owners, 8, LANES), jnp.float32),
            pltpu.SMEM((owners + 1,), jnp.int32),
        ]
        + [pltpu.SMEM(table.shape, table.dtype) for table in tables]
        + [pltpu.SemaphoreType.DMA((n,)) for n in (5, PACK_STEPS, PACK_STEPS, columns)],
        out_shape=[pltpu.HBM((owners, columns, first_height, LANES), jnp.bfloat16)]
        + [jax.ShapeDtypeStruct((spill_height, LANES), jnp.bfloat16)] * columns,
        compiler_params=pltpu.CompilerParams(vmem_limit_bytes=ALL_VMEM_BYTES),
        name="pack",
    )(
        at,
        *tables,
        footprint.reshape(all_slots // sizes.lags, sizes.lags, columns * part),
    )
    got = lax.all_to_all(
        send.reshape(devices, first_height, LANES), both, split_axis=0, concat_axis=0, tiled=True
    )
    mine = spills[0]
    spills = spills[:1] + [
        lax.ppermute(spills[d], "obs", [(i, i ^ d) for i in range(columns)])
        for d in range(1, columns)
    ]
    second_height = sizes.notes + sizes.second
    base_height, more_height = sizes.notes + sizes.base, sizes.second - sizes.base
    outs = [(base_height, part)] * owners + [(more_height, part)] * owners
    parts = pl.pallas_call(
        functools.partial(regroup_kernel, sizes),
        grid_spec=pltpu.PrefetchScalarGridSpec(
            num_scalar_prefetch=1,
            grid=(owners,),
            in_specs=[pl.BlockSpec((spill_height, LANES), lambda o, at: (0, 0))] * columns,
            out_specs=[pl.BlockSpec(shape, lambda o, at: (0, 0)) for shape in outs],
            scratch_shapes=[
                pltpu.VMEM((columns * sizes.spill, part), jnp.bfloat16),
                pltpu.VMEM((16, columns * sizes.spill), jnp.float32),
                pltpu.VMEM((sizes.second, columns * sizes.spill), jnp.bfloat16),
            ],
        ),
        out_shape=[jax.ShapeDtypeStruct(shape, jnp.bfloat16) for shape in outs],
        compiler_params=params,
        name="regroup",
    )(at, *spills)

    def swap(arrays):
        return arrays[:1] + [
            lax.ppermute(arrays[n], "flux", [(i, i ^ n) for i in range(owners)])
            for n in range(1, owners)
        ]

    parts = list(parts)
    bases, rests = swap(parts[:owners]), parts[owners:]

    sources = min(devices, 1024 // sizes.rows)
    chunks = devices // sources
    copies = devices if devices <= 64 else 1
    height = 8 * sizes.pages
    flux_spec = pl.BlockSpec((sizes.hours, sizes.tiles, part), lambda i, at: (0, 0, at[1]))
    base_specs = [pl.BlockSpec((base_height, part), lambda i, at: (0, 0))] * owners
    early, level, feet_first, read_first = pl.pallas_call(
        functools.partial(forward_first_kernel, sizes),
        grid_spec=pltpu.PrefetchScalarGridSpec(
            num_scalar_prefetch=1,
            grid=(chunks,),
            in_specs=[
                flux_spec,
                pl.BlockSpec((sources, first_height, LANES), lambda i, at: (i, 0, 0)),
                pl.BlockSpec((devices, 8, LANES), lambda i, at: (0, first_height // 8 - 1, 0)),
            ],
            out_specs=(
                pl.BlockSpec((height, LANES), lambda i, at: (0, 0)),
                pl.BlockSpec((8, LANES), lambda i, at: (0, 0)),
                pl.BlockSpec((sources * sizes.rows, part), lambda i, at: (i, 0)),
                pl.BlockSpec((8, sources * sizes.rows), lambda i, at: (0, i)),
            ),
        ),
        out_shape=(
            jax.ShapeDtypeStruct((height, LANES), jnp.float32),
            jax.ShapeDtypeStruct((8, LANES), jnp.int32),
            jax.ShapeDtypeStruct((devices * sizes.rows, part), jnp.bfloat16),
            jax.ShapeDtypeStruct((8, devices * sizes.rows), jnp.float32),
        ),
        compiler_params=params,
        name="forward_first",
    )(at, flux, got, got)

    smem, vmem = pl.BlockSpec(memory_space=pltpu.SMEM), pl.BlockSpec(memory_space=pltpu.VMEM)
    late_flux = lax.optimization_barrier((flux, mine))[0]
    own_flux = lax.dynamic_slice_in_dim(late_flux, lax.axis_index("obs") * part, part, axis=2)

    def forward_second(own_flux, before, bases, rests, more):
        return pl.pallas_call(
            functools.partial(forward_second_kernel, sizes, more > 0),
            in_specs=[smem] + [vmem] * (2 + len(bases) + len(rests)),
            out_specs=(vmem, vmem),
            out_shape=(
                jax.ShapeDtypeStruct((copies, height, LANES), jnp.float32),
                jax.ShapeDtypeStruct((8, owners * (more or sizes.base)), jnp.float32),
            ),
            compiler_params=params,
            name="forward_more" if more else "forward_second",
        )(at, own_flux, before, *bases, *rests)

    sums, read_second = forward_second(own_flux, early[None], bases, [], 0)
    kept = (feet_first, read_first, read_second)

    def finish(sixteenths):
        more = sizes.second * sixteenths // 16

        def run(own_flux, kept, sums, bases, rests, at):
            if more:
                rests = swap([rest[:more] for rest in rests])
                sums, read_more = forward_second(own_flux, sums, bases, rests, more)
                rests.append(read_more)
            else:
                rests = []
            if copies > 1:
                sums = lax.all_to_all(sums, both, split_axis=0, concat_axis=0, tiled=True)
            else:
                sums = lax.psum(sums, both)
            return pl.pallas_call(
                functools.partial(adjoint_kernel, sizes),
                in_specs=[smem] + [vmem] * (4 + len(bases) + len(rests)),
                out_specs=(vmem, pl.BlockSpec(memory_space=pltpu.HBM)),
                out_shape=(
                    jax.ShapeDtypeStruct((sizes.soundings, sizes.blocks), jnp.float32),
                    jax.ShapeDtypeStruct((sizes.hours, sizes.tiles, part), jnp.float32),
                ),
                scratch_shapes=[
                    pltpu.VMEM((sizes.hours, sizes.tiles, part), jnp.float32),
                    pltpu.SemaphoreType.DMA((2,)),
                ],
                compiler_params=params,
                name="adjoint",
            )(at, sums, *kept, *bases, *rests)

        return run

    modeled, gradient = lax.switch(
        level[0, 0], [finish(n) for n in REST], own_flux, kept, sums, bases, rests, at
    )
    return modeled.T, gradient.transpose(1, 0, 2)


def solution(mesh):
    placed = (
        P(("flux", "obs"), None, None, None, None),
        P(("flux", "obs"), None),
        P(("flux", "obs"), None),
        P(),
        P("flux", None, None),
        P(("flux", "obs"), None),
        P(("flux", "obs"), None),
    )
    return jax.shard_map(
        shards,
        mesh=mesh,
        in_specs=placed,
        out_specs=(P(("flux", "obs"), None), P("flux", None, "obs")),
        check_vma=False,
    )
```

```python
import functools

import jax
import jax.numpy as jnp
from jax import lax
from jax.experimental import pallas as pl
from jax.experimental.pallas import tpu as pltpu
from jax.sharding import PartitionSpec as P

LANES = 128
VMEM_BYTES = 48 * 1024 * 1024
ALL_VMEM_BYTES = 60 * 1024 * 1024
BASE = 256
REST = (0, 64, 128)
PACK_STEPS = 2


def iota(shape, dim):
    return lax.broadcasted_iota(jnp.int32, shape, dim)


def thirds(value):
    high = value.astype(jnp.bfloat16).astype(jnp.float32)
    rest = value - high
    middle = rest.astype(jnp.bfloat16).astype(jnp.float32)
    return high, middle, (rest - middle).astype(jnp.bfloat16).astype(jnp.float32)


class Sizes:
    def __init__(self, owners, columns, footprint, flux):
        self.owners, self.columns = owners, columns
        self.devices = owners * columns
        self.blocks, self.width, self.soundings, self.lags, cells = footprint
        self.tiles, self.hours = flux[0], flux[1]
        self.span = self.hours - self.lags + 1
        self.half = self.span * self.tiles // 2
        self.slots = self.blocks * self.width
        self.per_slot = self.soundings * self.lags
        self.part = cells // columns
        self.lane_tiles = self.part // LANES
        capacity = 2 * self.slots // owners
        self.first = capacity // 2 - capacity // 16
        self.rows = self.first * self.per_slot
        self.spill = (self.slots - owners // 2 * self.first) * self.per_slot
        self.spill_notes = -(-self.spill // LANES)
        self.second = columns * (capacity - self.first) * self.per_slot
        self.base = min(BASE, self.second)
        self.rest = self.second - self.base
        self.base_notes = 8 * -(-self.base // self.part)
        self.rest_notes = 8 * -(-self.rest // self.part)
        self.levels = tuple(n for n in REST if n < self.rest) + (self.rest,)
        self.states = self.blocks * self.soundings
        self.per_page = 8 * LANES // self.states
        self.pages = self.devices // self.per_page


def read_notes(sizes, notes, plane):
    lane = iota((1, notes.shape[1]), 1)
    inner = lax.rem(lane, jnp.int32(sizes.per_slot))
    base = notes[0:1]
    target = (base + sizes.half).astype(jnp.int32) + lax.rem(inner, jnp.int32(sizes.lags)) * sizes.tiles
    target = jnp.where(base > sizes.half - 0.5, -1, target)
    place = notes[1:2].astype(jnp.int32)
    block = lax.rem(place, jnp.int32(sizes.blocks))
    device = plane * sizes.columns + lax.div(place, jnp.int32(sizes.blocks))
    state = block * sizes.soundings + lax.div(inner, jnp.int32(sizes.lags))
    row = lax.div(device, jnp.int32(sizes.per_page)) * 8 + lax.rem(state, jnp.int32(8))
    column = lax.div(state, jnp.int32(8)) * sizes.per_page + lax.rem(device, jnp.int32(sizes.per_page))
    seen = notes[2:3] + notes[3:4] + notes[4:5]
    spread = notes[5:6] + notes[6:7] + notes[7:8]
    places = [each.astype(jnp.float32) for each in (target, row, column)]
    return jnp.concatenate(places + [seen, spread, jnp.zeros((3, lane.shape[1]), jnp.float32)], axis=0)


def first_round(sizes, ref, step):
    sources, count = ref.shape[0], sizes.rows
    feet = jnp.concatenate(
        [
            ref[:, n * count : (n + 1) * count, :].reshape(sources * count, LANES)
            for n in range(sizes.lane_tiles)
        ],
        axis=1,
    )
    end = sizes.lane_tiles * count
    notes = jnp.concatenate(
        [ref[s, end : end + 8, :].astype(jnp.float32)[:, :count] for s in range(sources)], axis=1
    )
    lane = iota((1, sources * count), 1)
    plane = lax.div(step * sources + lax.div(lane, jnp.int32(count)), jnp.int32(sizes.columns))
    return feet, notes, plane


def second_round(sizes, flux_index, refs, heights):
    count = refs[0].shape[0] - heights
    notes = [
        jnp.concatenate(
            [ref[n * 8 : (n + 1) * 8, :].astype(jnp.float32) for n in range(heights // 8)], axis=1
        )[:, :count]
        for ref in refs
    ]
    plane = lax.div(iota((1, len(refs) * count), 1), jnp.int32(count))
    feet = jnp.concatenate([ref[heights:, :] for ref in refs], axis=0)
    return feet, jnp.concatenate(notes, axis=1), lax.bitwise_xor(plane, flux_index)


def partial_sums(sizes, flux_ref, feet, read):
    target, row, column = (read[n : n + 1].astype(jnp.int32) for n in range(3))
    count = feet.shape[0]
    levels = sizes.hours * sizes.tiles
    products = lax.dot_general(
        flux_ref[...].reshape(levels, sizes.part),
        feet,
        (((1,), (1,)), ((), ())),
        preferred_element_type=jnp.float32,
    )
    chosen = jnp.where(iota((levels, count), 0) == target, products, 0.0)
    partial = jnp.sum(chosen, axis=0, keepdims=True)
    height = 8 * sizes.pages
    spread = jnp.where(iota((height, count), 0) == row, partial, 0.0)
    terms = jnp.concatenate(thirds(spread), axis=0).astype(jnp.bfloat16)
    lanes = (iota((LANES, count), 0) == column).astype(jnp.bfloat16)
    sums = lax.dot_general(
        terms, lanes, (((1,), (1,)), ((), ())), preferred_element_type=jnp.float32
    )
    return sums[:height] + sums[height : 2 * height] + sums[2 * height :]


def coefficients(sizes, model, read):
    target, row, column = (read[n : n + 1].astype(jnp.int32) for n in range(3))
    count = read.shape[1]
    height = 8 * sizes.pages
    lanes = (iota((LANES, count), 0) == column).astype(jnp.bfloat16)
    taken = jnp.dot(model, lanes, preferred_element_type=jnp.float32)
    taken = taken[:height] + taken[height : 2 * height] + taken[2 * height :]
    value = jnp.sum(
        jnp.where(iota((height, count), 0) == row, taken, 0.0), axis=0, keepdims=True
    )
    scaled = ((value - read[3:4]) / read[4:5]).astype(jnp.bfloat16).astype(jnp.float32)
    levels = sizes.hours * sizes.tiles
    return jnp.where(iota((levels, count), 0) == target, scaled, 0.0).astype(jnp.bfloat16)


def pack_kernel(sizes, at_ref, *refs):
    tables, feet_ref, send_ref = refs[:5], refs[5], refs[6]
    spills = refs[7 : 7 + sizes.columns]
    feet, sent, spilled, first_notes, count, *local = refs[7 + sizes.columns : -4]
    arrived, feet_arrived, sent_done, over_done = refs[-4:]
    list_ref, row_ref, hour_ref, seen_ref, var_ref = local
    owners, per_slot = sizes.owners, sizes.per_slot
    group = sizes.columns // PACK_STEPS
    mine = at_ref[1]
    tables = [
        pltpu.make_async_copy(table, here, arrived.at[n])
        for n, (table, here) in enumerate(zip(tables, local))
    ]
    for copy in tables:
        copy.start()
    firsts = [pl.multiple_of((i ^ (mine // group)) * group, group) for i in range(PACK_STEPS)]
    loads = []
    for i, first in enumerate(firsts):
        lanes = pl.ds(pl.multiple_of(first * sizes.part, LANES), group * sizes.part)
        loads.append(
            pltpu.make_async_copy(feet_ref.at[:, :, lanes], feet.at[i], feet_arrived.at[i])
        )
        loads[-1].start()
    for copy in tables:
        copy.wait()

    field, lane = iota((16, LANES), 0), iota((16, LANES), 1)
    inner = lane % per_slot
    sounding = inner // sizes.lags
    slot_at = lane // per_slot
    key_at = iota((1, sizes.slots * per_slot), 1)
    key = jnp.zeros(key_at.shape, jnp.int32)
    empty = jnp.where(field == 0, jnp.float32(sizes.half), 0.0)
    empty = jnp.where(field == 5, 1.0, jnp.where(field == 8, -1.0, empty))
    for o in range(owners):
        count[o] = 0
        first_notes[o] = empty[:8]
    count[owners] = 0
    lefts = [empty] * sizes.spill_notes
    for b in range(sizes.blocks):
        base = jnp.zeros(field.shape, jnp.float32)
        seen = jnp.zeros(field.shape, jnp.float32)
        spread = jnp.ones(field.shape, jnp.float32)
        for o in range(sizes.soundings):
            here = sounding == o
            hour = hour_ref[o, b] * sizes.tiles - sizes.half
            base = jnp.where(here, hour.astype(jnp.float32), base)
            seen = jnp.where(here, seen_ref[o, b], seen)
            spread = jnp.where(here, var_ref[o, b], spread)
        column = (b + sizes.blocks * at_ref[1]).astype(jnp.float32)
        pattern = jnp.where(field == 0, base, jnp.where(field == 1, column, 0.0))
        for n, term in enumerate(thirds(seen) + thirds(spread)):
            pattern = jnp.where(field == 2 + n, term, pattern)
        for k in range(sizes.width):
            stored = row_ref[list_ref[k, b]]
            owner = lax.div(stored, jnp.int32(sizes.tiles))
            tile = (stored - owner * sizes.tiles).astype(jnp.float32)
            position = count[owner]
            count[owner] = position + 1
            keep = position < sizes.first
            over = count[owners]
            count[owners] = over + jnp.where(keep, 0, 1)
            goes = jnp.where(
                keep, owner * sizes.first + position, owners * sizes.first + over
            )
            value = jnp.where(field == 0, pattern + tile, pattern)
            value = jnp.where(field == 8, owner.astype(jnp.float32), value)
            value = jnp.where(
                field == 9, (position - sizes.first).astype(jnp.float32), value
            )
            first_notes[owner] = jnp.where(
                slot_at[:8] == jnp.where(keep, position, -1), value[:8], first_notes[owner]
            )
            lefts = [
                jnp.where(
                    slot_at + n * (LANES // per_slot) == jnp.where(keep, -1, over), value, left
                )
                for n, left in enumerate(lefts)
            ]
            key = jnp.where(
                key_at // per_slot == b * sizes.width + k,
                goes * per_slot + key_at % per_slot,
                key,
            )
    counts = jnp.zeros((8, LANES), jnp.float32)
    for o in range(owners):
        over = jnp.maximum(count[o] - sizes.first, 0).astype(jnp.float32)
        counts = jnp.where(lane[:8] == sizes.rows + o, over, counts)
    for o in range(owners):
        first_notes[o] = jnp.where(lane[:8] < sizes.rows, first_notes[o], counts)
    place = (iota((owners * sizes.rows + sizes.spill, key.shape[1]), 0) == key).astype(
        jnp.bfloat16
    )
    rows, spill, tiles = sizes.rows, sizes.spill, sizes.lane_tiles
    end = tiles * rows
    stores = []
    for i, first in enumerate(firsts):
        loads[i].wait()
        packed = jnp.dot(
            place,
            feet[i].reshape(key.shape[1], group * sizes.part),
            preferred_element_type=jnp.float32,
        )
        for c in range(group):
            for o in range(owners):
                for n in range(tiles):
                    lanes = slice((c * tiles + n) * LANES, (c * tiles + n + 1) * LANES)
                    sent[i, o, c, n * rows : (n + 1) * rows, :] = packed[
                        o * rows : (o + 1) * rows, lanes
                    ].astype(jnp.bfloat16)
                sent[i, o, c, end : end + 8, :] = first_notes[o].astype(jnp.bfloat16)
            for n in range(tiles):
                lanes = slice((c * tiles + n) * LANES, (c * tiles + n + 1) * LANES)
                spilled[i, c, n * spill : (n + 1) * spill, :] = packed[
                    owners * rows :, lanes
                ].astype(jnp.bfloat16)
            for n, left in enumerate(lefts):
                first_note = tiles * spill + n * 16
                spilled[i, c, first_note : first_note + 16, :] = left.astype(jnp.bfloat16)
        stores.append(
            pltpu.make_async_copy(
                sent.at[i], send_ref.at[:, pl.ds(first, group)], sent_done.at[i]
            )
        )
        stores[-1].start()
        for d in range(i * group, (i + 1) * group):
            stores.append(
                pltpu.make_async_copy(spilled.at[i, (d ^ mine) % group], spills[d], over_done.at[d])
            )
            stores[-1].start()
    for copy in stores:
        copy.wait()


def level_of(sizes, ref):
    planes = [
        sum(
            ref[p * sizes.columns + j].astype(jnp.float32) for j in range(sizes.columns)
        )
        for p in range(sizes.owners)
    ]
    counts = functools.reduce(jnp.maximum, planes)[0:1]
    lane = iota(counts.shape, 1)
    counts = jnp.where((lane >= sizes.rows) & (lane < sizes.rows + sizes.owners), counts, 0.0)
    most = jnp.max(counts, axis=1, keepdims=True) * sizes.per_slot
    level = jnp.zeros((1, 1), jnp.int32)
    for n in sizes.levels[:-1]:
        level = level + jnp.where(most > sizes.base + n, 1, 0)
    return level


def regroup_kernel(sizes, start, count, heights, at_ref, *refs):
    columns, owners, spill = sizes.columns, sizes.owners, sizes.spill
    spills, outs, (feet,) = refs[:columns], refs[columns : columns + owners], refs[-1:]
    end = sizes.lane_tiles * spill
    notes = []
    for d, ref in enumerate(spills):
        for n in range(sizes.lane_tiles):
            feet[d * spill : (d + 1) * spill, n * LANES : (n + 1) * LANES] = ref[
                n * spill : (n + 1) * spill, :
            ]
        blocks = [
            ref[end + n * 16 : end + (n + 1) * 16, :].astype(jnp.float32)
            for n in range(sizes.spill_notes)
        ]
        notes.append(jnp.concatenate(blocks, axis=1)[:, :spill])
    owner_at = jnp.concatenate([each[8:9] for each in notes], axis=0)
    position = jnp.concatenate([each[9:10] for each in notes], axis=0).astype(jnp.int32)
    inner = lax.rem(iota(position.shape, 1), jnp.int32(sizes.per_slot))
    fields = jnp.concatenate([each[0:8] for each in notes], axis=1).astype(jnp.bfloat16)
    for n in range(owners):
        mine = owner_at == (at_ref[2] ^ n).astype(jnp.float32)
        counts = jnp.sum(jnp.where(mine, 1.0, 0.0), axis=1, keepdims=True).astype(jnp.int32)
        keys, total = [], jnp.zeros((1, 1), jnp.int32)
        for d in range(columns):
            row = total + position[d : d + 1] * sizes.per_slot + inner[d : d + 1] - start
            keys.append(jnp.where(mine[d : d + 1], row, -1))
            total = total + counts[d : d + 1]
        key = jnp.concatenate(keys, axis=1)
        place = (iota((count, columns * spill), 0) == key).astype(jnp.bfloat16)
        outs[n][heights:, :] = jnp.dot(
            place, feet[...], preferred_element_type=jnp.float32
        ).astype(jnp.bfloat16)
        moved = lax.dot_general(
            fields, place, (((1,), (1,)), ((), ())), preferred_element_type=jnp.float32
        )
        field, lane = iota(moved.shape, 0), iota(moved.shape, 1)
        empty = jnp.where(field == 0, jnp.float32(sizes.half), jnp.where(field == 5, 1.0, 0.0))
        moved = jnp.where(lane + start < total, moved, empty)
        for m in range(heights // 8):
            lanes = moved[:, m * sizes.part : (m + 1) * sizes.part].astype(jnp.bfloat16)
            outs[n][m * 8 : (m + 1) * 8, : lanes.shape[1]] = lanes


def forward_first_kernel(
    sizes, at_ref, flux_ref, got_ref, all_ref, out_ref, level_ref, feet_ref, read_ref
):
    step = pl.program_id(0)
    feet, notes, plane = first_round(sizes, got_ref, step)
    read = read_notes(sizes, notes, plane)
    feet_ref[...], read_ref[...] = feet, read
    sums = partial_sums(sizes, flux_ref, feet, read)

    @pl.when(step == 0)
    def _():
        out_ref[...] = sums
        level_ref[...] = jnp.broadcast_to(level_of(sizes, all_ref), level_ref.shape)

    @pl.when(step > 0)
    def _():
        out_ref[...] += sums


def forward_second_kernel(sizes, heights, at_ref, flux_ref, before_ref, *refs):
    *parts, out_ref, read_ref = refs
    feet, notes, plane = second_round(sizes, at_ref[2], parts, heights)
    read = read_notes(sizes, notes, plane)
    read_ref[...] = read
    sums = before_ref[0] + partial_sums(sizes, flux_ref, feet, read)
    out_ref[...] = jnp.broadcast_to(sums[None], out_ref.shape)


def adjoint_kernel(sizes, at_ref, sums_ref, feet_ref, read_ref, read_second_ref, *refs):
    bases, rests = refs[: sizes.owners], refs[sizes.owners : -4]
    modeled_ref, out_ref, grad_ref, written = refs[-4:]
    sums = jnp.sum(sums_ref[...], axis=0)
    model = jnp.concatenate(thirds(sums), axis=0).astype(jnp.bfloat16)
    me = at_ref[0]
    page, within = lax.div(me, sizes.per_page), lax.rem(me, sizes.per_page)
    lane = iota((8, LANES), 1)
    own = jnp.zeros((8, LANES), jnp.float32)
    for p in range(sizes.pages):
        own = jnp.where(page == p, sums[p * 8 : (p + 1) * 8], own)
    result = jnp.zeros(modeled_ref.shape, jnp.float32)
    at_block = iota(modeled_ref.shape, 1)
    each = 8 // sizes.soundings
    for q in range(sizes.states // 8):
        picked = jnp.where(lane == q * sizes.per_page + within, own, 0.0)
        column = jnp.sum(picked, axis=1, keepdims=True)
        for n in range(each):
            values = column[n * sizes.soundings : (n + 1) * sizes.soundings]
            result = jnp.where(at_block == q * each + n, values, result)
    modeled_ref[...] = result

    pairs = [(coefficients(sizes, model, read_ref[...]), feet_ref, 0)]
    second = coefficients(sizes, model, read_second_ref[...])
    for n, ref in enumerate(bases):
        pairs.append((second[:, n * sizes.base : (n + 1) * sizes.base], ref, sizes.base_notes))
    if rests:
        *rests, read_more_ref = rests
        last = coefficients(sizes, model, read_more_ref[...])
        more = rests[0].shape[0] - sizes.rest_notes
        for n, ref in enumerate(rests):
            pairs.append((last[:, n * more : (n + 1) * more], ref, sizes.rest_notes))
    half = sizes.part // 2 if sizes.part > LANES else sizes.part
    copies = []
    for n in range(sizes.part // half):
        lanes = slice(n * half, (n + 1) * half)
        terms = sum(
            jnp.dot(each, ref[first:, lanes], preferred_element_type=jnp.float32)
            for each, ref, first in pairs
        )
        grad_ref[:, :, lanes] = terms.reshape(sizes.hours, sizes.tiles, half)
        copies.append(
            pltpu.make_async_copy(grad_ref.at[:, :, lanes], out_ref.at[:, :, lanes], written.at[n])
        )
        copies[-1].start()
    for copy in copies:
        copy.wait()


def shards(footprint, obs_hour, tile_list, tile_row, flux, observed, obs_var):
    sizes = Sizes(
        lax.axis_size("flux"), lax.axis_size("obs"), footprint.shape, flux.shape
    )
    owners, columns, devices, part = sizes.owners, sizes.columns, sizes.devices, sizes.part
    both = ("flux", "obs")
    params = pltpu.CompilerParams(vmem_limit_bytes=VMEM_BYTES)
    me = lax.axis_index("flux") * columns + lax.axis_index("obs")
    at = jnp.stack([me, lax.axis_index("obs"), lax.axis_index("flux")])
    flux = flux.transpose(1, 0, 2)

    first_height = sizes.lane_tiles * sizes.rows + 8
    spill_height = sizes.lane_tiles * sizes.spill + sizes.spill_notes * 16
    all_slots = sizes.slots * sizes.per_slot
    group = columns // PACK_STEPS
    tables = (tile_list.T, tile_row, obs_hour.T, observed.T, obs_var.T)
    send, *spills = pl.pallas_call(
        functools.partial(pack_kernel, sizes),
        in_specs=[pl.BlockSpec(memory_space=pltpu.SMEM)]
        + [pl.BlockSpec(memory_space=pltpu.HBM)] * 6,
        out_specs=[pl.BlockSpec(memory_space=pltpu.HBM)] * (1 + columns),
        scratch_shapes=[
            pltpu.VMEM(
                (PACK_STEPS, all_slots // sizes.lags, sizes.lags, group * part), jnp.bfloat16
            ),
            pltpu.VMEM((PACK_STEPS, owners, group, first_height, LANES), jnp.bfloat16),
            pltpu.VMEM((PACK_STEPS, group, spill_height, LANES), jnp.bfloat16),
            pltpu.VMEM((owners, 8, LANES), jnp.float32),
            pltpu.SMEM((owners + 1,), jnp.int32),
        ]
        + [pltpu.SMEM(table.shape, table.dtype) for table in tables]
        + [pltpu.SemaphoreType.DMA((n,)) for n in (5, PACK_STEPS, PACK_STEPS, columns)],
        out_shape=[pltpu.HBM((owners, columns, first_height, LANES), jnp.bfloat16)]
        + [jax.ShapeDtypeStruct((spill_height, LANES), jnp.bfloat16)] * columns,
        compiler_params=pltpu.CompilerParams(vmem_limit_bytes=ALL_VMEM_BYTES),
        name="pack",
    )(
        at,
        *tables,
        footprint.reshape(all_slots // sizes.lags, sizes.lags, columns * part),
    )
    got = lax.all_to_all(
        send.reshape(devices, first_height, LANES), both, split_axis=0, concat_axis=0, tiled=True
    )
    mine = spills[0]
    spills = spills[:1] + [
        lax.ppermute(spills[d], "obs", [(i, i ^ d) for i in range(columns)])
        for d in range(1, columns)
    ]
    smem, vmem = pl.BlockSpec(memory_space=pltpu.SMEM), pl.BlockSpec(memory_space=pltpu.VMEM)

    def regroup(spills, start, count, heights, name):
        shape = jax.ShapeDtypeStruct((heights + count, part), jnp.bfloat16)
        return pl.pallas_call(
            functools.partial(regroup_kernel, sizes, start, count, heights),
            in_specs=[smem] + [vmem] * columns,
            out_specs=[vmem] * owners,
            out_shape=[shape] * owners,
            scratch_shapes=[pltpu.VMEM((columns * sizes.spill, part), jnp.bfloat16)],
            compiler_params=params,
            name=name,
        )(at, *spills)

    def swap(arrays):
        return arrays[:1] + [
            lax.ppermute(arrays[n], "flux", [(i, i ^ n) for i in range(owners)])
            for n in range(1, owners)
        ]

    bases = swap(list(regroup(spills, 0, sizes.base, sizes.base_notes, "regroup")))

    sources = min(devices, 1 << (1024 // sizes.rows).bit_length() - 1)
    chunks = devices // sources
    copies = devices if devices <= 64 else 1
    height = 8 * sizes.pages
    flux_spec = pl.BlockSpec((sizes.hours, sizes.tiles, part), lambda i, at: (0, 0, at[1]))
    early, level, feet_first, read_first = pl.pallas_call(
        functools.partial(forward_first_kernel, sizes),
        grid_spec=pltpu.PrefetchScalarGridSpec(
            num_scalar_prefetch=1,
            grid=(chunks,),
            in_specs=[
                flux_spec,
                pl.BlockSpec((sources, first_height, LANES), lambda i, at: (i, 0, 0)),
                pl.BlockSpec((devices, 8, LANES), lambda i, at: (0, first_height // 8 - 1, 0)),
            ],
            out_specs=(
                pl.BlockSpec((height, LANES), lambda i, at: (0, 0)),
                pl.BlockSpec((8, LANES), lambda i, at: (0, 0)),
                pl.BlockSpec((sources * sizes.rows, part), lambda i, at: (i, 0)),
                pl.BlockSpec((8, sources * sizes.rows), lambda i, at: (0, i)),
            ),
        ),
        out_shape=(
            jax.ShapeDtypeStruct((height, LANES), jnp.float32),
            jax.ShapeDtypeStruct((8, LANES), jnp.int32),
            jax.ShapeDtypeStruct((devices * sizes.rows, part), jnp.bfloat16),
            jax.ShapeDtypeStruct((8, devices * sizes.rows), jnp.float32),
        ),
        compiler_params=params,
        name="forward_first",
    )(at, flux, got, got)

    late_flux = lax.optimization_barrier((flux, mine))[0]
    own_flux = lax.dynamic_slice_in_dim(late_flux, lax.axis_index("obs") * part, part, axis=2)

    def forward_second(own_flux, before, parts, heights, name):
        return pl.pallas_call(
            functools.partial(forward_second_kernel, sizes, heights),
            in_specs=[smem] + [vmem] * (2 + len(parts)),
            out_specs=(vmem, vmem),
            out_shape=(
                jax.ShapeDtypeStruct((copies, height, LANES), jnp.float32),
                jax.ShapeDtypeStruct((8, owners * (parts[0].shape[0] - heights)), jnp.float32),
            ),
            compiler_params=params,
            name=name,
        )(at, own_flux, before, *parts)

    sums, read_second = forward_second(
        own_flux, early[None], bases, sizes.base_notes, "forward_second"
    )
    late_spills = lax.optimization_barrier((spills, early))[0]
    rests = list(regroup(late_spills, sizes.base, sizes.rest, sizes.rest_notes, "regroup_rest"))
    kept = (feet_first, read_first, read_second)

    def finish(more):
        def run(own_flux, kept, sums, bases, rests, at):
            if more:
                rests = swap([rest[: sizes.rest_notes + more] for rest in rests])
                sums, read_more = forward_second(
                    own_flux, sums, rests, sizes.rest_notes, "forward_more"
                )
                rests.append(read_more)
            else:
                rests = []
            if copies > 1:
                sums = lax.all_to_all(sums, both, split_axis=0, concat_axis=0, tiled=True)
            else:
                sums = lax.psum(sums, both)
            return pl.pallas_call(
                functools.partial(adjoint_kernel, sizes),
                in_specs=[smem] + [vmem] * (4 + len(bases) + len(rests)),
                out_specs=(vmem, pl.BlockSpec(memory_space=pltpu.HBM)),
                out_shape=(
                    jax.ShapeDtypeStruct((sizes.soundings, sizes.blocks), jnp.float32),
                    jax.ShapeDtypeStruct((sizes.hours, sizes.tiles, part), jnp.float32),
                ),
                scratch_shapes=[
                    pltpu.VMEM((sizes.hours, sizes.tiles, part), jnp.float32),
                    pltpu.SemaphoreType.DMA((2,)),
                ],
                compiler_params=params,
                name="adjoint",
            )(at, sums, *kept, *bases, *rests)

        return run

    modeled, gradient = lax.switch(
        level[0, 0], [finish(n) for n in sizes.levels], own_flux, kept, sums, bases, rests, at
    )
    return modeled.T, gradient.transpose(1, 0, 2)


def solution(mesh):
    placed = (
        P(("flux", "obs"), None, None, None, None),
        P(("flux", "obs"), None),
        P(("flux", "obs"), None),
        P(),
        P("flux", None, None),
        P(("flux", "obs"), None),
        P(("flux", "obs"), None),
    )
    return jax.shard_map(
        shards,
        mesh=mesh,
        in_specs=placed,
        out_specs=(P(("flux", "obs"), None), P("flux", None, "obs")),
        check_vma=False,
    )
```

```python
import functools

import jax
import jax.numpy as jnp
from jax import lax
from jax.experimental import pallas as pl
from jax.experimental.pallas import tpu as pltpu
from jax.sharding import PartitionSpec as P

LANES = 128
VMEM_BYTES = 48 * 1024 * 1024
ALL_VMEM_BYTES = 60 * 1024 * 1024
BASE = 256
REST = (0, 64, 128)
PACK_STEPS = 2


def iota(shape, dim):
    return lax.broadcasted_iota(jnp.int32, shape, dim)


def thirds(value):
    high = value.astype(jnp.bfloat16).astype(jnp.float32)
    rest = value - high
    middle = rest.astype(jnp.bfloat16).astype(jnp.float32)
    return high, middle, (rest - middle).astype(jnp.bfloat16).astype(jnp.float32)


class Sizes:
    def __init__(self, owners, columns, footprint, flux):
        self.owners, self.columns = owners, columns
        self.devices = owners * columns
        self.blocks, self.width, self.soundings, self.lags, cells = footprint
        self.tiles, self.hours = flux[0], flux[1]
        self.span = self.hours - self.lags + 1
        self.half = self.span * self.tiles // 2
        self.slots = self.blocks * self.width
        self.per_slot = self.soundings * self.lags
        self.part = cells // columns
        self.lane_tiles = self.part // LANES
        capacity = 2 * self.slots // owners
        self.first = capacity // 2 - capacity // 16
        self.rows = self.first * self.per_slot
        self.spill = (self.slots - owners // 2 * self.first) * self.per_slot
        self.spill_notes = -(-self.spill // LANES)
        self.second = columns * (capacity - self.first) * self.per_slot
        self.base = min(BASE, self.second)
        self.rest = self.second - self.base
        self.base_notes = 8 * -(-self.base // self.part)
        self.rest_notes = 8 * -(-self.rest // self.part)
        self.levels = tuple(n for n in REST if n < self.rest) + (self.rest,)
        self.states = self.blocks * self.soundings
        self.per_page = 8 * LANES // self.states
        self.pages = self.devices // self.per_page


def read_notes(sizes, notes, plane):
    lane = iota((1, notes.shape[1]), 1)
    inner = lax.rem(lane, jnp.int32(sizes.per_slot))
    base = notes[0:1]
    target = (base + sizes.half).astype(jnp.int32) + lax.rem(inner, jnp.int32(sizes.lags)) * sizes.tiles
    target = jnp.where(base > sizes.half - 0.5, -1, target)
    place = notes[1:2].astype(jnp.int32)
    block = lax.rem(place, jnp.int32(sizes.blocks))
    device = plane * sizes.columns + lax.div(place, jnp.int32(sizes.blocks))
    state = block * sizes.soundings + lax.div(inner, jnp.int32(sizes.lags))
    row = lax.div(device, jnp.int32(sizes.per_page)) * 8 + lax.rem(state, jnp.int32(8))
    column = lax.div(state, jnp.int32(8)) * sizes.per_page + lax.rem(device, jnp.int32(sizes.per_page))
    seen = notes[2:3] + notes[3:4] + notes[4:5]
    spread = notes[5:6] + notes[6:7] + notes[7:8]
    places = [each.astype(jnp.float32) for each in (target, row, column)]
    return jnp.concatenate(places + [seen, spread, jnp.zeros((3, lane.shape[1]), jnp.float32)], axis=0)


def first_round(sizes, ref, step):
    sources, count = ref.shape[0], sizes.rows
    feet = jnp.concatenate(
        [
            ref[:, n * count : (n + 1) * count, :].reshape(sources * count, LANES)
            for n in range(sizes.lane_tiles)
        ],
        axis=1,
    )
    end = sizes.lane_tiles * count
    notes = jnp.concatenate(
        [ref[s, end : end + 8, :].astype(jnp.float32)[:, :count] for s in range(sources)], axis=1
    )
    lane = iota((1, sources * count), 1)
    plane = lax.div(step * sources + lax.div(lane, jnp.int32(count)), jnp.int32(sizes.columns))
    return feet, notes, plane


def second_round(sizes, flux_index, refs, first, heights, count):
    notes = [
        jnp.concatenate(
            [ref[n * 8 : (n + 1) * 8, :].astype(jnp.float32) for n in range(heights // 8)], axis=1
        )[:, :count]
        for ref in refs
    ]
    plane = first + lax.div(iota((1, len(refs) * count), 1), jnp.int32(count))
    feet = jnp.concatenate([ref[heights : heights + count, :] for ref in refs], axis=0)
    return feet, jnp.concatenate(notes, axis=1), lax.bitwise_xor(plane, flux_index)


def partial_sums(sizes, flux_ref, feet, read):
    target, row, column = (read[n : n + 1].astype(jnp.int32) for n in range(3))
    count = feet.shape[0]
    levels = sizes.hours * sizes.tiles
    products = lax.dot_general(
        flux_ref[...].reshape(levels, sizes.part),
        feet,
        (((1,), (1,)), ((), ())),
        preferred_element_type=jnp.float32,
    )
    chosen = jnp.where(iota((levels, count), 0) == target, products, 0.0)
    partial = jnp.sum(chosen, axis=0, keepdims=True)
    height = 8 * sizes.pages
    spread = jnp.where(iota((height, count), 0) == row, partial, 0.0)
    terms = jnp.concatenate(thirds(spread), axis=0).astype(jnp.bfloat16)
    lanes = (iota((LANES, count), 0) == column).astype(jnp.bfloat16)
    sums = lax.dot_general(
        terms, lanes, (((1,), (1,)), ((), ())), preferred_element_type=jnp.float32
    )
    return sums[:height] + sums[height : 2 * height] + sums[2 * height :]


def coefficients(sizes, model, read):
    target, row, column = (read[n : n + 1].astype(jnp.int32) for n in range(3))
    count = read.shape[1]
    height = 8 * sizes.pages
    lanes = (iota((LANES, count), 0) == column).astype(jnp.bfloat16)
    taken = jnp.dot(model, lanes, preferred_element_type=jnp.float32)
    taken = taken[:height] + taken[height : 2 * height] + taken[2 * height :]
    value = jnp.sum(
        jnp.where(iota((height, count), 0) == row, taken, 0.0), axis=0, keepdims=True
    )
    scaled = ((value - read[3:4]) / read[4:5]).astype(jnp.bfloat16).astype(jnp.float32)
    levels = sizes.hours * sizes.tiles
    return jnp.where(iota((levels, count), 0) == target, scaled, 0.0).astype(jnp.bfloat16)


def pack_kernel(sizes, at_ref, *refs):
    tables, feet_ref, send_ref = refs[:5], refs[5], refs[6]
    spills = refs[7 : 7 + sizes.columns]
    feet, sent, spilled, first_notes, count, *local = refs[7 + sizes.columns : -4]
    arrived, feet_arrived, sent_done, over_done = refs[-4:]
    list_ref, row_ref, hour_ref, seen_ref, var_ref = local
    owners, per_slot = sizes.owners, sizes.per_slot
    group = sizes.columns // PACK_STEPS
    mine = at_ref[1]
    tables = [
        pltpu.make_async_copy(table, here, arrived.at[n])
        for n, (table, here) in enumerate(zip(tables, local))
    ]
    for copy in tables:
        copy.start()
    firsts = [pl.multiple_of((i ^ (mine // group)) * group, group) for i in range(PACK_STEPS)]
    loads = []
    for i, first in enumerate(firsts):
        lanes = pl.ds(pl.multiple_of(first * sizes.part, LANES), group * sizes.part)
        loads.append(
            pltpu.make_async_copy(feet_ref.at[:, :, lanes], feet.at[i], feet_arrived.at[i])
        )
        loads[-1].start()
    for copy in tables:
        copy.wait()

    field, lane = iota((16, LANES), 0), iota((16, LANES), 1)
    inner = lane % per_slot
    sounding = inner // sizes.lags
    slot_at = lane // per_slot
    key_at = iota((1, sizes.slots * per_slot), 1)
    key = jnp.zeros(key_at.shape, jnp.int32)
    empty = jnp.where(field == 0, jnp.float32(sizes.half), 0.0)
    empty = jnp.where(field == 5, 1.0, jnp.where(field == 8, -1.0, empty))
    for o in range(owners):
        count[o] = 0
        first_notes[o] = empty[:8]
    count[owners] = 0
    lefts = [empty] * sizes.spill_notes
    for b in range(sizes.blocks):
        base = jnp.zeros(field.shape, jnp.float32)
        seen = jnp.zeros(field.shape, jnp.float32)
        spread = jnp.ones(field.shape, jnp.float32)
        for o in range(sizes.soundings):
            here = sounding == o
            hour = hour_ref[o, b] * sizes.tiles - sizes.half
            base = jnp.where(here, hour.astype(jnp.float32), base)
            seen = jnp.where(here, seen_ref[o, b], seen)
            spread = jnp.where(here, var_ref[o, b], spread)
        column = (b + sizes.blocks * at_ref[1]).astype(jnp.float32)
        pattern = jnp.where(field == 0, base, jnp.where(field == 1, column, 0.0))
        for n, term in enumerate(thirds(seen) + thirds(spread)):
            pattern = jnp.where(field == 2 + n, term, pattern)
        for k in range(sizes.width):
            stored = row_ref[list_ref[k, b]]
            owner = lax.div(stored, jnp.int32(sizes.tiles))
            tile = (stored - owner * sizes.tiles).astype(jnp.float32)
            position = count[owner]
            count[owner] = position + 1
            keep = position < sizes.first
            over = count[owners]
            count[owners] = over + jnp.where(keep, 0, 1)
            goes = jnp.where(
                keep, owner * sizes.first + position, owners * sizes.first + over
            )
            value = jnp.where(field == 0, pattern + tile, pattern)
            value = jnp.where(field == 8, owner.astype(jnp.float32), value)
            value = jnp.where(
                field == 9, (position - sizes.first).astype(jnp.float32), value
            )
            first_notes[owner] = jnp.where(
                slot_at[:8] == jnp.where(keep, position, -1), value[:8], first_notes[owner]
            )
            lefts = [
                jnp.where(
                    slot_at + n * (LANES // per_slot) == jnp.where(keep, -1, over), value, left
                )
                for n, left in enumerate(lefts)
            ]
            key = jnp.where(
                key_at // per_slot == b * sizes.width + k,
                goes * per_slot + key_at % per_slot,
                key,
            )
    counts = jnp.zeros((8, LANES), jnp.float32)
    for o in range(owners):
        over = jnp.maximum(count[o] - sizes.first, 0).astype(jnp.float32)
        counts = jnp.where(lane[:8] == sizes.rows + o, over, counts)
    for o in range(owners):
        first_notes[o] = jnp.where(lane[:8] < sizes.rows, first_notes[o], counts)
    place = (iota((owners * sizes.rows + sizes.spill, key.shape[1]), 0) == key).astype(
        jnp.bfloat16
    )
    rows, spill, tiles = sizes.rows, sizes.spill, sizes.lane_tiles
    end = tiles * rows
    stores = []
    for i, first in enumerate(firsts):
        loads[i].wait()
        packed = jnp.dot(
            place,
            feet[i].reshape(key.shape[1], group * sizes.part),
            preferred_element_type=jnp.float32,
        )
        for c in range(group):
            for o in range(owners):
                for n in range(tiles):
                    lanes = slice((c * tiles + n) * LANES, (c * tiles + n + 1) * LANES)
                    sent[i, o, c, n * rows : (n + 1) * rows, :] = packed[
                        o * rows : (o + 1) * rows, lanes
                    ].astype(jnp.bfloat16)
                sent[i, o, c, end : end + 8, :] = first_notes[o].astype(jnp.bfloat16)
            for n in range(tiles):
                lanes = slice((c * tiles + n) * LANES, (c * tiles + n + 1) * LANES)
                spilled[i, c, n * spill : (n + 1) * spill, :] = packed[
                    owners * rows :, lanes
                ].astype(jnp.bfloat16)
            for n, left in enumerate(lefts):
                first_note = tiles * spill + n * 16
                spilled[i, c, first_note : first_note + 16, :] = left.astype(jnp.bfloat16)
        stores.append(
            pltpu.make_async_copy(
                sent.at[i], send_ref.at[:, pl.ds(first, group)], sent_done.at[i]
            )
        )
        stores[-1].start()
        for d in range(i * group, (i + 1) * group):
            stores.append(
                pltpu.make_async_copy(spilled.at[i, (d ^ mine) % group], spills[d], over_done.at[d])
            )
            stores[-1].start()
    for copy in stores:
        copy.wait()


def level_of(sizes, ref):
    planes = [
        sum(
            ref[p * sizes.columns + j].astype(jnp.float32) for j in range(sizes.columns)
        )
        for p in range(sizes.owners)
    ]
    counts = functools.reduce(jnp.maximum, planes)[0:1]
    lane = iota(counts.shape, 1)
    counts = jnp.where((lane >= sizes.rows) & (lane < sizes.rows + sizes.owners), counts, 0.0)
    most = jnp.max(counts, axis=1, keepdims=True) * sizes.per_slot
    level = jnp.zeros((1, 1), jnp.int32)
    for n in sizes.levels[:-1]:
        level = level + jnp.where(most > sizes.base + n, 1, 0)
    return level


def regroup_kernel(sizes, start, count, heights, at_ref, *refs):
    columns, owners, spill = sizes.columns, sizes.owners, sizes.spill
    spills, outs, (feet,) = refs[:columns], refs[columns : columns + owners], refs[-1:]
    end = sizes.lane_tiles * spill
    notes = []
    for d, ref in enumerate(spills):
        for n in range(sizes.lane_tiles):
            feet[d * spill : (d + 1) * spill, n * LANES : (n + 1) * LANES] = ref[
                n * spill : (n + 1) * spill, :
            ]
        blocks = [
            ref[end + n * 16 : end + (n + 1) * 16, :].astype(jnp.float32)
            for n in range(sizes.spill_notes)
        ]
        notes.append(jnp.concatenate(blocks, axis=1)[:, :spill])
    owner_at = jnp.concatenate([each[8:9] for each in notes], axis=0)
    position = jnp.concatenate([each[9:10] for each in notes], axis=0).astype(jnp.int32)
    inner = lax.rem(iota(position.shape, 1), jnp.int32(sizes.per_slot))
    fields = jnp.concatenate([each[0:8] for each in notes], axis=1).astype(jnp.bfloat16)
    for n in range(owners):
        mine = owner_at == (at_ref[2] ^ n).astype(jnp.float32)
        counts = jnp.sum(jnp.where(mine, 1.0, 0.0), axis=1, keepdims=True).astype(jnp.int32)
        keys, total = [], jnp.zeros((1, 1), jnp.int32)
        for d in range(columns):
            row = total + position[d : d + 1] * sizes.per_slot + inner[d : d + 1] - start
            keys.append(jnp.where(mine[d : d + 1], row, -1))
            total = total + counts[d : d + 1]
        key = jnp.concatenate(keys, axis=1)
        place = (iota((count, columns * spill), 0) == key).astype(jnp.bfloat16)
        outs[n][heights:, :] = jnp.dot(
            place, feet[...], preferred_element_type=jnp.float32
        ).astype(jnp.bfloat16)
        moved = lax.dot_general(
            fields, place, (((1,), (1,)), ((), ())), preferred_element_type=jnp.float32
        )
        field, lane = iota(moved.shape, 0), iota(moved.shape, 1)
        empty = jnp.where(field == 0, jnp.float32(sizes.half), jnp.where(field == 5, 1.0, 0.0))
        moved = jnp.where(lane + start < total, moved, empty)
        for m in range(heights // 8):
            lanes = moved[:, m * sizes.part : (m + 1) * sizes.part].astype(jnp.bfloat16)
            outs[n][m * 8 : (m + 1) * 8, : lanes.shape[1]] = lanes


def forward_first_kernel(
    sizes, at_ref, flux_ref, got_ref, all_ref, out_ref, level_ref, feet_ref, read_ref
):
    step = pl.program_id(0)
    feet, notes, plane = first_round(sizes, got_ref, step)
    read = read_notes(sizes, notes, plane)
    feet_ref[...], read_ref[...] = feet, read
    sums = partial_sums(sizes, flux_ref, feet, read)

    @pl.when(step == 0)
    def _():
        out_ref[...] = sums
        level_ref[...] = jnp.broadcast_to(level_of(sizes, all_ref), level_ref.shape)

    @pl.when(step > 0)
    def _():
        out_ref[...] += sums


def forward_second_kernel(sizes, first, heights, count, at_ref, flux_ref, before_ref, *refs):
    *parts, out_ref, read_ref = refs
    feet, notes, plane = second_round(sizes, at_ref[2], parts, first, heights, count)
    read = read_notes(sizes, notes, plane)
    read_ref[...] = read
    sums = before_ref[0] + partial_sums(sizes, flux_ref, feet, read)
    out_ref[...] = jnp.broadcast_to(sums[None], out_ref.shape)


def adjoint_kernel(
    sizes, more, at_ref, sums_ref, feet_ref, read_ref, read_second_ref, read_last_ref, *refs
):
    bases, rests = refs[: sizes.owners], refs[sizes.owners : -4]
    modeled_ref, out_ref, grad_ref, written = refs[-4:]
    sums = jnp.sum(sums_ref[...], axis=0)
    model = jnp.concatenate(thirds(sums), axis=0).astype(jnp.bfloat16)
    me = at_ref[0]
    page, within = lax.div(me, sizes.per_page), lax.rem(me, sizes.per_page)
    lane = iota((8, LANES), 1)
    own = jnp.zeros((8, LANES), jnp.float32)
    for p in range(sizes.pages):
        own = jnp.where(page == p, sums[p * 8 : (p + 1) * 8], own)
    result = jnp.zeros(modeled_ref.shape, jnp.float32)
    at_block = iota(modeled_ref.shape, 1)
    each = 8 // sizes.soundings
    for q in range(sizes.states // 8):
        picked = jnp.where(lane == q * sizes.per_page + within, own, 0.0)
        column = jnp.sum(picked, axis=1, keepdims=True)
        for n in range(each):
            values = column[n * sizes.soundings : (n + 1) * sizes.soundings]
            result = jnp.where(at_block == q * each + n, values, result)
    modeled_ref[...] = result

    pairs = [(coefficients(sizes, model, read_ref[...]), feet_ref, 0, feet_ref.shape[0])]
    reads = jnp.concatenate([read_second_ref[...], read_last_ref[...]], axis=1)
    second = coefficients(sizes, model, reads)
    for n, ref in enumerate(bases):
        pairs.append(
            (second[:, n * sizes.base : (n + 1) * sizes.base], ref, sizes.base_notes, sizes.base)
        )
    if rests:
        *rests, read_more_ref = rests
        last = coefficients(sizes, model, read_more_ref[...])
        for n, ref in enumerate(rests):
            pairs.append((last[:, n * more : (n + 1) * more], ref, sizes.rest_notes, more))
    half = sizes.part // 2 if sizes.part > LANES else sizes.part
    copies = []
    for n in range(sizes.part // half):
        lanes = slice(n * half, (n + 1) * half)
        terms = sum(
            jnp.dot(each, ref[first : first + count, lanes], preferred_element_type=jnp.float32)
            for each, ref, first, count in pairs
        )
        grad_ref[:, :, lanes] = terms.reshape(sizes.hours, sizes.tiles, half)
        copies.append(
            pltpu.make_async_copy(grad_ref.at[:, :, lanes], out_ref.at[:, :, lanes], written.at[n])
        )
        copies[-1].start()
    for copy in copies:
        copy.wait()


def shards(footprint, obs_hour, tile_list, tile_row, flux, observed, obs_var):
    sizes = Sizes(
        lax.axis_size("flux"), lax.axis_size("obs"), footprint.shape, flux.shape
    )
    owners, columns, devices, part = sizes.owners, sizes.columns, sizes.devices, sizes.part
    both = ("flux", "obs")
    params = pltpu.CompilerParams(vmem_limit_bytes=VMEM_BYTES)
    me = lax.axis_index("flux") * columns + lax.axis_index("obs")
    at = jnp.stack([me, lax.axis_index("obs"), lax.axis_index("flux")])
    flux = flux.transpose(1, 0, 2)

    first_height = sizes.lane_tiles * sizes.rows + 8
    spill_height = sizes.lane_tiles * sizes.spill + sizes.spill_notes * 16
    all_slots = sizes.slots * sizes.per_slot
    group = columns // PACK_STEPS
    tables = (tile_list.T, tile_row, obs_hour.T, observed.T, obs_var.T)
    send, *spills = pl.pallas_call(
        functools.partial(pack_kernel, sizes),
        in_specs=[pl.BlockSpec(memory_space=pltpu.SMEM)]
        + [pl.BlockSpec(memory_space=pltpu.HBM)] * 6,
        out_specs=[pl.BlockSpec(memory_space=pltpu.HBM)] * (1 + columns),
        scratch_shapes=[
            pltpu.VMEM(
                (PACK_STEPS, all_slots // sizes.lags, sizes.lags, group * part), jnp.bfloat16
            ),
            pltpu.VMEM((PACK_STEPS, owners, group, first_height, LANES), jnp.bfloat16),
            pltpu.VMEM((PACK_STEPS, group, spill_height, LANES), jnp.bfloat16),
            pltpu.VMEM((owners, 8, LANES), jnp.float32),
            pltpu.SMEM((owners + 1,), jnp.int32),
        ]
        + [pltpu.SMEM(table.shape, table.dtype) for table in tables]
        + [pltpu.SemaphoreType.DMA((n,)) for n in (5, PACK_STEPS, PACK_STEPS, columns)],
        out_shape=[pltpu.HBM((owners, columns, first_height, LANES), jnp.bfloat16)]
        + [jax.ShapeDtypeStruct((spill_height, LANES), jnp.bfloat16)] * columns,
        compiler_params=pltpu.CompilerParams(vmem_limit_bytes=ALL_VMEM_BYTES),
        name="pack",
    )(
        at,
        *tables,
        footprint.reshape(all_slots // sizes.lags, sizes.lags, columns * part),
    )
    got = lax.all_to_all(
        send.reshape(devices, first_height, LANES), both, split_axis=0, concat_axis=0, tiled=True
    )
    mine = spills[0]
    spills = spills[:1] + [
        lax.ppermute(spills[d], "obs", [(i, i ^ d) for i in range(columns)])
        for d in range(1, columns)
    ]
    smem, vmem = pl.BlockSpec(memory_space=pltpu.SMEM), pl.BlockSpec(memory_space=pltpu.VMEM)

    def regroup(spills, start, count, heights, name):
        shape = jax.ShapeDtypeStruct((heights + count, part), jnp.bfloat16)
        return pl.pallas_call(
            functools.partial(regroup_kernel, sizes, start, count, heights),
            in_specs=[smem] + [vmem] * columns,
            out_specs=[vmem] * owners,
            out_shape=[shape] * owners,
            scratch_shapes=[pltpu.VMEM((columns * sizes.spill, part), jnp.bfloat16)],
            compiler_params=params,
            name=name,
        )(at, *spills)

    def swap(arrays):
        return arrays[:1] + [
            lax.ppermute(arrays[n], "flux", [(i, i ^ n) for i in range(owners)])
            for n in range(1, owners)
        ]

    bases = swap(list(regroup(spills, 0, sizes.base, sizes.base_notes, "regroup")))

    sources = min(devices, 1 << (1024 // sizes.rows).bit_length() - 1)
    chunks = devices // sources
    copies = devices if devices <= 64 else 1
    height = 8 * sizes.pages
    flux_spec = pl.BlockSpec((sizes.hours, sizes.tiles, part), lambda i, at: (0, 0, at[1]))
    early, level, feet_first, read_first = pl.pallas_call(
        functools.partial(forward_first_kernel, sizes),
        grid_spec=pltpu.PrefetchScalarGridSpec(
            num_scalar_prefetch=1,
            grid=(chunks,),
            in_specs=[
                flux_spec,
                pl.BlockSpec((sources, first_height, LANES), lambda i, at: (i, 0, 0)),
                pl.BlockSpec((devices, 8, LANES), lambda i, at: (0, first_height // 8 - 1, 0)),
            ],
            out_specs=(
                pl.BlockSpec((height, LANES), lambda i, at: (0, 0)),
                pl.BlockSpec((8, LANES), lambda i, at: (0, 0)),
                pl.BlockSpec((sources * sizes.rows, part), lambda i, at: (i, 0)),
                pl.BlockSpec((8, sources * sizes.rows), lambda i, at: (0, i)),
            ),
        ),
        out_shape=(
            jax.ShapeDtypeStruct((height, LANES), jnp.float32),
            jax.ShapeDtypeStruct((8, LANES), jnp.int32),
            jax.ShapeDtypeStruct((devices * sizes.rows, part), jnp.bfloat16),
            jax.ShapeDtypeStruct((8, devices * sizes.rows), jnp.float32),
        ),
        compiler_params=params,
        name="forward_first",
    )(at, flux, got, got)

    late_flux = lax.optimization_barrier((flux, mine))[0]
    own_flux = lax.dynamic_slice_in_dim(late_flux, lax.axis_index("obs") * part, part, axis=2)

    def forward_second(own_flux, before, parts, first, heights, count, name):
        return pl.pallas_call(
            functools.partial(forward_second_kernel, sizes, first, heights, count),
            in_specs=[smem] + [vmem] * (2 + len(parts)),
            out_specs=(vmem, vmem),
            out_shape=(
                jax.ShapeDtypeStruct((copies, height, LANES), jnp.float32),
                jax.ShapeDtypeStruct((8, len(parts) * count), jnp.float32),
            ),
            compiler_params=params,
            name=name,
        )(at, own_flux, before, *parts)

    late_spills = lax.optimization_barrier((spills, early))[0]
    rests = list(regroup(late_spills, sizes.base, sizes.rest, sizes.rest_notes, "regroup_rest"))

    def follow(more):
        def run(rests):
            height = sizes.rest_notes + more
            moved = swap([rest[:height] for rest in rests])
            return rests[:1] + [
                lax.dynamic_update_slice(rest, part_of, (0, 0))
                for rest, part_of in zip(rests[1:], moved[1:])
            ]

        return run if more else lambda rests: rests

    level = level[0, 0]
    rests = lax.switch(level, [follow(n) for n in sizes.levels], rests)

    reads = []
    sums = early[None]
    for first, end in ((0, owners - 1), (owners - 1, owners)):
        sums, read = forward_second(
            own_flux, sums, bases[first:end], first, sizes.base_notes, sizes.base, "forward_second"
        )
        reads.append(read)
    kept = (feet_first, read_first, *reads)

    def finish(more):
        def run(own_flux, kept, sums, bases, rests, at):
            if more:
                sums, read_more = forward_second(
                    own_flux, sums, rests, 0, sizes.rest_notes, more, "forward_more"
                )
                rests = rests + [read_more]
            else:
                rests = []
            if copies > 1:
                sums = lax.all_to_all(sums, both, split_axis=0, concat_axis=0, tiled=True)
            else:
                sums = lax.psum(sums, both)
            return pl.pallas_call(
                functools.partial(adjoint_kernel, sizes, more),
                in_specs=[smem] + [vmem] * (5 + len(bases) + len(rests)),
                out_specs=(vmem, pl.BlockSpec(memory_space=pltpu.HBM)),
                out_shape=(
                    jax.ShapeDtypeStruct((sizes.soundings, sizes.blocks), jnp.float32),
                    jax.ShapeDtypeStruct((sizes.hours, sizes.tiles, part), jnp.float32),
                ),
                scratch_shapes=[
                    pltpu.VMEM((sizes.hours, sizes.tiles, part), jnp.float32),
                    pltpu.SemaphoreType.DMA((2,)),
                ],
                compiler_params=params,
                name="adjoint",
            )(at, sums, *kept, *bases, *rests)

        return run

    modeled, gradient = lax.switch(
        level, [finish(n) for n in sizes.levels], own_flux, kept, sums, bases, rests, at
    )
    return modeled.T, gradient.transpose(1, 0, 2)


def solution(mesh):
    placed = (
        P(("flux", "obs"), None, None, None, None),
        P(("flux", "obs"), None),
        P(("flux", "obs"), None),
        P(),
        P("flux", None, None),
        P(("flux", "obs"), None),
        P(("flux", "obs"), None),
    )
    return jax.shard_map(
        shards,
        mesh=mesh,
        in_specs=placed,
        out_specs=(P(("flux", "obs"), None), P("flux", None, "obs")),
        check_vma=False,
    )
```

```python
import functools

import jax
import jax.numpy as jnp
from jax import lax
from jax.experimental import pallas as pl
from jax.experimental.pallas import tpu as pltpu
from jax.sharding import PartitionSpec as P

LANES = 128
VMEM_BYTES = 48 * 1024 * 1024
ALL_VMEM_BYTES = 60 * 1024 * 1024
BASE = 256
REST = (0, 64, 128)
PACK_STEPS = 2


def iota(shape, dim):
    return lax.broadcasted_iota(jnp.int32, shape, dim)


def thirds(value):
    high = value.astype(jnp.bfloat16).astype(jnp.float32)
    rest = value - high
    middle = rest.astype(jnp.bfloat16).astype(jnp.float32)
    return high, middle, (rest - middle).astype(jnp.bfloat16).astype(jnp.float32)


class Sizes:
    def __init__(self, owners, columns, footprint, flux):
        self.owners, self.columns = owners, columns
        self.devices = owners * columns
        self.blocks, self.width, self.soundings, self.lags, cells = footprint
        self.tiles, self.hours = flux[0], flux[1]
        self.span = self.hours - self.lags + 1
        self.half = self.span * self.tiles // 2
        self.slots = self.blocks * self.width
        self.per_slot = self.soundings * self.lags
        self.part = cells // columns
        self.lane_tiles = self.part // LANES
        capacity = 2 * self.slots // owners
        self.first = capacity // 2 - capacity // 16
        self.rows = self.first * self.per_slot
        self.spill = (self.slots - owners // 2 * self.first) * self.per_slot
        self.spill_notes = -(-self.spill // LANES)
        self.second = columns * (capacity - self.first) * self.per_slot
        self.base = min(BASE, self.second)
        self.rest = self.second - self.base
        self.base_notes = 8 * -(-self.base // self.part)
        self.rest_notes = 8 * -(-self.rest // self.part)
        self.levels = tuple(n for n in REST if n < self.rest) + (self.rest,)
        self.states = self.blocks * self.soundings
        self.per_page = 8 * LANES // self.states
        self.pages = self.devices // self.per_page


def read_notes(sizes, notes, plane):
    lane = iota((1, notes.shape[1]), 1)
    inner = lax.rem(lane, jnp.int32(sizes.per_slot))
    base = notes[0:1]
    target = (base + sizes.half).astype(jnp.int32) + lax.rem(inner, jnp.int32(sizes.lags)) * sizes.tiles
    target = jnp.where(base > sizes.half - 0.5, -1, target)
    place = notes[1:2].astype(jnp.int32)
    block = lax.rem(place, jnp.int32(sizes.blocks))
    device = plane * sizes.columns + lax.div(place, jnp.int32(sizes.blocks))
    state = block * sizes.soundings + lax.div(inner, jnp.int32(sizes.lags))
    row = lax.div(device, jnp.int32(sizes.per_page)) * 8 + lax.rem(state, jnp.int32(8))
    column = lax.div(state, jnp.int32(8)) * sizes.per_page + lax.rem(device, jnp.int32(sizes.per_page))
    seen = notes[2:3] + notes[3:4] + notes[4:5]
    spread = notes[5:6] + notes[6:7] + notes[7:8]
    places = [each.astype(jnp.float32) for each in (target, row, column)]
    return jnp.concatenate(places + [seen, spread, jnp.zeros((3, lane.shape[1]), jnp.float32)], axis=0)


def first_round(sizes, ref, step):
    sources, count = ref.shape[0], sizes.rows
    feet = jnp.concatenate(
        [
            ref[:, n * count : (n + 1) * count, :].reshape(sources * count, LANES)
            for n in range(sizes.lane_tiles)
        ],
        axis=1,
    )
    end = sizes.lane_tiles * count
    notes = jnp.concatenate(
        [ref[s, end : end + 8, :].astype(jnp.float32)[:, :count] for s in range(sources)], axis=1
    )
    lane = iota((1, sources * count), 1)
    plane = lax.div(step * sources + lax.div(lane, jnp.int32(count)), jnp.int32(sizes.columns))
    return feet, notes, plane


def second_round(sizes, flux_index, refs, first, heights, count):
    notes = [
        jnp.concatenate(
            [ref[n * 8 : (n + 1) * 8, :].astype(jnp.float32) for n in range(heights // 8)], axis=1
        )[:, :count]
        for ref in refs
    ]
    plane = first + lax.div(iota((1, len(refs) * count), 1), jnp.int32(count))
    feet = jnp.concatenate([ref[heights : heights + count, :] for ref in refs], axis=0)
    return feet, jnp.concatenate(notes, axis=1), lax.bitwise_xor(plane, flux_index)


def partial_sums(sizes, flux_ref, feet, read):
    target, row, column = (read[n : n + 1].astype(jnp.int32) for n in range(3))
    count = feet.shape[0]
    levels = sizes.hours * sizes.tiles
    products = lax.dot_general(
        flux_ref[...].reshape(levels, sizes.part),
        feet,
        (((1,), (1,)), ((), ())),
        preferred_element_type=jnp.float32,
    )
    chosen = jnp.where(iota((levels, count), 0) == target, products, 0.0)
    partial = jnp.sum(chosen, axis=0, keepdims=True)
    height = 8 * sizes.pages
    spread = jnp.where(iota((height, count), 0) == row, partial, 0.0)
    terms = jnp.concatenate(thirds(spread), axis=0).astype(jnp.bfloat16)
    lanes = (iota((LANES, count), 0) == column).astype(jnp.bfloat16)
    sums = lax.dot_general(
        terms, lanes, (((1,), (1,)), ((), ())), preferred_element_type=jnp.float32
    )
    return sums[:height] + sums[height : 2 * height] + sums[2 * height :]


def coefficients(sizes, model, read):
    target, row, column = (read[n : n + 1].astype(jnp.int32) for n in range(3))
    count = read.shape[1]
    height = 8 * sizes.pages
    lanes = (iota((LANES, count), 0) == column).astype(jnp.bfloat16)
    taken = jnp.dot(model, lanes, preferred_element_type=jnp.float32)
    taken = taken[:height] + taken[height : 2 * height] + taken[2 * height :]
    value = jnp.sum(
        jnp.where(iota((height, count), 0) == row, taken, 0.0), axis=0, keepdims=True
    )
    scaled = ((value - read[3:4]) / read[4:5]).astype(jnp.bfloat16).astype(jnp.float32)
    levels = sizes.hours * sizes.tiles
    return jnp.where(iota((levels, count), 0) == target, scaled, 0.0).astype(jnp.bfloat16)


def pack_kernel(sizes, at_ref, *refs):
    tables, feet_ref, send_ref = refs[:5], refs[5], refs[6]
    spills = refs[7 : 7 + sizes.columns]
    feet, sent, spilled, first_notes, count, *local = refs[7 + sizes.columns : -4]
    arrived, feet_arrived, sent_done, over_done = refs[-4:]
    list_ref, row_ref, hour_ref, seen_ref, var_ref = local
    owners, per_slot = sizes.owners, sizes.per_slot
    group = sizes.columns // PACK_STEPS
    mine = at_ref[1]
    tables = [
        pltpu.make_async_copy(table, here, arrived.at[n])
        for n, (table, here) in enumerate(zip(tables, local))
    ]
    for copy in tables:
        copy.start()
    firsts = [pl.multiple_of((i ^ (mine // group)) * group, group) for i in range(PACK_STEPS)]
    loads = []
    for i, first in enumerate(firsts):
        lanes = pl.ds(pl.multiple_of(first * sizes.part, LANES), group * sizes.part)
        loads.append(
            pltpu.make_async_copy(feet_ref.at[:, :, lanes], feet.at[i], feet_arrived.at[i])
        )
        loads[-1].start()
    for copy in tables:
        copy.wait()

    field, lane = iota((16, LANES), 0), iota((16, LANES), 1)
    inner = lane % per_slot
    sounding = inner // sizes.lags
    slot_at = lane // per_slot
    key_at = iota((1, sizes.slots * per_slot), 1)
    key = jnp.zeros(key_at.shape, jnp.int32)
    empty = jnp.where(field == 0, jnp.float32(sizes.half), 0.0)
    empty = jnp.where(field == 5, 1.0, jnp.where(field == 8, -1.0, empty))
    for o in range(owners):
        count[o] = 0
        first_notes[o] = empty[:8]
    count[owners] = 0
    lefts = [empty] * sizes.spill_notes
    for b in range(sizes.blocks):
        base = jnp.zeros(field.shape, jnp.float32)
        seen = jnp.zeros(field.shape, jnp.float32)
        spread = jnp.ones(field.shape, jnp.float32)
        for o in range(sizes.soundings):
            here = sounding == o
            hour = hour_ref[o, b] * sizes.tiles - sizes.half
            base = jnp.where(here, hour.astype(jnp.float32), base)
            seen = jnp.where(here, seen_ref[o, b], seen)
            spread = jnp.where(here, var_ref[o, b], spread)
        column = (b + sizes.blocks * at_ref[1]).astype(jnp.float32)
        pattern = jnp.where(field == 0, base, jnp.where(field == 1, column, 0.0))
        for n, term in enumerate(thirds(seen) + thirds(spread)):
            pattern = jnp.where(field == 2 + n, term, pattern)
        for k in range(sizes.width):
            stored = row_ref[list_ref[k, b]]
            owner = lax.div(stored, jnp.int32(sizes.tiles))
            tile = (stored - owner * sizes.tiles).astype(jnp.float32)
            position = count[owner]
            count[owner] = position + 1
            keep = position < sizes.first
            over = count[owners]
            count[owners] = over + jnp.where(keep, 0, 1)
            goes = jnp.where(
                keep, owner * sizes.first + position, owners * sizes.first + over
            )
            value = jnp.where(field == 0, pattern + tile, pattern)
            value = jnp.where(field == 8, owner.astype(jnp.float32), value)
            value = jnp.where(
                field == 9, (position - sizes.first).astype(jnp.float32), value
            )
            first_notes[owner] = jnp.where(
                slot_at[:8] == jnp.where(keep, position, -1), value[:8], first_notes[owner]
            )
            lefts = [
                jnp.where(
                    slot_at + n * (LANES // per_slot) == jnp.where(keep, -1, over), value, left
                )
                for n, left in enumerate(lefts)
            ]
            key = jnp.where(
                key_at // per_slot == b * sizes.width + k,
                goes * per_slot + key_at % per_slot,
                key,
            )
    counts = jnp.zeros((8, LANES), jnp.float32)
    for o in range(owners):
        over = jnp.maximum(count[o] - sizes.first, 0).astype(jnp.float32)
        counts = jnp.where(lane[:8] == sizes.rows + o, over, counts)
    for o in range(owners):
        first_notes[o] = jnp.where(lane[:8] < sizes.rows, first_notes[o], counts)
    place = (iota((owners * sizes.rows + sizes.spill, key.shape[1]), 0) == key).astype(
        jnp.bfloat16
    )
    rows, spill, tiles = sizes.rows, sizes.spill, sizes.lane_tiles
    end = tiles * rows
    stores = []
    for i, first in enumerate(firsts):
        loads[i].wait()
        packed = jnp.dot(
            place,
            feet[i].reshape(key.shape[1], group * sizes.part),
            preferred_element_type=jnp.float32,
        )
        for c in range(group):
            for o in range(owners):
                for n in range(tiles):
                    lanes = slice((c * tiles + n) * LANES, (c * tiles + n + 1) * LANES)
                    sent[i, o, c, n * rows : (n + 1) * rows, :] = packed[
                        o * rows : (o + 1) * rows, lanes
                    ].astype(jnp.bfloat16)
                sent[i, o, c, end : end + 8, :] = first_notes[o].astype(jnp.bfloat16)
            for n in range(tiles):
                lanes = slice((c * tiles + n) * LANES, (c * tiles + n + 1) * LANES)
                spilled[i, c, n * spill : (n + 1) * spill, :] = packed[
                    owners * rows :, lanes
                ].astype(jnp.bfloat16)
            for n, left in enumerate(lefts):
                first_note = tiles * spill + n * 16
                spilled[i, c, first_note : first_note + 16, :] = left.astype(jnp.bfloat16)
        stores.append(
            pltpu.make_async_copy(
                sent.at[i], send_ref.at[:, pl.ds(first, group)], sent_done.at[i]
            )
        )
        stores[-1].start()
        for d in range(i * group, (i + 1) * group):
            stores.append(
                pltpu.make_async_copy(spilled.at[i, (d ^ mine) % group], spills[d], over_done.at[d])
            )
            stores[-1].start()
    for copy in stores:
        copy.wait()


def level_of(sizes, ref):
    planes = [
        sum(
            ref[p * sizes.columns + j].astype(jnp.float32) for j in range(sizes.columns)
        )
        for p in range(sizes.owners)
    ]
    counts = functools.reduce(jnp.maximum, planes)[0:1]
    lane = iota(counts.shape, 1)
    counts = jnp.where((lane >= sizes.rows) & (lane < sizes.rows + sizes.owners), counts, 0.0)
    most = jnp.max(counts, axis=1, keepdims=True) * sizes.per_slot
    level = jnp.zeros((1, 1), jnp.int32)
    for n in sizes.levels[:-1]:
        level = level + jnp.where(most > sizes.base + n, 1, 0)
    return level


def regroup_kernel(sizes, start, count, heights, at_ref, *refs):
    columns, owners, spill = sizes.columns, sizes.owners, sizes.spill
    spills, outs, (feet,) = refs[:columns], refs[columns : columns + owners], refs[-1:]
    end = sizes.lane_tiles * spill
    notes = []
    for d, ref in enumerate(spills):
        for n in range(sizes.lane_tiles):
            feet[d * spill : (d + 1) * spill, n * LANES : (n + 1) * LANES] = ref[
                n * spill : (n + 1) * spill, :
            ]
        blocks = [
            ref[end + n * 16 : end + (n + 1) * 16, :].astype(jnp.float32)
            for n in range(sizes.spill_notes)
        ]
        notes.append(jnp.concatenate(blocks, axis=1)[:, :spill])
    owner_at = jnp.concatenate([each[8:9] for each in notes], axis=0)
    position = jnp.concatenate([each[9:10] for each in notes], axis=0).astype(jnp.int32)
    inner = lax.rem(iota(position.shape, 1), jnp.int32(sizes.per_slot))
    fields = jnp.concatenate([each[0:8] for each in notes], axis=1).astype(jnp.bfloat16)
    for n in range(owners):
        mine = owner_at == (at_ref[2] ^ n).astype(jnp.float32)
        counts = jnp.sum(jnp.where(mine, 1.0, 0.0), axis=1, keepdims=True).astype(jnp.int32)
        keys, total = [], jnp.zeros((1, 1), jnp.int32)
        for d in range(columns):
            row = total + position[d : d + 1] * sizes.per_slot + inner[d : d + 1] - start
            keys.append(jnp.where(mine[d : d + 1], row, -1))
            total = total + counts[d : d + 1]
        key = jnp.concatenate(keys, axis=1)
        place = (iota((count, columns * spill), 0) == key).astype(jnp.bfloat16)
        outs[n][heights:, :] = jnp.dot(
            place, feet[...], preferred_element_type=jnp.float32
        ).astype(jnp.bfloat16)
        moved = lax.dot_general(
            fields, place, (((1,), (1,)), ((), ())), preferred_element_type=jnp.float32
        )
        field, lane = iota(moved.shape, 0), iota(moved.shape, 1)
        empty = jnp.where(field == 0, jnp.float32(sizes.half), jnp.where(field == 5, 1.0, 0.0))
        moved = jnp.where(lane + start < total, moved, empty)
        for m in range(heights // 8):
            lanes = moved[:, m * sizes.part : (m + 1) * sizes.part].astype(jnp.bfloat16)
            outs[n][m * 8 : (m + 1) * 8, : lanes.shape[1]] = lanes


def forward_first_kernel(
    sizes, at_ref, flux_ref, got_ref, all_ref, out_ref, level_ref, feet_ref, read_ref
):
    step = pl.program_id(0)
    feet, notes, plane = first_round(sizes, got_ref, step)
    read = read_notes(sizes, notes, plane)
    feet_ref[...], read_ref[...] = feet, read
    sums = partial_sums(sizes, flux_ref, feet, read)

    @pl.when(step == 0)
    def _():
        out_ref[...] = sums
        level_ref[...] = jnp.broadcast_to(level_of(sizes, all_ref), level_ref.shape)

    @pl.when(step > 0)
    def _():
        out_ref[...] += sums


def forward_second_kernel(sizes, first, heights, count, at_ref, flux_ref, before_ref, *refs):
    *parts, out_ref, read_ref = refs
    feet, notes, plane = second_round(sizes, at_ref[2], parts, first, heights, count)
    read = read_notes(sizes, notes, plane)
    read_ref[...] = read
    sums = before_ref[0] + partial_sums(sizes, flux_ref, feet, read)
    out_ref[...] = jnp.broadcast_to(sums[None], out_ref.shape)


def adjoint_kernel(
    sizes, more, at_ref, sums_ref, feet_ref, read_ref, read_second_ref, read_last_ref, *refs
):
    bases, rests = refs[: sizes.owners], refs[sizes.owners : -4]
    modeled_ref, out_ref, grad_ref, written = refs[-4:]
    sums = jnp.sum(sums_ref[...], axis=0)
    model = jnp.concatenate(thirds(sums), axis=0).astype(jnp.bfloat16)
    me = at_ref[0]
    page, within = lax.div(me, sizes.per_page), lax.rem(me, sizes.per_page)
    lane = iota((8, LANES), 1)
    own = jnp.zeros((8, LANES), jnp.float32)
    for p in range(sizes.pages):
        own = jnp.where(page == p, sums[p * 8 : (p + 1) * 8], own)
    result = jnp.zeros(modeled_ref.shape, jnp.float32)
    at_block = iota(modeled_ref.shape, 1)
    each = 8 // sizes.soundings
    for q in range(sizes.states // 8):
        picked = jnp.where(lane == q * sizes.per_page + within, own, 0.0)
        column = jnp.sum(picked, axis=1, keepdims=True)
        for n in range(each):
            values = column[n * sizes.soundings : (n + 1) * sizes.soundings]
            result = jnp.where(at_block == q * each + n, values, result)
    modeled_ref[...] = result

    pairs = [(coefficients(sizes, model, read_ref[...]), feet_ref, 0, feet_ref.shape[0])]
    reads = jnp.concatenate([read_second_ref[...], read_last_ref[...]], axis=1)
    second = coefficients(sizes, model, reads)
    for n, ref in enumerate(bases):
        pairs.append(
            (second[:, n * sizes.base : (n + 1) * sizes.base], ref, sizes.base_notes, sizes.base)
        )
    if rests:
        *rests, read_more_ref = rests
        last = coefficients(sizes, model, read_more_ref[...])
        for n, ref in enumerate(rests):
            pairs.append((last[:, n * more : (n + 1) * more], ref, sizes.rest_notes, more))
    half = sizes.part // 2 if sizes.part > LANES else sizes.part
    copies = []
    for n in range(sizes.part // half):
        lanes = slice(n * half, (n + 1) * half)
        terms = sum(
            jnp.dot(each, ref[first : first + count, lanes], preferred_element_type=jnp.float32)
            for each, ref, first, count in pairs
        )
        grad_ref[:, :, lanes] = terms.reshape(sizes.hours, sizes.tiles, half)
        copies.append(
            pltpu.make_async_copy(grad_ref.at[:, :, lanes], out_ref.at[:, :, lanes], written.at[n])
        )
        copies[-1].start()
    for copy in copies:
        copy.wait()


def shards(footprint, obs_hour, tile_list, tile_row, flux, observed, obs_var):
    sizes = Sizes(
        lax.axis_size("flux"), lax.axis_size("obs"), footprint.shape, flux.shape
    )
    owners, columns, devices, part = sizes.owners, sizes.columns, sizes.devices, sizes.part
    both = ("flux", "obs")
    params = pltpu.CompilerParams(vmem_limit_bytes=VMEM_BYTES)
    me = lax.axis_index("flux") * columns + lax.axis_index("obs")
    at = jnp.stack([me, lax.axis_index("obs"), lax.axis_index("flux")])
    flux = flux.transpose(1, 0, 2)

    first_height = sizes.lane_tiles * sizes.rows + 8
    spill_height = sizes.lane_tiles * sizes.spill + sizes.spill_notes * 16
    all_slots = sizes.slots * sizes.per_slot
    group = columns // PACK_STEPS
    tables = (tile_list.T, tile_row, obs_hour.T, observed.T, obs_var.T)
    send, *spills = pl.pallas_call(
        functools.partial(pack_kernel, sizes),
        in_specs=[pl.BlockSpec(memory_space=pltpu.SMEM)]
        + [pl.BlockSpec(memory_space=pltpu.HBM)] * 6,
        out_specs=[pl.BlockSpec(memory_space=pltpu.HBM)] * (1 + columns),
        scratch_shapes=[
            pltpu.VMEM(
                (PACK_STEPS, all_slots // sizes.lags, sizes.lags, group * part), jnp.bfloat16
            ),
            pltpu.VMEM((PACK_STEPS, owners, group, first_height, LANES), jnp.bfloat16),
            pltpu.VMEM((PACK_STEPS, group, spill_height, LANES), jnp.bfloat16),
            pltpu.VMEM((owners, 8, LANES), jnp.float32),
            pltpu.SMEM((owners + 1,), jnp.int32),
        ]
        + [pltpu.SMEM(table.shape, table.dtype) for table in tables]
        + [pltpu.SemaphoreType.DMA((n,)) for n in (5, PACK_STEPS, PACK_STEPS, columns)],
        out_shape=[pltpu.HBM((owners, columns, first_height, LANES), jnp.bfloat16)]
        + [jax.ShapeDtypeStruct((spill_height, LANES), jnp.bfloat16)] * columns,
        compiler_params=pltpu.CompilerParams(vmem_limit_bytes=ALL_VMEM_BYTES),
        name="pack",
    )(
        at,
        *tables,
        footprint.reshape(all_slots // sizes.lags, sizes.lags, columns * part),
    )
    got = lax.all_to_all(
        send.reshape(devices, first_height, LANES), both, split_axis=0, concat_axis=0, tiled=True
    )
    mine = spills[0]
    spills = spills[:1] + [
        lax.ppermute(spills[d], "obs", [(i, i ^ d) for i in range(columns)])
        for d in range(1, columns)
    ]
    smem, vmem = pl.BlockSpec(memory_space=pltpu.SMEM), pl.BlockSpec(memory_space=pltpu.VMEM)

    def regroup(spills, start, count, heights, name):
        shape = jax.ShapeDtypeStruct((heights + count, part), jnp.bfloat16)
        return pl.pallas_call(
            functools.partial(regroup_kernel, sizes, start, count, heights),
            in_specs=[smem] + [vmem] * columns,
            out_specs=[vmem] * owners,
            out_shape=[shape] * owners,
            scratch_shapes=[pltpu.VMEM((columns * sizes.spill, part), jnp.bfloat16)],
            compiler_params=params,
            name=name,
        )(at, *spills)

    def swap(arrays):
        return arrays[:1] + [
            lax.ppermute(arrays[n], "flux", [(i, i ^ n) for i in range(owners)])
            for n in range(1, owners)
        ]

    bases = swap(list(regroup(spills, 0, sizes.base, sizes.base_notes, "regroup")))

    sources = min(devices, 1 << (1024 // sizes.rows).bit_length() - 1)
    chunks = devices // sources
    copies = devices if devices <= 64 else 1
    height = 8 * sizes.pages
    flux_spec = pl.BlockSpec((sizes.hours, sizes.tiles, part), lambda i, at: (0, 0, at[1]))
    early, level, feet_first, read_first = pl.pallas_call(
        functools.partial(forward_first_kernel, sizes),
        grid_spec=pltpu.PrefetchScalarGridSpec(
            num_scalar_prefetch=1,
            grid=(chunks,),
            in_specs=[
                flux_spec,
                pl.BlockSpec((sources, first_height, LANES), lambda i, at: (i, 0, 0)),
                pl.BlockSpec((devices, 8, LANES), lambda i, at: (0, first_height // 8 - 1, 0)),
            ],
            out_specs=(
                pl.BlockSpec((height, LANES), lambda i, at: (0, 0)),
                pl.BlockSpec((8, LANES), lambda i, at: (0, 0)),
                pl.BlockSpec((sources * sizes.rows, part), lambda i, at: (i, 0)),
                pl.BlockSpec((8, sources * sizes.rows), lambda i, at: (0, i)),
            ),
        ),
        out_shape=(
            jax.ShapeDtypeStruct((height, LANES), jnp.float32),
            jax.ShapeDtypeStruct((8, LANES), jnp.int32),
            jax.ShapeDtypeStruct((devices * sizes.rows, part), jnp.bfloat16),
            jax.ShapeDtypeStruct((8, devices * sizes.rows), jnp.float32),
        ),
        compiler_params=params,
        name="forward_first",
    )(at, flux, got, got)

    late_flux = lax.optimization_barrier((flux, mine))[0]
    own_flux = lax.dynamic_slice_in_dim(late_flux, lax.axis_index("obs") * part, part, axis=2)

    def forward_second(own_flux, before, parts, first, heights, count, name):
        return pl.pallas_call(
            functools.partial(forward_second_kernel, sizes, first, heights, count),
            in_specs=[smem] + [vmem] * (2 + len(parts)),
            out_specs=(vmem, vmem),
            out_shape=(
                jax.ShapeDtypeStruct((copies, height, LANES), jnp.float32),
                jax.ShapeDtypeStruct((8, len(parts) * count), jnp.float32),
            ),
            compiler_params=params,
            name=name,
        )(at, own_flux, before, *parts)

    late_spills = lax.optimization_barrier((spills, early))[0]
    rests = list(regroup(late_spills, sizes.base, sizes.rest, sizes.rest_notes, "regroup_rest"))

    def follow(more):
        def run(rests):
            height, results, before = sizes.rest_notes + more, rests[:1], ()
            for n in range(1, owners):
                rest = lax.optimization_barrier((rests[n][:height], before))[0]
                before = lax.ppermute(rest, "flux", [(i, i ^ n) for i in range(owners)])
                results.append(lax.dynamic_update_slice(rests[n], before, (0, 0)))
            return results

        return run if more else lambda rests: rests

    level = level[0, 0]
    rests = lax.switch(level, [follow(n) for n in sizes.levels], rests)

    reads = []
    sums = early[None]
    for first, end in ((0, owners - 1), (owners - 1, owners)):
        sums, read = forward_second(
            own_flux, sums, bases[first:end], first, sizes.base_notes, sizes.base, "forward_second"
        )
        reads.append(read)
    kept = (feet_first, read_first, *reads)

    def finish(more):
        def run(own_flux, kept, sums, bases, rests, at):
            if more:
                sums, read_more = forward_second(
                    own_flux, sums, rests, 0, sizes.rest_notes, more, "forward_more"
                )
                rests = rests + [read_more]
            else:
                rests = []
            if copies > 1:
                sums = lax.all_to_all(sums, both, split_axis=0, concat_axis=0, tiled=True)
            else:
                sums = lax.psum(sums, both)
            return pl.pallas_call(
                functools.partial(adjoint_kernel, sizes, more),
                in_specs=[smem] + [vmem] * (5 + len(bases) + len(rests)),
                out_specs=(vmem, pl.BlockSpec(memory_space=pltpu.HBM)),
                out_shape=(
                    jax.ShapeDtypeStruct((sizes.soundings, sizes.blocks), jnp.float32),
                    jax.ShapeDtypeStruct((sizes.hours, sizes.tiles, part), jnp.float32),
                ),
                scratch_shapes=[
                    pltpu.VMEM((sizes.hours, sizes.tiles, part), jnp.float32),
                    pltpu.SemaphoreType.DMA((2,)),
                ],
                compiler_params=params,
                name="adjoint",
            )(at, sums, *kept, *bases, *rests)

        return run

    modeled, gradient = lax.switch(
        level, [finish(n) for n in sizes.levels], own_flux, kept, sums, bases, rests, at
    )
    return modeled.T, gradient.transpose(1, 0, 2)


def solution(mesh):
    placed = (
        P(("flux", "obs"), None, None, None, None),
        P(("flux", "obs"), None),
        P(("flux", "obs"), None),
        P(),
        P("flux", None, None),
        P(("flux", "obs"), None),
        P(("flux", "obs"), None),
    )
    return jax.shard_map(
        shards,
        mesh=mesh,
        in_specs=placed,
        out_specs=(P(("flux", "obs"), None), P("flux", None, "obs")),
        check_vma=False,
    )
```

```python
import functools

import jax
import jax.numpy as jnp
from jax import lax
from jax.experimental import pallas as pl
from jax.experimental.pallas import tpu as pltpu
from jax.sharding import PartitionSpec as P

LANES = 128
VMEM_BYTES = 48 * 1024 * 1024
ALL_VMEM_BYTES = 60 * 1024 * 1024
BASE = 256
REST = (0, 64, 128)
PACK_STEPS = 2


def iota(shape, dim):
    return lax.broadcasted_iota(jnp.int32, shape, dim)


def thirds(value):
    high = value.astype(jnp.bfloat16).astype(jnp.float32)
    rest = value - high
    middle = rest.astype(jnp.bfloat16).astype(jnp.float32)
    return high, middle, (rest - middle).astype(jnp.bfloat16).astype(jnp.float32)


class Sizes:
    def __init__(self, owners, columns, footprint, flux):
        self.owners, self.columns = owners, columns
        self.devices = owners * columns
        self.blocks, self.width, self.soundings, self.lags, cells = footprint
        self.tiles, self.hours = flux[0], flux[1]
        self.span = self.hours - self.lags + 1
        self.half = self.span * self.tiles // 2
        self.slots = self.blocks * self.width
        self.per_slot = self.soundings * self.lags
        self.part = cells // columns
        self.lane_tiles = self.part // LANES
        capacity = 2 * self.slots // owners
        self.first = capacity // 2 - capacity // 16
        self.rows = self.first * self.per_slot
        self.spill = (self.slots - owners // 2 * self.first) * self.per_slot
        self.spill_notes = -(-self.spill // LANES)
        self.second = columns * (capacity - self.first) * self.per_slot
        self.base = min(BASE, self.second)
        self.rest = self.second - self.base
        self.base_notes = 8 * -(-self.base // self.part)
        self.rest_notes = 8 * -(-self.rest // self.part)
        self.levels = tuple(n for n in REST if n < self.rest) + (self.rest,)
        self.states = self.blocks * self.soundings
        self.per_page = 8 * LANES // self.states
        self.pages = self.devices // self.per_page


def read_notes(sizes, notes, plane):
    lane = iota((1, notes.shape[1]), 1)
    inner = lax.rem(lane, jnp.int32(sizes.per_slot))
    base = notes[0:1]
    target = (base + sizes.half).astype(jnp.int32) + lax.rem(inner, jnp.int32(sizes.lags)) * sizes.tiles
    target = jnp.where(base > sizes.half - 0.5, -1, target)
    place = notes[1:2].astype(jnp.int32)
    block = lax.rem(place, jnp.int32(sizes.blocks))
    device = plane * sizes.columns + lax.div(place, jnp.int32(sizes.blocks))
    state = block * sizes.soundings + lax.div(inner, jnp.int32(sizes.lags))
    row = lax.div(device, jnp.int32(sizes.per_page)) * 8 + lax.rem(state, jnp.int32(8))
    column = lax.div(state, jnp.int32(8)) * sizes.per_page + lax.rem(device, jnp.int32(sizes.per_page))
    seen = notes[2:3] + notes[3:4] + notes[4:5]
    spread = notes[5:6] + notes[6:7] + notes[7:8]
    places = [each.astype(jnp.float32) for each in (target, row, column)]
    return jnp.concatenate(places + [seen, spread, jnp.zeros((3, lane.shape[1]), jnp.float32)], axis=0)


def first_round(sizes, ref, step):
    sources, count = ref.shape[0], sizes.rows
    feet = jnp.concatenate(
        [
            ref[:, n * count : (n + 1) * count, :].reshape(sources * count, LANES)
            for n in range(sizes.lane_tiles)
        ],
        axis=1,
    )
    end = sizes.lane_tiles * count
    notes = jnp.concatenate(
        [ref[s, end : end + 8, :].astype(jnp.float32)[:, :count] for s in range(sources)], axis=1
    )
    lane = iota((1, sources * count), 1)
    plane = lax.div(step * sources + lax.div(lane, jnp.int32(count)), jnp.int32(sizes.columns))
    return feet, notes, plane


def second_round(sizes, flux_index, refs, first, heights, count):
    notes = [
        jnp.concatenate(
            [ref[n * 8 : (n + 1) * 8, :].astype(jnp.float32) for n in range(heights // 8)], axis=1
        )[:, :count]
        for ref in refs
    ]
    plane = first + lax.div(iota((1, len(refs) * count), 1), jnp.int32(count))
    feet = jnp.concatenate([ref[heights : heights + count, :] for ref in refs], axis=0)
    return feet, jnp.concatenate(notes, axis=1), lax.bitwise_xor(plane, flux_index)


def partial_sums(sizes, flux_ref, feet, read):
    target, row, column = (read[n : n + 1].astype(jnp.int32) for n in range(3))
    count = feet.shape[0]
    levels = sizes.hours * sizes.tiles
    products = lax.dot_general(
        flux_ref[...].reshape(levels, sizes.part),
        feet,
        (((1,), (1,)), ((), ())),
        preferred_element_type=jnp.float32,
    )
    chosen = jnp.where(iota((levels, count), 0) == target, products, 0.0)
    partial = jnp.sum(chosen, axis=0, keepdims=True)
    height = 8 * sizes.pages
    spread = jnp.where(iota((height, count), 0) == row, partial, 0.0)
    terms = jnp.concatenate(thirds(spread), axis=0).astype(jnp.bfloat16)
    lanes = (iota((LANES, count), 0) == column).astype(jnp.bfloat16)
    sums = lax.dot_general(
        terms, lanes, (((1,), (1,)), ((), ())), preferred_element_type=jnp.float32
    )
    return sums[:height] + sums[height : 2 * height] + sums[2 * height :]


def coefficients(sizes, model, read):
    target, row, column = (read[n : n + 1].astype(jnp.int32) for n in range(3))
    count = read.shape[1]
    height = 8 * sizes.pages
    lanes = (iota((LANES, count), 0) == column).astype(jnp.bfloat16)
    taken = jnp.dot(model, lanes, preferred_element_type=jnp.float32)
    taken = taken[:height] + taken[height : 2 * height] + taken[2 * height :]
    value = jnp.sum(
        jnp.where(iota((height, count), 0) == row, taken, 0.0), axis=0, keepdims=True
    )
    scaled = ((value - read[3:4]) / read[4:5]).astype(jnp.bfloat16).astype(jnp.float32)
    levels = sizes.hours * sizes.tiles
    return jnp.where(iota((levels, count), 0) == target, scaled, 0.0).astype(jnp.bfloat16)


def pack_kernel(sizes, at_ref, *refs):
    tables, feet_ref, send_ref = refs[:5], refs[5], refs[6]
    spills = refs[7 : 7 + sizes.columns]
    feet, sent, spilled, first_notes, count, *local = refs[7 + sizes.columns : -4]
    arrived, feet_arrived, sent_done, over_done = refs[-4:]
    list_ref, row_ref, hour_ref, seen_ref, var_ref = local
    owners, per_slot = sizes.owners, sizes.per_slot
    group = sizes.columns // PACK_STEPS
    mine = at_ref[1]
    tables = [
        pltpu.make_async_copy(table, here, arrived.at[n])
        for n, (table, here) in enumerate(zip(tables, local))
    ]
    for copy in tables:
        copy.start()
    firsts = [pl.multiple_of((i ^ (mine // group)) * group, group) for i in range(PACK_STEPS)]
    loads = []
    for i, first in enumerate(firsts):
        lanes = pl.ds(pl.multiple_of(first * sizes.part, LANES), group * sizes.part)
        loads.append(
            pltpu.make_async_copy(feet_ref.at[:, :, lanes], feet.at[i], feet_arrived.at[i])
        )
        loads[-1].start()
    for copy in tables:
        copy.wait()

    field, lane = iota((16, LANES), 0), iota((16, LANES), 1)
    inner = lane % per_slot
    sounding = inner // sizes.lags
    slot_at = lane // per_slot
    key_at = iota((1, sizes.slots * per_slot), 1)
    key = jnp.zeros(key_at.shape, jnp.int32)
    empty = jnp.where(field == 0, jnp.float32(sizes.half), 0.0)
    empty = jnp.where(field == 5, 1.0, jnp.where(field == 8, -1.0, empty))
    for o in range(owners):
        count[o] = 0
        first_notes[o] = empty[:8]
    count[owners] = 0
    lefts = [empty] * sizes.spill_notes
    for b in range(sizes.blocks):
        base = jnp.zeros(field.shape, jnp.float32)
        seen = jnp.zeros(field.shape, jnp.float32)
        spread = jnp.ones(field.shape, jnp.float32)
        for o in range(sizes.soundings):
            here = sounding == o
            hour = hour_ref[o, b] * sizes.tiles - sizes.half
            base = jnp.where(here, hour.astype(jnp.float32), base)
            seen = jnp.where(here, seen_ref[o, b], seen)
            spread = jnp.where(here, var_ref[o, b], spread)
        column = (b + sizes.blocks * at_ref[1]).astype(jnp.float32)
        pattern = jnp.where(field == 0, base, jnp.where(field == 1, column, 0.0))
        for n, term in enumerate(thirds(seen) + thirds(spread)):
            pattern = jnp.where(field == 2 + n, term, pattern)
        for k in range(sizes.width):
            stored = row_ref[list_ref[k, b]]
            owner = lax.div(stored, jnp.int32(sizes.tiles))
            tile = (stored - owner * sizes.tiles).astype(jnp.float32)
            position = count[owner]
            count[owner] = position + 1
            keep = position < sizes.first
            over = count[owners]
            count[owners] = over + jnp.where(keep, 0, 1)
            goes = jnp.where(
                keep, owner * sizes.first + position, owners * sizes.first + over
            )
            value = jnp.where(field == 0, pattern + tile, pattern)
            value = jnp.where(field == 8, owner.astype(jnp.float32), value)
            value = jnp.where(
                field == 9, (position - sizes.first).astype(jnp.float32), value
            )
            first_notes[owner] = jnp.where(
                slot_at[:8] == jnp.where(keep, position, -1), value[:8], first_notes[owner]
            )
            lefts = [
                jnp.where(
                    slot_at + n * (LANES // per_slot) == jnp.where(keep, -1, over), value, left
                )
                for n, left in enumerate(lefts)
            ]
            key = jnp.where(
                key_at // per_slot == b * sizes.width + k,
                goes * per_slot + key_at % per_slot,
                key,
            )
    counts = jnp.zeros((8, LANES), jnp.float32)
    for o in range(owners):
        over = jnp.maximum(count[o] - sizes.first, 0).astype(jnp.float32)
        counts = jnp.where(lane[:8] == sizes.rows + o, over, counts)
    for o in range(owners):
        first_notes[o] = jnp.where(lane[:8] < sizes.rows, first_notes[o], counts)
    place = (iota((owners * sizes.rows + sizes.spill, key.shape[1]), 0) == key).astype(
        jnp.bfloat16
    )
    rows, spill, tiles = sizes.rows, sizes.spill, sizes.lane_tiles
    end = tiles * rows
    stores = []
    for i, first in enumerate(firsts):
        loads[i].wait()
        packed = jnp.dot(
            place,
            feet[i].reshape(key.shape[1], group * sizes.part),
            preferred_element_type=jnp.float32,
        )
        for c in range(group):
            for o in range(owners):
                for n in range(tiles):
                    lanes = slice((c * tiles + n) * LANES, (c * tiles + n + 1) * LANES)
                    sent[i, o, c, n * rows : (n + 1) * rows, :] = packed[
                        o * rows : (o + 1) * rows, lanes
                    ].astype(jnp.bfloat16)
                sent[i, o, c, end : end + 8, :] = first_notes[o].astype(jnp.bfloat16)
            for n in range(tiles):
                lanes = slice((c * tiles + n) * LANES, (c * tiles + n + 1) * LANES)
                spilled[i, c, n * spill : (n + 1) * spill, :] = packed[
                    owners * rows :, lanes
                ].astype(jnp.bfloat16)
            for n, left in enumerate(lefts):
                first_note = tiles * spill + n * 16
                spilled[i, c, first_note : first_note + 16, :] = left.astype(jnp.bfloat16)
        stores.append(
            pltpu.make_async_copy(
                sent.at[i], send_ref.at[:, pl.ds(first, group)], sent_done.at[i]
            )
        )
        stores[-1].start()
        for d in range(i * group, (i + 1) * group):
            stores.append(
                pltpu.make_async_copy(spilled.at[i, (d ^ mine) % group], spills[d], over_done.at[d])
            )
            stores[-1].start()
    for copy in stores:
        copy.wait()


def level_of(sizes, ref):
    planes = [
        sum(
            ref[p * sizes.columns + j].astype(jnp.float32) for j in range(sizes.columns)
        )
        for p in range(sizes.owners)
    ]
    counts = functools.reduce(jnp.maximum, planes)[0:1]
    lane = iota(counts.shape, 1)
    counts = jnp.where((lane >= sizes.rows) & (lane < sizes.rows + sizes.owners), counts, 0.0)
    most = jnp.max(counts, axis=1, keepdims=True) * sizes.per_slot
    level = jnp.zeros((1, 1), jnp.int32)
    for n in sizes.levels[:-1]:
        level = level + jnp.where(most > sizes.base + n, 1, 0)
    return level


def regroup_kernel(sizes, start, count, heights, at_ref, *refs):
    columns, owners, spill = sizes.columns, sizes.owners, sizes.spill
    spills, outs, (feet,) = refs[:columns], refs[columns : columns + owners], refs[-1:]
    end = sizes.lane_tiles * spill
    notes = []
    for d, ref in enumerate(spills):
        for n in range(sizes.lane_tiles):
            feet[d * spill : (d + 1) * spill, n * LANES : (n + 1) * LANES] = ref[
                n * spill : (n + 1) * spill, :
            ]
        blocks = [
            ref[end + n * 16 : end + (n + 1) * 16, :].astype(jnp.float32)
            for n in range(sizes.spill_notes)
        ]
        notes.append(jnp.concatenate(blocks, axis=1)[:, :spill])
    owner_at = jnp.concatenate([each[8:9] for each in notes], axis=0)
    position = jnp.concatenate([each[9:10] for each in notes], axis=0).astype(jnp.int32)
    inner = lax.rem(iota(position.shape, 1), jnp.int32(sizes.per_slot))
    fields = jnp.concatenate([each[0:8] for each in notes], axis=1).astype(jnp.bfloat16)
    for n in range(owners):
        mine = owner_at == (at_ref[2] ^ n).astype(jnp.float32)
        counts = jnp.sum(jnp.where(mine, 1.0, 0.0), axis=1, keepdims=True).astype(jnp.int32)
        keys, total = [], jnp.zeros((1, 1), jnp.int32)
        for d in range(columns):
            row = total + position[d : d + 1] * sizes.per_slot + inner[d : d + 1] - start
            keys.append(jnp.where(mine[d : d + 1], row, -1))
            total = total + counts[d : d + 1]
        key = jnp.concatenate(keys, axis=1)
        place = (iota((count, columns * spill), 0) == key).astype(jnp.bfloat16)
        outs[n][heights:, :] = jnp.dot(
            place, feet[...], preferred_element_type=jnp.float32
        ).astype(jnp.bfloat16)
        moved = lax.dot_general(
            fields, place, (((1,), (1,)), ((), ())), preferred_element_type=jnp.float32
        )
        field, lane = iota(moved.shape, 0), iota(moved.shape, 1)
        empty = jnp.where(field == 0, jnp.float32(sizes.half), jnp.where(field == 5, 1.0, 0.0))
        moved = jnp.where(lane + start < total, moved, empty)
        for m in range(heights // 8):
            lanes = moved[:, m * sizes.part : (m + 1) * sizes.part].astype(jnp.bfloat16)
            outs[n][m * 8 : (m + 1) * 8, : lanes.shape[1]] = lanes


def forward_first_kernel(
    sizes, at_ref, flux_ref, got_ref, all_ref, out_ref, level_ref, feet_ref, read_ref
):
    step = pl.program_id(0)
    feet, notes, plane = first_round(sizes, got_ref, step)
    read = read_notes(sizes, notes, plane)
    feet_ref[...], read_ref[...] = feet, read
    sums = partial_sums(sizes, flux_ref, feet, read)

    @pl.when(step == 0)
    def _():
        out_ref[...] = sums
        level_ref[...] = jnp.broadcast_to(level_of(sizes, all_ref), level_ref.shape)

    @pl.when(step > 0)
    def _():
        out_ref[...] += sums


def forward_second_kernel(sizes, first, heights, count, at_ref, flux_ref, before_ref, *refs):
    *parts, out_ref, read_ref = refs
    feet, notes, plane = second_round(sizes, at_ref[2], parts, first, heights, count)
    read = read_notes(sizes, notes, plane)
    read_ref[...] = read
    sums = before_ref[0] + partial_sums(sizes, flux_ref, feet, read)
    out_ref[...] = jnp.broadcast_to(sums[None], out_ref.shape)


def adjoint_kernel(
    sizes, more, at_ref, sums_ref, feet_ref, read_ref, read_second_ref, read_last_ref, *refs
):
    bases, rests = refs[: sizes.owners], refs[sizes.owners : -4]
    modeled_ref, out_ref, grad_ref, written = refs[-4:]
    sums = jnp.sum(sums_ref[...], axis=0)
    model = jnp.concatenate(thirds(sums), axis=0).astype(jnp.bfloat16)
    me = at_ref[0]
    page, within = lax.div(me, sizes.per_page), lax.rem(me, sizes.per_page)
    lane = iota((8, LANES), 1)
    own = jnp.zeros((8, LANES), jnp.float32)
    for p in range(sizes.pages):
        own = jnp.where(page == p, sums[p * 8 : (p + 1) * 8], own)
    result = jnp.zeros(modeled_ref.shape, jnp.float32)
    at_block = iota(modeled_ref.shape, 1)
    each = 8 // sizes.soundings
    for q in range(sizes.states // 8):
        picked = jnp.where(lane == q * sizes.per_page + within, own, 0.0)
        column = jnp.sum(picked, axis=1, keepdims=True)
        for n in range(each):
            values = column[n * sizes.soundings : (n + 1) * sizes.soundings]
            result = jnp.where(at_block == q * each + n, values, result)
    modeled_ref[...] = result

    pairs = [(coefficients(sizes, model, read_ref[...]), feet_ref, 0, feet_ref.shape[0])]
    reads = jnp.concatenate([read_second_ref[...], read_last_ref[...]], axis=1)
    second = coefficients(sizes, model, reads)
    for n, ref in enumerate(bases):
        pairs.append(
            (second[:, n * sizes.base : (n + 1) * sizes.base], ref, sizes.base_notes, sizes.base)
        )
    if rests:
        *rests, read_more_ref = rests
        last = coefficients(sizes, model, read_more_ref[...])
        for n, ref in enumerate(rests):
            pairs.append((last[:, n * more : (n + 1) * more], ref, sizes.rest_notes, more))
    half = sizes.part // 2 if sizes.part > LANES else sizes.part
    copies = []
    for n in range(sizes.part // half):
        lanes = slice(n * half, (n + 1) * half)
        terms = sum(
            jnp.dot(each, ref[first : first + count, lanes], preferred_element_type=jnp.float32)
            for each, ref, first, count in pairs
        )
        grad_ref[:, :, lanes] = terms.reshape(sizes.hours, sizes.tiles, half)
        copies.append(
            pltpu.make_async_copy(grad_ref.at[:, :, lanes], out_ref.at[:, :, lanes], written.at[n])
        )
        copies[-1].start()
    for copy in copies:
        copy.wait()


def shards(footprint, obs_hour, tile_list, tile_row, flux, observed, obs_var):
    sizes = Sizes(
        lax.axis_size("flux"), lax.axis_size("obs"), footprint.shape, flux.shape
    )
    owners, columns, devices, part = sizes.owners, sizes.columns, sizes.devices, sizes.part
    both = ("flux", "obs")
    params = pltpu.CompilerParams(vmem_limit_bytes=VMEM_BYTES)
    me = lax.axis_index("flux") * columns + lax.axis_index("obs")
    at = jnp.stack([me, lax.axis_index("obs"), lax.axis_index("flux")])
    flux = flux.transpose(1, 0, 2)

    first_height = sizes.lane_tiles * sizes.rows + 8
    spill_height = sizes.lane_tiles * sizes.spill + sizes.spill_notes * 16
    all_slots = sizes.slots * sizes.per_slot
    group = columns // PACK_STEPS
    tables = (tile_list.T, tile_row, obs_hour.T, observed.T, obs_var.T)
    send, *spills = pl.pallas_call(
        functools.partial(pack_kernel, sizes),
        in_specs=[pl.BlockSpec(memory_space=pltpu.SMEM)]
        + [pl.BlockSpec(memory_space=pltpu.HBM)] * 6,
        out_specs=[pl.BlockSpec(memory_space=pltpu.HBM)] * (1 + columns),
        scratch_shapes=[
            pltpu.VMEM(
                (PACK_STEPS, all_slots // sizes.lags, sizes.lags, group * part), jnp.bfloat16
            ),
            pltpu.VMEM((PACK_STEPS, owners, group, first_height, LANES), jnp.bfloat16),
            pltpu.VMEM((PACK_STEPS, group, spill_height, LANES), jnp.bfloat16),
            pltpu.VMEM((owners, 8, LANES), jnp.float32),
            pltpu.SMEM((owners + 1,), jnp.int32),
        ]
        + [pltpu.SMEM(table.shape, table.dtype) for table in tables]
        + [pltpu.SemaphoreType.DMA((n,)) for n in (5, PACK_STEPS, PACK_STEPS, columns)],
        out_shape=[pltpu.HBM((owners, columns, first_height, LANES), jnp.bfloat16)]
        + [jax.ShapeDtypeStruct((spill_height, LANES), jnp.bfloat16)] * columns,
        compiler_params=pltpu.CompilerParams(vmem_limit_bytes=ALL_VMEM_BYTES),
        name="pack",
    )(
        at,
        *tables,
        footprint.reshape(all_slots // sizes.lags, sizes.lags, columns * part),
    )
    got = lax.all_to_all(
        send.reshape(devices, first_height, LANES), both, split_axis=0, concat_axis=0, tiled=True
    )
    mine = spills[0]
    spills = spills[:1] + [
        lax.ppermute(spills[d], "obs", [(i, i ^ d) for i in range(columns)])
        for d in range(1, columns)
    ]
    smem, vmem = pl.BlockSpec(memory_space=pltpu.SMEM), pl.BlockSpec(memory_space=pltpu.VMEM)

    def regroup(spills, start, count, heights, name):
        shape = jax.ShapeDtypeStruct((heights + count, part), jnp.bfloat16)
        return pl.pallas_call(
            functools.partial(regroup_kernel, sizes, start, count, heights),
            in_specs=[smem] + [vmem] * columns,
            out_specs=[vmem] * owners,
            out_shape=[shape] * owners,
            scratch_shapes=[pltpu.VMEM((columns * sizes.spill, part), jnp.bfloat16)],
            compiler_params=params,
            name=name,
        )(at, *spills)

    def swap(arrays):
        return arrays[:1] + [
            lax.ppermute(arrays[n], "flux", [(i, i ^ n) for i in range(owners)])
            for n in range(1, owners)
        ]

    bases = swap(list(regroup(spills, 0, sizes.base, sizes.base_notes, "regroup")))

    sources = min(devices, 1 << (1024 // sizes.rows).bit_length() - 1)
    chunks = devices // sources
    copies = devices if devices <= 64 else 1
    height = 8 * sizes.pages
    flux_spec = pl.BlockSpec((sizes.hours, sizes.tiles, part), lambda i, at: (0, 0, at[1]))
    early, level, feet_first, read_first = pl.pallas_call(
        functools.partial(forward_first_kernel, sizes),
        grid_spec=pltpu.PrefetchScalarGridSpec(
            num_scalar_prefetch=1,
            grid=(chunks,),
            in_specs=[
                flux_spec,
                pl.BlockSpec((sources, first_height, LANES), lambda i, at: (i, 0, 0)),
                pl.BlockSpec((devices, 8, LANES), lambda i, at: (0, first_height // 8 - 1, 0)),
            ],
            out_specs=(
                pl.BlockSpec((height, LANES), lambda i, at: (0, 0)),
                pl.BlockSpec((8, LANES), lambda i, at: (0, 0)),
                pl.BlockSpec((sources * sizes.rows, part), lambda i, at: (i, 0)),
                pl.BlockSpec((8, sources * sizes.rows), lambda i, at: (0, i)),
            ),
        ),
        out_shape=(
            jax.ShapeDtypeStruct((height, LANES), jnp.float32),
            jax.ShapeDtypeStruct((8, LANES), jnp.int32),
            jax.ShapeDtypeStruct((devices * sizes.rows, part), jnp.bfloat16),
            jax.ShapeDtypeStruct((8, devices * sizes.rows), jnp.float32),
        ),
        compiler_params=params,
        name="forward_first",
    )(at, flux, got, got)

    late_flux = lax.optimization_barrier((flux, mine))[0]
    own_flux = lax.dynamic_slice_in_dim(late_flux, lax.axis_index("obs") * part, part, axis=2)

    def forward_second(own_flux, before, parts, first, heights, count, name):
        return pl.pallas_call(
            functools.partial(forward_second_kernel, sizes, first, heights, count),
            in_specs=[smem] + [vmem] * (2 + len(parts)),
            out_specs=(vmem, vmem),
            out_shape=(
                jax.ShapeDtypeStruct((copies, height, LANES), jnp.float32),
                jax.ShapeDtypeStruct((8, len(parts) * count), jnp.float32),
            ),
            compiler_params=params,
            name=name,
        )(at, own_flux, before, *parts)

    late_spills = lax.optimization_barrier((spills, early))[0]
    rests = list(regroup(late_spills, sizes.base, sizes.rest, sizes.rest_notes, "regroup_rest"))

    level = level[0, 0]

    sums, read_second = forward_second(
        own_flux, early[None], bases[:-1], 0, sizes.base_notes, sizes.base, "forward_second"
    )
    kept = (feet_first, read_first, read_second)

    def finish(more):
        def run(own_flux, kept, sums, bases, rests, at):
            if more:
                rests = swap([rest[: sizes.rest_notes + more] for rest in rests])
            sums, read_last = forward_second(
                own_flux, sums, bases[-1:], owners - 1, sizes.base_notes, sizes.base, "forward_last"
            )
            if more:
                sums, read_more = forward_second(
                    own_flux, sums, rests, 0, sizes.rest_notes, more, "forward_more"
                )
                rests = rests + [read_more]
            else:
                rests = []
            if copies > 1:
                sums = lax.all_to_all(sums, both, split_axis=0, concat_axis=0, tiled=True)
            else:
                sums = lax.psum(sums, both)
            return pl.pallas_call(
                functools.partial(adjoint_kernel, sizes, more),
                in_specs=[smem] + [vmem] * (5 + len(bases) + len(rests)),
                out_specs=(vmem, pl.BlockSpec(memory_space=pltpu.HBM)),
                out_shape=(
                    jax.ShapeDtypeStruct((sizes.soundings, sizes.blocks), jnp.float32),
                    jax.ShapeDtypeStruct((sizes.hours, sizes.tiles, part), jnp.float32),
                ),
                scratch_shapes=[
                    pltpu.VMEM((sizes.hours, sizes.tiles, part), jnp.float32),
                    pltpu.SemaphoreType.DMA((2,)),
                ],
                compiler_params=params,
                name="adjoint",
            )(at, sums, *kept, read_last, *bases, *rests)

        return run

    modeled, gradient = lax.switch(
        level, [finish(n) for n in sizes.levels], own_flux, kept, sums, bases, rests, at
    )
    return modeled.T, gradient.transpose(1, 0, 2)


def solution(mesh):
    placed = (
        P(("flux", "obs"), None, None, None, None),
        P(("flux", "obs"), None),
        P(("flux", "obs"), None),
        P(),
        P("flux", None, None),
        P(("flux", "obs"), None),
        P(("flux", "obs"), None),
    )
    return jax.shard_map(
        shards,
        mesh=mesh,
        in_specs=placed,
        out_specs=(P(("flux", "obs"), None), P("flux", None, "obs")),
        check_vma=False,
    )
```

```python
import functools

import jax
import jax.numpy as jnp
from jax import lax
from jax.experimental import pallas as pl
from jax.experimental.pallas import tpu as pltpu
from jax.sharding import PartitionSpec as P

LANES = 128
VMEM_BYTES = 48 * 1024 * 1024
ALL_VMEM_BYTES = 60 * 1024 * 1024
BASE = 240
REST = (0, 64, 128)
PACK_STEPS = 2


def iota(shape, dim):
    return lax.broadcasted_iota(jnp.int32, shape, dim)


def thirds(value):
    high = value.astype(jnp.bfloat16).astype(jnp.float32)
    rest = value - high
    middle = rest.astype(jnp.bfloat16).astype(jnp.float32)
    return high, middle, (rest - middle).astype(jnp.bfloat16).astype(jnp.float32)


class Sizes:
    def __init__(self, owners, columns, footprint, flux):
        self.owners, self.columns = owners, columns
        self.devices = owners * columns
        self.blocks, self.width, self.soundings, self.lags, cells = footprint
        self.tiles, self.hours = flux[0], flux[1]
        self.span = self.hours - self.lags + 1
        self.half = self.span * self.tiles // 2
        self.slots = self.blocks * self.width
        self.per_slot = self.soundings * self.lags
        self.part = cells // columns
        self.lane_tiles = self.part // LANES
        capacity = 2 * self.slots // owners
        self.first = capacity // 2 - capacity // 16
        self.rows = self.first * self.per_slot
        self.spill = (self.slots - owners // 2 * self.first) * self.per_slot
        self.spill_notes = -(-self.spill // LANES)
        self.second = columns * (capacity - self.first) * self.per_slot
        self.base = min(BASE, self.second)
        self.rest = self.second - self.base
        self.base_notes = 8 * -(-self.base // self.part)
        self.rest_notes = 8 * -(-self.rest // self.part)
        self.levels = tuple(n for n in REST if n < self.rest) + (self.rest,)
        self.states = self.blocks * self.soundings
        self.per_page = 8 * LANES // self.states
        self.pages = self.devices // self.per_page


def read_notes(sizes, notes, plane):
    lane = iota((1, notes.shape[1]), 1)
    inner = lax.rem(lane, jnp.int32(sizes.per_slot))
    base = notes[0:1]
    target = (base + sizes.half).astype(jnp.int32) + lax.rem(inner, jnp.int32(sizes.lags)) * sizes.tiles
    target = jnp.where(base > sizes.half - 0.5, -1, target)
    place = notes[1:2].astype(jnp.int32)
    block = lax.rem(place, jnp.int32(sizes.blocks))
    device = plane * sizes.columns + lax.div(place, jnp.int32(sizes.blocks))
    state = block * sizes.soundings + lax.div(inner, jnp.int32(sizes.lags))
    row = lax.div(device, jnp.int32(sizes.per_page)) * 8 + lax.rem(state, jnp.int32(8))
    column = lax.div(state, jnp.int32(8)) * sizes.per_page + lax.rem(device, jnp.int32(sizes.per_page))
    seen = notes[2:3] + notes[3:4] + notes[4:5]
    spread = notes[5:6] + notes[6:7] + notes[7:8]
    places = [each.astype(jnp.float32) for each in (target, row, column)]
    return jnp.concatenate(places + [seen, spread, jnp.zeros((3, lane.shape[1]), jnp.float32)], axis=0)


def first_round(sizes, ref, step):
    sources, count = ref.shape[0], sizes.rows
    feet = jnp.concatenate(
        [
            ref[:, n * count : (n + 1) * count, :].reshape(sources * count, LANES)
            for n in range(sizes.lane_tiles)
        ],
        axis=1,
    )
    end = sizes.lane_tiles * count
    notes = jnp.concatenate(
        [ref[s, end : end + 8, :].astype(jnp.float32)[:, :count] for s in range(sources)], axis=1
    )
    lane = iota((1, sources * count), 1)
    plane = lax.div(step * sources + lax.div(lane, jnp.int32(count)), jnp.int32(sizes.columns))
    return feet, notes, plane


def second_round(sizes, flux_index, refs, first, heights, count):
    notes = [
        jnp.concatenate(
            [ref[n * 8 : (n + 1) * 8, :].astype(jnp.float32) for n in range(heights // 8)], axis=1
        )[:, :count]
        for ref in refs
    ]
    plane = first + lax.div(iota((1, len(refs) * count), 1), jnp.int32(count))
    feet = jnp.concatenate([ref[heights : heights + count, :] for ref in refs], axis=0)
    return feet, jnp.concatenate(notes, axis=1), lax.bitwise_xor(plane, flux_index)


def partial_sums(sizes, flux_ref, feet, read):
    target, row, column = (read[n : n + 1].astype(jnp.int32) for n in range(3))
    count = feet.shape[0]
    levels = sizes.hours * sizes.tiles
    products = lax.dot_general(
        flux_ref[...].reshape(levels, sizes.part),
        feet,
        (((1,), (1,)), ((), ())),
        preferred_element_type=jnp.float32,
    )
    chosen = jnp.where(iota((levels, count), 0) == target, products, 0.0)
    partial = jnp.sum(chosen, axis=0, keepdims=True)
    height = 8 * sizes.pages
    spread = jnp.where(iota((height, count), 0) == row, partial, 0.0)
    terms = jnp.concatenate(thirds(spread), axis=0).astype(jnp.bfloat16)
    lanes = (iota((LANES, count), 0) == column).astype(jnp.bfloat16)
    sums = lax.dot_general(
        terms, lanes, (((1,), (1,)), ((), ())), preferred_element_type=jnp.float32
    )
    return sums[:height] + sums[height : 2 * height] + sums[2 * height :]


def coefficients(sizes, model, read):
    target, row, column = (read[n : n + 1].astype(jnp.int32) for n in range(3))
    count = read.shape[1]
    height = 8 * sizes.pages
    lanes = (iota((LANES, count), 0) == column).astype(jnp.bfloat16)
    taken = jnp.dot(model, lanes, preferred_element_type=jnp.float32)
    taken = taken[:height] + taken[height : 2 * height] + taken[2 * height :]
    value = jnp.sum(
        jnp.where(iota((height, count), 0) == row, taken, 0.0), axis=0, keepdims=True
    )
    scaled = ((value - read[3:4]) / read[4:5]).astype(jnp.bfloat16).astype(jnp.float32)
    levels = sizes.hours * sizes.tiles
    return jnp.where(iota((levels, count), 0) == target, scaled, 0.0).astype(jnp.bfloat16)


def pack_kernel(sizes, at_ref, *refs):
    tables, feet_ref, send_ref = refs[:5], refs[5], refs[6]
    spills = refs[7 : 7 + sizes.columns]
    feet, sent, spilled, first_notes, count, *local = refs[7 + sizes.columns : -4]
    arrived, feet_arrived, sent_done, over_done = refs[-4:]
    list_ref, row_ref, hour_ref, seen_ref, var_ref = local
    owners, per_slot = sizes.owners, sizes.per_slot
    group = sizes.columns // PACK_STEPS
    mine = at_ref[1]
    tables = [
        pltpu.make_async_copy(table, here, arrived.at[n])
        for n, (table, here) in enumerate(zip(tables, local))
    ]
    for copy in tables:
        copy.start()
    firsts = [pl.multiple_of((i ^ (mine // group)) * group, group) for i in range(PACK_STEPS)]
    loads = []
    for i, first in enumerate(firsts):
        lanes = pl.ds(pl.multiple_of(first * sizes.part, LANES), group * sizes.part)
        loads.append(
            pltpu.make_async_copy(feet_ref.at[:, :, lanes], feet.at[i], feet_arrived.at[i])
        )
        loads[-1].start()
    for copy in tables:
        copy.wait()

    field, lane = iota((16, LANES), 0), iota((16, LANES), 1)
    inner = lane % per_slot
    sounding = inner // sizes.lags
    slot_at = lane // per_slot
    key_at = iota((1, sizes.slots * per_slot), 1)
    key = jnp.zeros(key_at.shape, jnp.int32)
    empty = jnp.where(field == 0, jnp.float32(sizes.half), 0.0)
    empty = jnp.where(field == 5, 1.0, jnp.where(field == 8, -1.0, empty))
    for o in range(owners):
        count[o] = 0
        first_notes[o] = empty[:8]
    count[owners] = 0
    lefts = [empty] * sizes.spill_notes
    for b in range(sizes.blocks):
        base = jnp.zeros(field.shape, jnp.float32)
        seen = jnp.zeros(field.shape, jnp.float32)
        spread = jnp.ones(field.shape, jnp.float32)
        for o in range(sizes.soundings):
            here = sounding == o
            hour = hour_ref[o, b] * sizes.tiles - sizes.half
            base = jnp.where(here, hour.astype(jnp.float32), base)
            seen = jnp.where(here, seen_ref[o, b], seen)
            spread = jnp.where(here, var_ref[o, b], spread)
        column = (b + sizes.blocks * at_ref[1]).astype(jnp.float32)
        pattern = jnp.where(field == 0, base, jnp.where(field == 1, column, 0.0))
        for n, term in enumerate(thirds(seen) + thirds(spread)):
            pattern = jnp.where(field == 2 + n, term, pattern)
        for k in range(sizes.width):
            stored = row_ref[list_ref[k, b]]
            owner = lax.div(stored, jnp.int32(sizes.tiles))
            tile = (stored - owner * sizes.tiles).astype(jnp.float32)
            position = count[owner]
            count[owner] = position + 1
            keep = position < sizes.first
            over = count[owners]
            count[owners] = over + jnp.where(keep, 0, 1)
            goes = jnp.where(
                keep, owner * sizes.first + position, owners * sizes.first + over
            )
            value = jnp.where(field == 0, pattern + tile, pattern)
            value = jnp.where(field == 8, owner.astype(jnp.float32), value)
            value = jnp.where(
                field == 9, (position - sizes.first).astype(jnp.float32), value
            )
            first_notes[owner] = jnp.where(
                slot_at[:8] == jnp.where(keep, position, -1), value[:8], first_notes[owner]
            )
            lefts = [
                jnp.where(
                    slot_at + n * (LANES // per_slot) == jnp.where(keep, -1, over), value, left
                )
                for n, left in enumerate(lefts)
            ]
            key = jnp.where(
                key_at // per_slot == b * sizes.width + k,
                goes * per_slot + key_at % per_slot,
                key,
            )
    counts = jnp.zeros((8, LANES), jnp.float32)
    for o in range(owners):
        over = jnp.maximum(count[o] - sizes.first, 0).astype(jnp.float32)
        counts = jnp.where(lane[:8] == sizes.rows + o, over, counts)
    for o in range(owners):
        first_notes[o] = jnp.where(lane[:8] < sizes.rows, first_notes[o], counts)
    place = (iota((owners * sizes.rows + sizes.spill, key.shape[1]), 0) == key).astype(
        jnp.bfloat16
    )
    rows, spill, tiles = sizes.rows, sizes.spill, sizes.lane_tiles
    end = tiles * rows
    stores = []
    for i, first in enumerate(firsts):
        loads[i].wait()
        packed = jnp.dot(
            place,
            feet[i].reshape(key.shape[1], group * sizes.part),
            preferred_element_type=jnp.float32,
        )
        for c in range(group):
            for o in range(owners):
                for n in range(tiles):
                    lanes = slice((c * tiles + n) * LANES, (c * tiles + n + 1) * LANES)
                    sent[i, o, c, n * rows : (n + 1) * rows, :] = packed[
                        o * rows : (o + 1) * rows, lanes
                    ].astype(jnp.bfloat16)
                sent[i, o, c, end : end + 8, :] = first_notes[o].astype(jnp.bfloat16)
            for n in range(tiles):
                lanes = slice((c * tiles + n) * LANES, (c * tiles + n + 1) * LANES)
                spilled[i, c, n * spill : (n + 1) * spill, :] = packed[
                    owners * rows :, lanes
                ].astype(jnp.bfloat16)
            for n, left in enumerate(lefts):
                first_note = tiles * spill + n * 16
                spilled[i, c, first_note : first_note + 16, :] = left.astype(jnp.bfloat16)
        stores.append(
            pltpu.make_async_copy(
                sent.at[i], send_ref.at[:, pl.ds(first, group)], sent_done.at[i]
            )
        )
        stores[-1].start()
        for d in range(i * group, (i + 1) * group):
            stores.append(
                pltpu.make_async_copy(spilled.at[i, (d ^ mine) % group], spills[d], over_done.at[d])
            )
            stores[-1].start()
    for copy in stores:
        copy.wait()


def level_of(sizes, ref):
    planes = [
        sum(
            ref[p * sizes.columns + j].astype(jnp.float32) for j in range(sizes.columns)
        )
        for p in range(sizes.owners)
    ]
    counts = functools.reduce(jnp.maximum, planes)[0:1]
    lane = iota(counts.shape, 1)
    counts = jnp.where((lane >= sizes.rows) & (lane < sizes.rows + sizes.owners), counts, 0.0)
    most = jnp.max(counts, axis=1, keepdims=True) * sizes.per_slot
    level = jnp.zeros((1, 1), jnp.int32)
    for n in sizes.levels[:-1]:
        level = level + jnp.where(most > sizes.base + n, 1, 0)
    return level


def regroup_kernel(sizes, start, count, heights, at_ref, *refs):
    columns, owners, spill = sizes.columns, sizes.owners, sizes.spill
    spills, outs, (feet,) = refs[:columns], refs[columns : columns + owners], refs[-1:]
    end = sizes.lane_tiles * spill
    notes = []
    for d, ref in enumerate(spills):
        for n in range(sizes.lane_tiles):
            feet[d * spill : (d + 1) * spill, n * LANES : (n + 1) * LANES] = ref[
                n * spill : (n + 1) * spill, :
            ]
        blocks = [
            ref[end + n * 16 : end + (n + 1) * 16, :].astype(jnp.float32)
            for n in range(sizes.spill_notes)
        ]
        notes.append(jnp.concatenate(blocks, axis=1)[:, :spill])
    owner_at = jnp.concatenate([each[8:9] for each in notes], axis=0)
    position = jnp.concatenate([each[9:10] for each in notes], axis=0).astype(jnp.int32)
    inner = lax.rem(iota(position.shape, 1), jnp.int32(sizes.per_slot))
    fields = jnp.concatenate([each[0:8] for each in notes], axis=1).astype(jnp.bfloat16)
    for n in range(owners):
        mine = owner_at == (at_ref[2] ^ n).astype(jnp.float32)
        counts = jnp.sum(jnp.where(mine, 1.0, 0.0), axis=1, keepdims=True).astype(jnp.int32)
        keys, total = [], jnp.zeros((1, 1), jnp.int32)
        for d in range(columns):
            row = total + position[d : d + 1] * sizes.per_slot + inner[d : d + 1] - start
            keys.append(jnp.where(mine[d : d + 1], row, -1))
            total = total + counts[d : d + 1]
        key = jnp.concatenate(keys, axis=1)
        place = (iota((count, columns * spill), 0) == key).astype(jnp.bfloat16)
        outs[n][heights:, :] = jnp.dot(
            place, feet[...], preferred_element_type=jnp.float32
        ).astype(jnp.bfloat16)
        moved = lax.dot_general(
            fields, place, (((1,), (1,)), ((), ())), preferred_element_type=jnp.float32
        )
        field, lane = iota(moved.shape, 0), iota(moved.shape, 1)
        empty = jnp.where(field == 0, jnp.float32(sizes.half), jnp.where(field == 5, 1.0, 0.0))
        moved = jnp.where(lane + start < total, moved, empty)
        for m in range(heights // 8):
            lanes = moved[:, m * sizes.part : (m + 1) * sizes.part].astype(jnp.bfloat16)
            outs[n][m * 8 : (m + 1) * 8, : lanes.shape[1]] = lanes


def forward_first_kernel(
    sizes, at_ref, flux_ref, got_ref, all_ref, out_ref, level_ref, feet_ref, read_ref
):
    step = pl.program_id(0)
    feet, notes, plane = first_round(sizes, got_ref, step)
    read = read_notes(sizes, notes, plane)
    feet_ref[...], read_ref[...] = feet, read
    sums = partial_sums(sizes, flux_ref, feet, read)

    @pl.when(step == 0)
    def _():
        out_ref[...] = sums
        level_ref[...] = jnp.broadcast_to(level_of(sizes, all_ref), level_ref.shape)

    @pl.when(step > 0)
    def _():
        out_ref[...] += sums


def forward_second_kernel(sizes, first, heights, count, at_ref, flux_ref, before_ref, *refs):
    *parts, out_ref, read_ref = refs
    feet, notes, plane = second_round(sizes, at_ref[2], parts, first, heights, count)
    read = read_notes(sizes, notes, plane)
    read_ref[...] = read
    sums = before_ref[0] + partial_sums(sizes, flux_ref, feet, read)
    out_ref[...] = jnp.broadcast_to(sums[None], out_ref.shape)


def adjoint_kernel(
    sizes, more, at_ref, sums_ref, feet_ref, read_ref, read_second_ref, read_last_ref, *refs
):
    bases, rests = refs[: sizes.owners], refs[sizes.owners : -4]
    modeled_ref, out_ref, grad_ref, written = refs[-4:]
    sums = jnp.sum(sums_ref[...], axis=0)
    model = jnp.concatenate(thirds(sums), axis=0).astype(jnp.bfloat16)
    pairs = [(coefficients(sizes, model, read_ref[...]), feet_ref, 0, feet_ref.shape[0])]
    reads = jnp.concatenate([read_second_ref[...], read_last_ref[...]], axis=1)
    second = coefficients(sizes, model, reads)
    for n, ref in enumerate(bases):
        pairs.append(
            (second[:, n * sizes.base : (n + 1) * sizes.base], ref, sizes.base_notes, sizes.base)
        )
    if rests:
        *rests, read_more_ref = rests
        last = coefficients(sizes, model, read_more_ref[...])
        for n, ref in enumerate(rests):
            pairs.append((last[:, n * more : (n + 1) * more], ref, sizes.rest_notes, more))
    half = sizes.part // 2 if sizes.part > LANES else sizes.part
    copies = []
    for n in range(sizes.part // half):
        lanes = slice(n * half, (n + 1) * half)
        terms = sum(
            jnp.dot(each, ref[first : first + count, lanes], preferred_element_type=jnp.float32)
            for each, ref, first, count in pairs
        )
        grad_ref[:, :, lanes] = terms.reshape(sizes.hours, sizes.tiles, half)
        copies.append(
            pltpu.make_async_copy(grad_ref.at[:, :, lanes], out_ref.at[:, :, lanes], written.at[n])
        )
        copies[-1].start()
    me = at_ref[0]
    page, within = lax.div(me, sizes.per_page), lax.rem(me, sizes.per_page)
    lane = iota((8, LANES), 1)
    own = jnp.zeros((8, LANES), jnp.float32)
    for p in range(sizes.pages):
        own = jnp.where(page == p, sums[p * 8 : (p + 1) * 8], own)
    result = jnp.zeros(modeled_ref.shape, jnp.float32)
    at_block = iota(modeled_ref.shape, 1)
    each = 8 // sizes.soundings
    for q in range(sizes.states // 8):
        picked = jnp.where(lane == q * sizes.per_page + within, own, 0.0)
        column = jnp.sum(picked, axis=1, keepdims=True)
        for n in range(each):
            values = column[n * sizes.soundings : (n + 1) * sizes.soundings]
            result = jnp.where(at_block == q * each + n, values, result)
    modeled_ref[...] = result
    for copy in copies:
        copy.wait()


def shards(footprint, obs_hour, tile_list, tile_row, flux, observed, obs_var):
    sizes = Sizes(
        lax.axis_size("flux"), lax.axis_size("obs"), footprint.shape, flux.shape
    )
    owners, columns, devices, part = sizes.owners, sizes.columns, sizes.devices, sizes.part
    both = ("flux", "obs")
    params = pltpu.CompilerParams(vmem_limit_bytes=VMEM_BYTES)
    me = lax.axis_index("flux") * columns + lax.axis_index("obs")
    at = jnp.stack([me, lax.axis_index("obs"), lax.axis_index("flux")])
    flux = flux.transpose(1, 0, 2)

    first_height = sizes.lane_tiles * sizes.rows + 8
    spill_height = sizes.lane_tiles * sizes.spill + sizes.spill_notes * 16
    all_slots = sizes.slots * sizes.per_slot
    group = columns // PACK_STEPS
    tables = (tile_list.T, tile_row, obs_hour.T, observed.T, obs_var.T)
    send, *spills = pl.pallas_call(
        functools.partial(pack_kernel, sizes),
        in_specs=[pl.BlockSpec(memory_space=pltpu.SMEM)]
        + [pl.BlockSpec(memory_space=pltpu.HBM)] * 6,
        out_specs=[pl.BlockSpec(memory_space=pltpu.HBM)] * (1 + columns),
        scratch_shapes=[
            pltpu.VMEM(
                (PACK_STEPS, all_slots // sizes.lags, sizes.lags, group * part), jnp.bfloat16
            ),
            pltpu.VMEM((PACK_STEPS, owners, group, first_height, LANES), jnp.bfloat16),
            pltpu.VMEM((PACK_STEPS, group, spill_height, LANES), jnp.bfloat16),
            pltpu.VMEM((owners, 8, LANES), jnp.float32),
            pltpu.SMEM((owners + 1,), jnp.int32),
        ]
        + [pltpu.SMEM(table.shape, table.dtype) for table in tables]
        + [pltpu.SemaphoreType.DMA((n,)) for n in (5, PACK_STEPS, PACK_STEPS, columns)],
        out_shape=[pltpu.HBM((owners, columns, first_height, LANES), jnp.bfloat16)]
        + [jax.ShapeDtypeStruct((spill_height, LANES), jnp.bfloat16)] * columns,
        compiler_params=pltpu.CompilerParams(vmem_limit_bytes=ALL_VMEM_BYTES),
        name="pack",
    )(
        at,
        *tables,
        footprint.reshape(all_slots // sizes.lags, sizes.lags, columns * part),
    )
    got = lax.all_to_all(
        send.reshape(devices, first_height, LANES), both, split_axis=0, concat_axis=0, tiled=True
    )
    mine = spills[0]
    spills = spills[:1] + [
        lax.ppermute(spills[d], "obs", [(i, i ^ d) for i in range(columns)])
        for d in range(1, columns)
    ]
    smem, vmem = pl.BlockSpec(memory_space=pltpu.SMEM), pl.BlockSpec(memory_space=pltpu.VMEM)

    def regroup(spills, start, count, heights, name):
        shape = jax.ShapeDtypeStruct((heights + count, part), jnp.bfloat16)
        return pl.pallas_call(
            functools.partial(regroup_kernel, sizes, start, count, heights),
            in_specs=[smem] + [vmem] * columns,
            out_specs=[vmem] * owners,
            out_shape=[shape] * owners,
            scratch_shapes=[pltpu.VMEM((columns * sizes.spill, part), jnp.bfloat16)],
            compiler_params=params,
            name=name,
        )(at, *spills)

    def swap(arrays):
        return arrays[:1] + [
            lax.ppermute(arrays[n], "flux", [(i, i ^ n) for i in range(owners)])
            for n in range(1, owners)
        ]

    bases = swap(list(regroup(spills, 0, sizes.base, sizes.base_notes, "regroup")))

    sources = min(devices, 1 << (1024 // sizes.rows).bit_length() - 1)
    chunks = devices // sources
    copies = devices if devices <= 64 else 1
    height = 8 * sizes.pages
    flux_spec = pl.BlockSpec((sizes.hours, sizes.tiles, part), lambda i, at: (0, 0, at[1]))
    early, level, feet_first, read_first = pl.pallas_call(
        functools.partial(forward_first_kernel, sizes),
        grid_spec=pltpu.PrefetchScalarGridSpec(
            num_scalar_prefetch=1,
            grid=(chunks,),
            in_specs=[
                flux_spec,
                pl.BlockSpec((sources, first_height, LANES), lambda i, at: (i, 0, 0)),
                pl.BlockSpec((devices, 8, LANES), lambda i, at: (0, first_height // 8 - 1, 0)),
            ],
            out_specs=(
                pl.BlockSpec((height, LANES), lambda i, at: (0, 0)),
                pl.BlockSpec((8, LANES), lambda i, at: (0, 0)),
                pl.BlockSpec((sources * sizes.rows, part), lambda i, at: (i, 0)),
                pl.BlockSpec((8, sources * sizes.rows), lambda i, at: (0, i)),
            ),
        ),
        out_shape=(
            jax.ShapeDtypeStruct((height, LANES), jnp.float32),
            jax.ShapeDtypeStruct((8, LANES), jnp.int32),
            jax.ShapeDtypeStruct((devices * sizes.rows, part), jnp.bfloat16),
            jax.ShapeDtypeStruct((8, devices * sizes.rows), jnp.float32),
        ),
        compiler_params=params,
        name="forward_first",
    )(at, flux, got, got)

    late_flux = lax.optimization_barrier((flux, mine))[0]
    own_flux = lax.dynamic_slice_in_dim(late_flux, lax.axis_index("obs") * part, part, axis=2)

    def forward_second(own_flux, before, parts, first, heights, count, name):
        return pl.pallas_call(
            functools.partial(forward_second_kernel, sizes, first, heights, count),
            in_specs=[smem] + [vmem] * (2 + len(parts)),
            out_specs=(vmem, vmem),
            out_shape=(
                jax.ShapeDtypeStruct((copies, height, LANES), jnp.float32),
                jax.ShapeDtypeStruct((8, len(parts) * count), jnp.float32),
            ),
            compiler_params=params,
            name=name,
        )(at, own_flux, before, *parts)

    late_spills = lax.optimization_barrier((spills, early))[0]
    rests = list(regroup(late_spills, sizes.base, sizes.rest, sizes.rest_notes, "regroup_rest"))

    level = level[0, 0]

    sums, read_second = forward_second(
        own_flux, early[None], bases[:-1], 0, sizes.base_notes, sizes.base, "forward_second"
    )
    kept = (feet_first, read_first, read_second)

    def finish(more):
        def run(own_flux, kept, sums, bases, rests, at):
            if more:
                rests = swap([rest[: sizes.rest_notes + more] for rest in rests])
            sums, read_last = forward_second(
                own_flux, sums, bases[-1:], owners - 1, sizes.base_notes, sizes.base, "forward_last"
            )
            if more:
                sums, read_more = forward_second(
                    own_flux, sums, rests, 0, sizes.rest_notes, more, "forward_more"
                )
                rests = rests + [read_more]
            else:
                rests = []
            if copies > 1:
                sums = lax.all_to_all(sums, both, split_axis=0, concat_axis=0, tiled=True)
            else:
                sums = lax.psum(sums, both)
            return pl.pallas_call(
                functools.partial(adjoint_kernel, sizes, more),
                in_specs=[smem] + [vmem] * (5 + len(bases) + len(rests)),
                out_specs=(vmem, pl.BlockSpec(memory_space=pltpu.HBM)),
                out_shape=(
                    jax.ShapeDtypeStruct((sizes.soundings, sizes.blocks), jnp.float32),
                    jax.ShapeDtypeStruct((sizes.hours, sizes.tiles, part), jnp.float32),
                ),
                scratch_shapes=[
                    pltpu.VMEM((sizes.hours, sizes.tiles, part), jnp.float32),
                    pltpu.SemaphoreType.DMA((2,)),
                ],
                compiler_params=params,
                name="adjoint",
            )(at, sums, *kept, read_last, *bases, *rests)

        return run

    modeled, gradient = lax.switch(
        level, [finish(n) for n in sizes.levels], own_flux, kept, sums, bases, rests, at
    )
    return modeled.T, gradient.transpose(1, 0, 2)


def solution(mesh):
    placed = (
        P(("flux", "obs"), None, None, None, None),
        P(("flux", "obs"), None),
        P(("flux", "obs"), None),
        P(),
        P("flux", None, None),
        P(("flux", "obs"), None),
        P(("flux", "obs"), None),
    )
    return jax.shard_map(
        shards,
        mesh=mesh,
        in_specs=placed,
        out_specs=(P(("flux", "obs"), None), P("flux", None, "obs")),
        check_vma=False,
    )
```

```python
import functools

import jax
import jax.numpy as jnp
from jax import lax
from jax.experimental import pallas as pl
from jax.experimental.pallas import tpu as pltpu
from jax.sharding import PartitionSpec as P

LANES = 128
VMEM_BYTES = 48 * 1024 * 1024
ALL_VMEM_BYTES = 60 * 1024 * 1024
BASE = 240
REST = (0, 64, 144)
PACK_STEPS = 2


def iota(shape, dim):
    return lax.broadcasted_iota(jnp.int32, shape, dim)


def thirds(value):
    high = value.astype(jnp.bfloat16).astype(jnp.float32)
    rest = value - high
    middle = rest.astype(jnp.bfloat16).astype(jnp.float32)
    return high, middle, (rest - middle).astype(jnp.bfloat16).astype(jnp.float32)


class Sizes:
    def __init__(self, owners, columns, footprint, flux):
        self.owners, self.columns = owners, columns
        self.devices = owners * columns
        self.blocks, self.width, self.soundings, self.lags, cells = footprint
        self.tiles, self.hours = flux[0], flux[1]
        self.span = self.hours - self.lags + 1
        self.half = self.span * self.tiles // 2
        self.slots = self.blocks * self.width
        self.per_slot = self.soundings * self.lags
        self.part = cells // columns
        self.lane_tiles = self.part // LANES
        capacity = 2 * self.slots // owners
        self.first = capacity // 2 - capacity // 16
        self.rows = self.first * self.per_slot
        self.spill = (self.slots - owners // 2 * self.first) * self.per_slot
        self.spill_notes = -(-self.spill // LANES)
        self.second = columns * (capacity - self.first) * self.per_slot
        self.base = min(BASE, self.second)
        self.rest = self.second - self.base
        self.base_notes = 8 * -(-self.base // self.part)
        self.rest_notes = 8 * -(-self.rest // self.part)
        self.levels = tuple(n for n in REST if n < self.rest) + (self.rest,)
        self.states = self.blocks * self.soundings
        self.per_page = 8 * LANES // self.states
        self.pages = self.devices // self.per_page


def read_notes(sizes, notes, plane):
    lane = iota((1, notes.shape[1]), 1)
    inner = lax.rem(lane, jnp.int32(sizes.per_slot))
    base = notes[0:1]
    target = (base + sizes.half).astype(jnp.int32) + lax.rem(inner, jnp.int32(sizes.lags)) * sizes.tiles
    target = jnp.where(base > sizes.half - 0.5, -1, target)
    place = notes[1:2].astype(jnp.int32)
    block = lax.rem(place, jnp.int32(sizes.blocks))
    device = plane * sizes.columns + lax.div(place, jnp.int32(sizes.blocks))
    state = block * sizes.soundings + lax.div(inner, jnp.int32(sizes.lags))
    row = lax.div(device, jnp.int32(sizes.per_page)) * 8 + lax.rem(state, jnp.int32(8))
    column = lax.div(state, jnp.int32(8)) * sizes.per_page + lax.rem(device, jnp.int32(sizes.per_page))
    seen = notes[2:3] + notes[3:4] + notes[4:5]
    spread = notes[5:6] + notes[6:7] + notes[7:8]
    places = [each.astype(jnp.float32) for each in (target, row, column)]
    return jnp.concatenate(places + [seen, spread, jnp.zeros((3, lane.shape[1]), jnp.float32)], axis=0)


def first_round(sizes, ref, step):
    sources, count = ref.shape[0], sizes.rows
    feet = jnp.concatenate(
        [
            ref[:, n * count : (n + 1) * count, :].reshape(sources * count, LANES)
            for n in range(sizes.lane_tiles)
        ],
        axis=1,
    )
    end = sizes.lane_tiles * count
    notes = jnp.concatenate(
        [ref[s, end : end + 8, :].astype(jnp.float32)[:, :count] for s in range(sources)], axis=1
    )
    lane = iota((1, sources * count), 1)
    plane = lax.div(step * sources + lax.div(lane, jnp.int32(count)), jnp.int32(sizes.columns))
    return feet, notes, plane


def second_round(sizes, flux_index, refs, first, heights, count):
    notes = [
        jnp.concatenate(
            [ref[n * 8 : (n + 1) * 8, :].astype(jnp.float32) for n in range(heights // 8)], axis=1
        )[:, :count]
        for ref in refs
    ]
    plane = first + lax.div(iota((1, len(refs) * count), 1), jnp.int32(count))
    feet = jnp.concatenate([ref[heights : heights + count, :] for ref in refs], axis=0)
    return feet, jnp.concatenate(notes, axis=1), lax.bitwise_xor(plane, flux_index)


def partial_sums(sizes, flux_ref, feet, read):
    target, row, column = (read[n : n + 1].astype(jnp.int32) for n in range(3))
    count = feet.shape[0]
    levels = sizes.hours * sizes.tiles
    products = lax.dot_general(
        flux_ref[...].reshape(levels, sizes.part),
        feet,
        (((1,), (1,)), ((), ())),
        preferred_element_type=jnp.float32,
    )
    chosen = jnp.where(iota((levels, count), 0) == target, products, 0.0)
    partial = jnp.sum(chosen, axis=0, keepdims=True)
    height = 8 * sizes.pages
    spread = jnp.where(iota((height, count), 0) == row, partial, 0.0)
    terms = jnp.concatenate(thirds(spread), axis=0).astype(jnp.bfloat16)
    lanes = (iota((LANES, count), 0) == column).astype(jnp.bfloat16)
    sums = lax.dot_general(
        terms, lanes, (((1,), (1,)), ((), ())), preferred_element_type=jnp.float32
    )
    return sums[:height] + sums[height : 2 * height] + sums[2 * height :]


def coefficients(sizes, model, read):
    target, row, column = (read[n : n + 1].astype(jnp.int32) for n in range(3))
    count = read.shape[1]
    height = 8 * sizes.pages
    lanes = (iota((LANES, count), 0) == column).astype(jnp.bfloat16)
    taken = jnp.dot(model, lanes, preferred_element_type=jnp.float32)
    taken = taken[:height] + taken[height : 2 * height] + taken[2 * height :]
    value = jnp.sum(
        jnp.where(iota((height, count), 0) == row, taken, 0.0), axis=0, keepdims=True
    )
    scaled = ((value - read[3:4]) / read[4:5]).astype(jnp.bfloat16).astype(jnp.float32)
    levels = sizes.hours * sizes.tiles
    return jnp.where(iota((levels, count), 0) == target, scaled, 0.0).astype(jnp.bfloat16)


def pack_kernel(sizes, at_ref, *refs):
    tables, feet_ref, send_ref = refs[:5], refs[5], refs[6]
    spills = refs[7 : 7 + sizes.columns]
    feet, sent, spilled, first_notes, count, *local = refs[7 + sizes.columns : -4]
    arrived, feet_arrived, sent_done, over_done = refs[-4:]
    list_ref, row_ref, hour_ref, seen_ref, var_ref = local
    owners, per_slot = sizes.owners, sizes.per_slot
    group = sizes.columns // PACK_STEPS
    mine = at_ref[1]
    tables = [
        pltpu.make_async_copy(table, here, arrived.at[n])
        for n, (table, here) in enumerate(zip(tables, local))
    ]
    for copy in tables:
        copy.start()
    firsts = [pl.multiple_of((i ^ (mine // group)) * group, group) for i in range(PACK_STEPS)]
    loads = []
    for i, first in enumerate(firsts):
        lanes = pl.ds(pl.multiple_of(first * sizes.part, LANES), group * sizes.part)
        loads.append(
            pltpu.make_async_copy(feet_ref.at[:, :, lanes], feet.at[i], feet_arrived.at[i])
        )
        loads[-1].start()
    for copy in tables:
        copy.wait()

    field, lane = iota((16, LANES), 0), iota((16, LANES), 1)
    inner = lane % per_slot
    sounding = inner // sizes.lags
    slot_at = lane // per_slot
    key_at = iota((1, sizes.slots * per_slot), 1)
    key = jnp.zeros(key_at.shape, jnp.int32)
    empty = jnp.where(field == 0, jnp.float32(sizes.half), 0.0)
    empty = jnp.where(field == 5, 1.0, jnp.where(field == 8, -1.0, empty))
    for o in range(owners):
        count[o] = 0
        first_notes[o] = empty[:8]
    count[owners] = 0
    lefts = [empty] * sizes.spill_notes
    for b in range(sizes.blocks):
        base = jnp.zeros(field.shape, jnp.float32)
        seen = jnp.zeros(field.shape, jnp.float32)
        spread = jnp.ones(field.shape, jnp.float32)
        for o in range(sizes.soundings):
            here = sounding == o
            hour = hour_ref[o, b] * sizes.tiles - sizes.half
            base = jnp.where(here, hour.astype(jnp.float32), base)
            seen = jnp.where(here, seen_ref[o, b], seen)
            spread = jnp.where(here, var_ref[o, b], spread)
        column = (b + sizes.blocks * at_ref[1]).astype(jnp.float32)
        pattern = jnp.where(field == 0, base, jnp.where(field == 1, column, 0.0))
        for n, term in enumerate(thirds(seen) + thirds(spread)):
            pattern = jnp.where(field == 2 + n, term, pattern)
        for k in range(sizes.width):
            stored = row_ref[list_ref[k, b]]
            owner = lax.div(stored, jnp.int32(sizes.tiles))
            tile = (stored - owner * sizes.tiles).astype(jnp.float32)
            position = count[owner]
            count[owner] = position + 1
            keep = position < sizes.first
            over = count[owners]
            count[owners] = over + jnp.where(keep, 0, 1)
            goes = jnp.where(
                keep, owner * sizes.first + position, owners * sizes.first + over
            )
            value = jnp.where(field == 0, pattern + tile, pattern)
            value = jnp.where(field == 8, owner.astype(jnp.float32), value)
            value = jnp.where(
                field == 9, (position - sizes.first).astype(jnp.float32), value
            )
            first_notes[owner] = jnp.where(
                slot_at[:8] == jnp.where(keep, position, -1), value[:8], first_notes[owner]
            )
            lefts = [
                jnp.where(
                    slot_at + n * (LANES // per_slot) == jnp.where(keep, -1, over), value, left
                )
                for n, left in enumerate(lefts)
            ]
            key = jnp.where(
                key_at // per_slot == b * sizes.width + k,
                goes * per_slot + key_at % per_slot,
                key,
            )
    counts = jnp.zeros((8, LANES), jnp.float32)
    for o in range(owners):
        over = jnp.maximum(count[o] - sizes.first, 0).astype(jnp.float32)
        counts = jnp.where(lane[:8] == sizes.rows + o, over, counts)
    for o in range(owners):
        first_notes[o] = jnp.where(lane[:8] < sizes.rows, first_notes[o], counts)
    place = (iota((owners * sizes.rows + sizes.spill, key.shape[1]), 0) == key).astype(
        jnp.bfloat16
    )
    rows, spill, tiles = sizes.rows, sizes.spill, sizes.lane_tiles
    end = tiles * rows
    stores = []
    for i, first in enumerate(firsts):
        loads[i].wait()
        packed = jnp.dot(
            place,
            feet[i].reshape(key.shape[1], group * sizes.part),
            preferred_element_type=jnp.float32,
        )
        for c in range(group):
            for o in range(owners):
                for n in range(tiles):
                    lanes = slice((c * tiles + n) * LANES, (c * tiles + n + 1) * LANES)
                    sent[i, o, c, n * rows : (n + 1) * rows, :] = packed[
                        o * rows : (o + 1) * rows, lanes
                    ].astype(jnp.bfloat16)
                sent[i, o, c, end : end + 8, :] = first_notes[o].astype(jnp.bfloat16)
            for n in range(tiles):
                lanes = slice((c * tiles + n) * LANES, (c * tiles + n + 1) * LANES)
                spilled[i, c, n * spill : (n + 1) * spill, :] = packed[
                    owners * rows :, lanes
                ].astype(jnp.bfloat16)
            for n, left in enumerate(lefts):
                first_note = tiles * spill + n * 16
                spilled[i, c, first_note : first_note + 16, :] = left.astype(jnp.bfloat16)
        stores.append(
            pltpu.make_async_copy(
                sent.at[i], send_ref.at[:, pl.ds(first, group)], sent_done.at[i]
            )
        )
        stores[-1].start()
        for d in range(i * group, (i + 1) * group):
            stores.append(
                pltpu.make_async_copy(spilled.at[i, (d ^ mine) % group], spills[d], over_done.at[d])
            )
            stores[-1].start()
    for copy in stores:
        copy.wait()


def level_of(sizes, ref):
    planes = [
        sum(
            ref[p * sizes.columns + j].astype(jnp.float32) for j in range(sizes.columns)
        )
        for p in range(sizes.owners)
    ]
    counts = functools.reduce(jnp.maximum, planes)[0:1]
    lane = iota(counts.shape, 1)
    counts = jnp.where((lane >= sizes.rows) & (lane < sizes.rows + sizes.owners), counts, 0.0)
    most = jnp.max(counts, axis=1, keepdims=True) * sizes.per_slot
    level = jnp.zeros((1, 1), jnp.int32)
    for n in sizes.levels[:-1]:
        level = level + jnp.where(most > sizes.base + n, 1, 0)
    return level


def regroup_kernel(sizes, start, count, heights, at_ref, *refs):
    columns, owners, spill = sizes.columns, sizes.owners, sizes.spill
    spills, outs, (feet,) = refs[:columns], refs[columns : columns + owners], refs[-1:]
    end = sizes.lane_tiles * spill
    notes = []
    for d, ref in enumerate(spills):
        for n in range(sizes.lane_tiles):
            feet[d * spill : (d + 1) * spill, n * LANES : (n + 1) * LANES] = ref[
                n * spill : (n + 1) * spill, :
            ]
        blocks = [
            ref[end + n * 16 : end + (n + 1) * 16, :].astype(jnp.float32)
            for n in range(sizes.spill_notes)
        ]
        notes.append(jnp.concatenate(blocks, axis=1)[:, :spill])
    owner_at = jnp.concatenate([each[8:9] for each in notes], axis=0)
    position = jnp.concatenate([each[9:10] for each in notes], axis=0).astype(jnp.int32)
    inner = lax.rem(iota(position.shape, 1), jnp.int32(sizes.per_slot))
    fields = jnp.concatenate([each[0:8] for each in notes], axis=1).astype(jnp.bfloat16)
    for n in range(owners):
        mine = owner_at == (at_ref[2] ^ n).astype(jnp.float32)
        counts = jnp.sum(jnp.where(mine, 1.0, 0.0), axis=1, keepdims=True).astype(jnp.int32)
        keys, total = [], jnp.zeros((1, 1), jnp.int32)
        for d in range(columns):
            row = total + position[d : d + 1] * sizes.per_slot + inner[d : d + 1] - start
            keys.append(jnp.where(mine[d : d + 1], row, -1))
            total = total + counts[d : d + 1]
        key = jnp.concatenate(keys, axis=1)
        place = (iota((count, columns * spill), 0) == key).astype(jnp.bfloat16)
        outs[n][heights:, :] = jnp.dot(
            place, feet[...], preferred_element_type=jnp.float32
        ).astype(jnp.bfloat16)
        moved = lax.dot_general(
            fields, place, (((1,), (1,)), ((), ())), preferred_element_type=jnp.float32
        )
        field, lane = iota(moved.shape, 0), iota(moved.shape, 1)
        empty = jnp.where(field == 0, jnp.float32(sizes.half), jnp.where(field == 5, 1.0, 0.0))
        moved = jnp.where(lane + start < total, moved, empty)
        for m in range(heights // 8):
            lanes = moved[:, m * sizes.part : (m + 1) * sizes.part].astype(jnp.bfloat16)
            outs[n][m * 8 : (m + 1) * 8, : lanes.shape[1]] = lanes


def forward_first_kernel(
    sizes, at_ref, flux_ref, got_ref, all_ref, out_ref, level_ref, feet_ref, read_ref
):
    step = pl.program_id(0)
    feet, notes, plane = first_round(sizes, got_ref, step)
    read = read_notes(sizes, notes, plane)
    feet_ref[...], read_ref[...] = feet, read
    sums = partial_sums(sizes, flux_ref, feet, read)

    @pl.when(step == 0)
    def _():
        out_ref[...] = sums
        level_ref[...] = jnp.broadcast_to(level_of(sizes, all_ref), level_ref.shape)

    @pl.when(step > 0)
    def _():
        out_ref[...] += sums


def forward_second_kernel(sizes, first, heights, count, at_ref, flux_ref, before_ref, *refs):
    *parts, out_ref, read_ref = refs
    feet, notes, plane = second_round(sizes, at_ref[2], parts, first, heights, count)
    read = read_notes(sizes, notes, plane)
    read_ref[...] = read
    sums = before_ref[0] + partial_sums(sizes, flux_ref, feet, read)
    out_ref[...] = jnp.broadcast_to(sums[None], out_ref.shape)


def adjoint_kernel(
    sizes, more, at_ref, sums_ref, feet_ref, read_ref, read_second_ref, read_last_ref, *refs
):
    bases, rests = refs[: sizes.owners], refs[sizes.owners : -4]
    modeled_ref, out_ref, grad_ref, written = refs[-4:]
    sums = jnp.sum(sums_ref[...], axis=0)
    model = jnp.concatenate(thirds(sums), axis=0).astype(jnp.bfloat16)
    pairs = [(coefficients(sizes, model, read_ref[...]), feet_ref, 0, feet_ref.shape[0])]
    reads = jnp.concatenate([read_second_ref[...], read_last_ref[...]], axis=1)
    second = coefficients(sizes, model, reads)
    for n, ref in enumerate(bases):
        pairs.append(
            (second[:, n * sizes.base : (n + 1) * sizes.base], ref, sizes.base_notes, sizes.base)
        )
    if rests:
        *rests, read_more_ref = rests
        last = coefficients(sizes, model, read_more_ref[...])
        for n, ref in enumerate(rests):
            pairs.append((last[:, n * more : (n + 1) * more], ref, sizes.rest_notes, more))
    half = sizes.part // 2 if sizes.part > LANES else sizes.part
    copies = []
    for n in range(sizes.part // half):
        lanes = slice(n * half, (n + 1) * half)
        terms = sum(
            jnp.dot(each, ref[first : first + count, lanes], preferred_element_type=jnp.float32)
            for each, ref, first, count in pairs
        )
        grad_ref[:, :, lanes] = terms.reshape(sizes.hours, sizes.tiles, half)
        copies.append(
            pltpu.make_async_copy(grad_ref.at[:, :, lanes], out_ref.at[:, :, lanes], written.at[n])
        )
        copies[-1].start()
    me = at_ref[0]
    page, within = lax.div(me, sizes.per_page), lax.rem(me, sizes.per_page)
    lane = iota((8, LANES), 1)
    own = jnp.zeros((8, LANES), jnp.float32)
    for p in range(sizes.pages):
        own = jnp.where(page == p, sums[p * 8 : (p + 1) * 8], own)
    result = jnp.zeros(modeled_ref.shape, jnp.float32)
    at_block = iota(modeled_ref.shape, 1)
    each = 8 // sizes.soundings
    for q in range(sizes.states // 8):
        picked = jnp.where(lane == q * sizes.per_page + within, own, 0.0)
        column = jnp.sum(picked, axis=1, keepdims=True)
        for n in range(each):
            values = column[n * sizes.soundings : (n + 1) * sizes.soundings]
            result = jnp.where(at_block == q * each + n, values, result)
    modeled_ref[...] = result
    for copy in copies:
        copy.wait()


def shards(footprint, obs_hour, tile_list, tile_row, flux, observed, obs_var):
    sizes = Sizes(
        lax.axis_size("flux"), lax.axis_size("obs"), footprint.shape, flux.shape
    )
    owners, columns, devices, part = sizes.owners, sizes.columns, sizes.devices, sizes.part
    both = ("flux", "obs")
    params = pltpu.CompilerParams(vmem_limit_bytes=VMEM_BYTES)
    me = lax.axis_index("flux") * columns + lax.axis_index("obs")
    at = jnp.stack([me, lax.axis_index("obs"), lax.axis_index("flux")])
    flux = flux.transpose(1, 0, 2)

    first_height = sizes.lane_tiles * sizes.rows + 8
    spill_height = sizes.lane_tiles * sizes.spill + sizes.spill_notes * 16
    all_slots = sizes.slots * sizes.per_slot
    group = columns // PACK_STEPS
    tables = (tile_list.T, tile_row, obs_hour.T, observed.T, obs_var.T)
    send, *spills = pl.pallas_call(
        functools.partial(pack_kernel, sizes),
        in_specs=[pl.BlockSpec(memory_space=pltpu.SMEM)]
        + [pl.BlockSpec(memory_space=pltpu.HBM)] * 6,
        out_specs=[pl.BlockSpec(memory_space=pltpu.HBM)] * (1 + columns),
        scratch_shapes=[
            pltpu.VMEM(
                (PACK_STEPS, all_slots // sizes.lags, sizes.lags, group * part), jnp.bfloat16
            ),
            pltpu.VMEM((PACK_STEPS, owners, group, first_height, LANES), jnp.bfloat16),
            pltpu.VMEM((PACK_STEPS, group, spill_height, LANES), jnp.bfloat16),
            pltpu.VMEM((owners, 8, LANES), jnp.float32),
            pltpu.SMEM((owners + 1,), jnp.int32),
        ]
        + [pltpu.SMEM(table.shape, table.dtype) for table in tables]
        + [pltpu.SemaphoreType.DMA((n,)) for n in (5, PACK_STEPS, PACK_STEPS, columns)],
        out_shape=[pltpu.HBM((owners, columns, first_height, LANES), jnp.bfloat16)]
        + [jax.ShapeDtypeStruct((spill_height, LANES), jnp.bfloat16)] * columns,
        compiler_params=pltpu.CompilerParams(vmem_limit_bytes=ALL_VMEM_BYTES),
        name="pack",
    )(
        at,
        *tables,
        footprint.reshape(all_slots // sizes.lags, sizes.lags, columns * part),
    )
    got = lax.all_to_all(
        send.reshape(devices, first_height, LANES), both, split_axis=0, concat_axis=0, tiled=True
    )
    mine = spills[0]
    spills = spills[:1] + [
        lax.ppermute(spills[d], "obs", [(i, i ^ d) for i in range(columns)])
        for d in range(1, columns)
    ]
    smem, vmem = pl.BlockSpec(memory_space=pltpu.SMEM), pl.BlockSpec(memory_space=pltpu.VMEM)

    def regroup(spills, start, count, heights, name):
        shape = jax.ShapeDtypeStruct((heights + count, part), jnp.bfloat16)
        return pl.pallas_call(
            functools.partial(regroup_kernel, sizes, start, count, heights),
            in_specs=[smem] + [vmem] * columns,
            out_specs=[vmem] * owners,
            out_shape=[shape] * owners,
            scratch_shapes=[pltpu.VMEM((columns * sizes.spill, part), jnp.bfloat16)],
            compiler_params=params,
            name=name,
        )(at, *spills)

    def swap(arrays):
        return arrays[:1] + [
            lax.ppermute(arrays[n], "flux", [(i, i ^ n) for i in range(owners)])
            for n in range(1, owners)
        ]

    bases = swap(list(regroup(spills, 0, sizes.base, sizes.base_notes, "regroup")))

    sources = min(devices, 1 << (1024 // sizes.rows).bit_length() - 1)
    chunks = devices // sources
    copies = devices if devices <= 64 else 1
    height = 8 * sizes.pages
    flux_spec = pl.BlockSpec((sizes.hours, sizes.tiles, part), lambda i, at: (0, 0, at[1]))
    early, level, feet_first, read_first = pl.pallas_call(
        functools.partial(forward_first_kernel, sizes),
        grid_spec=pltpu.PrefetchScalarGridSpec(
            num_scalar_prefetch=1,
            grid=(chunks,),
            in_specs=[
                flux_spec,
                pl.BlockSpec((sources, first_height, LANES), lambda i, at: (i, 0, 0)),
                pl.BlockSpec((devices, 8, LANES), lambda i, at: (0, first_height // 8 - 1, 0)),
            ],
            out_specs=(
                pl.BlockSpec((height, LANES), lambda i, at: (0, 0)),
                pl.BlockSpec((8, LANES), lambda i, at: (0, 0)),
                pl.BlockSpec((sources * sizes.rows, part), lambda i, at: (i, 0)),
                pl.BlockSpec((8, sources * sizes.rows), lambda i, at: (0, i)),
            ),
        ),
        out_shape=(
            jax.ShapeDtypeStruct((height, LANES), jnp.float32),
            jax.ShapeDtypeStruct((8, LANES), jnp.int32),
            jax.ShapeDtypeStruct((devices * sizes.rows, part), jnp.bfloat16),
            jax.ShapeDtypeStruct((8, devices * sizes.rows), jnp.float32),
        ),
        compiler_params=params,
        name="forward_first",
    )(at, flux, got, got)

    late_flux = lax.optimization_barrier((flux, mine))[0]
    own_flux = lax.dynamic_slice_in_dim(late_flux, lax.axis_index("obs") * part, part, axis=2)

    def forward_second(own_flux, before, parts, first, heights, count, name):
        return pl.pallas_call(
            functools.partial(forward_second_kernel, sizes, first, heights, count),
            in_specs=[smem] + [vmem] * (2 + len(parts)),
            out_specs=(vmem, vmem),
            out_shape=(
                jax.ShapeDtypeStruct((copies, height, LANES), jnp.float32),
                jax.ShapeDtypeStruct((8, len(parts) * count), jnp.float32),
            ),
            compiler_params=params,
            name=name,
        )(at, own_flux, before, *parts)

    late_spills = lax.optimization_barrier((spills, early))[0]
    rests = list(regroup(late_spills, sizes.base, sizes.rest, sizes.rest_notes, "regroup_rest"))

    level = level[0, 0]

    sums, read_second = forward_second(
        own_flux, early[None], bases[:-1], 0, sizes.base_notes, sizes.base, "forward_second"
    )
    kept = (feet_first, read_first, read_second)

    def finish(more):
        def run(own_flux, kept, sums, bases, rests, at):
            if more:
                rests = swap([rest[: sizes.rest_notes + more] for rest in rests])
            sums, read_last = forward_second(
                own_flux, sums, bases[-1:], owners - 1, sizes.base_notes, sizes.base, "forward_last"
            )
            if more:
                sums, read_more = forward_second(
                    own_flux, sums, rests, 0, sizes.rest_notes, more, "forward_more"
                )
                rests = rests + [read_more]
            else:
                rests = []
            if copies > 1:
                sums = lax.all_to_all(sums, both, split_axis=0, concat_axis=0, tiled=True)
            else:
                sums = lax.psum(sums, both)
            return pl.pallas_call(
                functools.partial(adjoint_kernel, sizes, more),
                in_specs=[smem] + [vmem] * (5 + len(bases) + len(rests)),
                out_specs=(vmem, pl.BlockSpec(memory_space=pltpu.HBM)),
                out_shape=(
                    jax.ShapeDtypeStruct((sizes.soundings, sizes.blocks), jnp.float32),
                    jax.ShapeDtypeStruct((sizes.hours, sizes.tiles, part), jnp.float32),
                ),
                scratch_shapes=[
                    pltpu.VMEM((sizes.hours, sizes.tiles, part), jnp.float32),
                    pltpu.SemaphoreType.DMA((2,)),
                ],
                compiler_params=params,
                name="adjoint",
            )(at, sums, *kept, read_last, *bases, *rests)

        return run

    modeled, gradient = lax.switch(
        level, [finish(n) for n in sizes.levels], own_flux, kept, sums, bases, rests, at
    )
    return modeled.T, gradient.transpose(1, 0, 2)


def solution(mesh):
    placed = (
        P(("flux", "obs"), None, None, None, None),
        P(("flux", "obs"), None),
        P(("flux", "obs"), None),
        P(),
        P("flux", None, None),
        P(("flux", "obs"), None),
        P(("flux", "obs"), None),
    )
    return jax.shard_map(
        shards,
        mesh=mesh,
        in_specs=placed,
        out_specs=(P(("flux", "obs"), None), P("flux", None, "obs")),
        check_vma=False,
    )
```
